32 devices in a mesh: seq: 8 (over z, y), head: 4 (over x, core).
Axes of the slice: x: 2, y: 2, z: 4, core: 2. Of those that a mesh axis runs over, the one named last changes fastest.
Arguments:
- tokens: bfloat16 [4, 2048, 1024], P(None, 'seq'), may hold values from -6 to 6
- norm_gain: float32 [1024], replicated, as said below
- gate_weight: bfloat16 [1024, 2048], P(None, 'head'), may hold values from -0.1875 to 0.1875
- value_weight: bfloat16 [1024, 2048], P(None, 'head'), as said below
- shared_weight: bfloat16 [1024, 256], replicated, may hold values from -0.0234375 to 0.0234375
- step_weight: bfloat16 [1024, 32], P(None, 'head'), may hold values from -0.1875 to 0.1875
- conv_value: float32 [4, 2048], P(None, 'head'), may hold values from -3 to 3
- conv_value_bias: float32 [2048], P('head'), may hold values from -1.8 to 1.8
- conv_shared: float32 [4, 256], replicated, may hold values from -3 to 3
- conv_shared_bias: float32 [256], replicated, may hold values from -0.6 to 0.6
- step_bias: float32 [32], P('head'), may hold values from -1 to 1
- decay_rate: float32 [32], P('head'), as said below
- skip_weight: float32 [32], P('head'), may hold values from 0.5 to 1.5
- out_gain: float32 [2048], P('head'), may hold values from 0.5 to 1.5
- output_weight: bfloat16 [2048, 1024], P('head'), may hold values from -0.125 to 0.125
- cotangent: bfloat16 [4, 2048, 1024], P(None, 'seq', 'head'), may hold values from -6 to 6
Outputs:
- mixed: bfloat16 [4, 2048, 1024], P(None, 'seq', 'head')
- grad_tokens: float32 [4, 2048, 1024], P(None, 'seq', 'head')
- grad_norm_gain: float32 [1024], P('head')
- grad_w_gate: float32 [1024, 2048], P(None, 'head')
- grad_w_value: float32 [1024, 2048], P(None, 'head')
- grad_w_shared: float32 [1024, 256], replicated
- grad_w_step: float32 [1024, 32], P(None, 'head')
- grad_conv_value: float32 [4, 2048], P(None, 'head')
- grad_conv_value_bias: float32 [2048], P('head')
- grad_conv_shared: float32 [4, 256], replicated
- grad_conv_shared_bias: float32 [256], replicated
- grad_step_bias: float32 [32], P('head')
- grad_decay_rate: float32 [32], P('head')
- grad_skip_weight: float32 [32], P('head')
- grad_out_gain: float32 [2048], P('head')
- output_weight_gradient: float32 [2048, 1024], P('head')
The draws below stay inside these ranges and needn't reach their ends.
Inputs may be any that keep to these rules, and one draw needn't show every extreme that they name: `norm_gain`: gains of the input norm, each between 0.28 and 2.6. Entries of value_weight lie within 10 / sqrt(1024). `decay_rate`: each rate lies between 0.3 / 2048 and 1 / 24.
All inputs are finite; a program needn't handle non-finite values.
Results may differ from the reference program's by a relative error of at most 0.019.
Values may be sent and summed in bfloat16 or wider, within the bound.
A program may use at most 320 MiB of HBM per device.

```python
import math
import jax
import jax.numpy as jnp
from jax import lax

D = 1024
HEADS = 32
HEADDIM = 64
STATE = 128
CONV = 4
GROUP = 256
SEQS = 4
INNER = 2048
SEQ_LEN = 2048


def draw_norm_gain(key, part):
    key = jax.random.fold_in(key, 11)
    ramp = jnp.exp(jnp.linspace(math.log(0.6), math.log(1.8), D))
    noise = jnp.clip(0.1 * jax.random.normal(key, (D,), jnp.float32), -0.3, 0.3)
    return ramp * (1.0 + noise)


def draw_value_weight(key, part):
    key = jax.random.fold_in(key, 12)
    ramp = jnp.exp(jnp.linspace(math.log(0.75), math.log(1.5), INNER))
    entries = jnp.clip(jax.random.normal(key, (D, INNER), jnp.float32), -5.0, 5.0)
    return (entries * ramp[None, :] / math.sqrt(D)).astype(jnp.bfloat16)


def draw_decay_rate(key, part):
    key = jax.random.fold_in(key, 13)
    pick_key, fast_key, slow_key = jax.random.split(key, 3)
    share = 0.5
    fast_rate = jnp.exp(jax.random.uniform(fast_key, (HEADS,), jnp.float32, math.log(1.0 / 40.0), math.log(1.0 / 24.0)))
    slow_rate = jnp.exp(jax.random.uniform(slow_key, (HEADS,), jnp.float32, math.log(0.3 / SEQ_LEN), math.log(2.0 / SEQ_LEN)))
    return jnp.where(jax.random.uniform(pick_key, (HEADS,), jnp.float32) < share, fast_rate, slow_rate)


def block_levels(own_key, dims, cuts, smallest, largest):
    factor_of = 1.0
    for position, shards_of in cuts:
        draws = jax.random.uniform(jax.random.fold_in(jax.random.fold_in(own_key, 6), position), (shards_of,), jnp.float32, smallest / len(cuts), largest / len(cuts))
        factor_of = factor_of * jnp.repeat(jnp.exp(draws), dims[position] // shards_of).reshape((-1,) + (1,) * (len(dims) - 1 - position))
    return factor_of


def centred(rng, extent, width, bound, cuts=(), kind=jnp.bfloat16):
    gain = block_levels(rng, extent, cuts, -0.22, 0.18) if cuts else 1.0
    result = jax.random.normal(rng, extent, jnp.float32) * width * gain
    return jnp.minimum(jnp.maximum(result, -bound), bound).astype(kind)


def setup_inputs(seed: int = 0) -> dict:
    key_of = jax.random.split(jax.random.key(seed), 17)
    tokens = centred(key_of[0], (SEQS, SEQ_LEN, D), 1.0, 6.0, ((1, 8),))
    norm_gain = draw_norm_gain(jax.random.fold_in(key_of[16], 71), 0)
    gate_weight = centred(key_of[2], (D, INNER), D ** -0.5, 0.1875, ((1, 4),))
    value_weight = draw_value_weight(jax.random.fold_in(key_of[16], 71), 0)
    shared_weight = centred(key_of[4], (D, 2 * STATE), (64 * D) ** -0.5, 0.0234375)
    step_weight = centred(key_of[5], (D, HEADS), D ** -0.5, 0.1875, ((1, 4),))
    conv_value = centred(key_of[6], (CONV, INNER), CONV ** -0.5, 3.0, ((1, 4),), jnp.float32)
    conv_value_bias = centred(key_of[7], (INNER,), 0.3, 1.8, ((0, 4),), jnp.float32)
    conv_shared = centred(key_of[8], (CONV, 2 * STATE), CONV ** -0.5, 3.0, (), jnp.float32)
    conv_shared_bias = centred(key_of[9], (2 * STATE,), 0.1, 0.6, (), jnp.float32)
    step_bias = jnp.clip(jax.random.uniform(key_of[10], (HEADS,), jnp.float32, -1.0, 1.0) * block_levels(key_of[10], (HEADS,), ((0, 4),), -0.4, 0.0), -1.0, 1.0)
    decay_rate = draw_decay_rate(jax.random.fold_in(key_of[16], 71), 0)
    skip_weight = jnp.clip(0.5 + 1.0 * jax.random.uniform(key_of[12], (HEADS,), jnp.float32) ** block_levels(key_of[12], (HEADS,), ((0, 4),), -0.2, 0.2), 0.5, 1.5)
    out_gain = jnp.clip(1.0 + 0.1 * jax.random.normal(key_of[13], (INNER,), jnp.float32), 0.5, 1.5)
    output_weight = centred(key_of[14], (INNER, D), INNER ** -0.5, 0.125, ((0, 4),))
    cotangent = centred(key_of[15], (SEQS, SEQ_LEN, D), 1.0, 6.0, ((1, 8), (2, 4)))
    return dict(tokens=tokens, norm_gain=norm_gain, gate_weight=gate_weight, value_weight=value_weight, shared_weight=shared_weight, step_weight=step_weight, conv_value=conv_value, conv_value_bias=conv_value_bias, conv_shared=conv_shared, conv_shared_bias=conv_shared_bias, step_bias=step_bias, decay_rate=decay_rate, skip_weight=skip_weight, out_gain=out_gain, output_weight=output_weight, cotangent=cotangent)


EPSILON = 1e-05
FULL_PRECISION = lax.Precision.HIGHEST

@jax.custom_vjp
def low(v):
    return lax.optimization_barrier(v.astype(jnp.bfloat16)).astype(jnp.float32)

@jax.custom_vjp
def lower_backward(v):
    return v

def low_keep(v):
    return (low(v), None)

def low_pass(kept, grad):
    return (grad,)

def back_keep(v):
    return (v, None)

def back_low(kept, grad):
    return (low(grad),)
low.defvjp(low_keep, low_pass)
lower_backward.defvjp(back_keep, back_low)

def silu_act(argument):
    return argument * jax.nn.sigmoid(argument)

def causal_conv(signal, weight_matrix, bias_row):
    taps = weight_matrix.shape[0]
    seq_total = signal.shape[1]
    padded = jnp.pad(signal, ((0, 0), (taps - 1, 0), (0, 0)))
    running = bias_row + jnp.zeros_like(signal)
    for offset in range(taps):
        running = running + weight_matrix[offset] * padded[:, offset:offset + seq_total, :]
    return running

def group_core(carry_state, pieces):
    values, keys_state, reads_state, logdecay, steps, skip_row = pieces
    cumulative = jnp.cumsum(logdecay, axis=1)
    scores = jnp.einsum('stn,sun->stu', reads_state, keys_state, precision=FULL_PRECISION)
    block_rows = cumulative.shape[1]
    causal_mask = (lax.broadcasted_iota(jnp.int32, (block_rows, block_rows), 0) >= lax.broadcasted_iota(jnp.int32, (block_rows, block_rows), 1))[None, :, :, None]
    log_gaps = cumulative[:, :, None, :] - cumulative[:, None, :, :]
    decays = jnp.where(causal_mask, jnp.exp(jnp.where(causal_mask, log_gaps, 0.0)), 0.0)
    weights = decays * scores[:, :, :, None] * steps[:, None, :, :]
    inner = jnp.einsum('stuh,suhp->sthp', weights, values, precision=FULL_PRECISION)
    outer = jnp.exp(cumulative)[..., None] * jnp.einsum('stn,shpn->sthp', reads_state, carry_state, precision=FULL_PRECISION)
    output = inner + outer + skip_row[:, None] * values
    tail_weight = jnp.exp(cumulative[:, -1:, :] - cumulative) * steps
    new_state = jnp.exp(cumulative[:, -1, :])[:, :, None, None] * carry_state + jnp.einsum('sth,sthp,stn->shpn', tail_weight, values, keys_state, precision=FULL_PRECISION)
    return (new_state, output)

def forward(input_rows, norm_gain, gate_weight, value_weight, shared_weight, step_weight, conv_value, conv_value_bias, conv_shared, conv_shared_bias, step_bias, decay_rate, skip_weight, out_gain, output_weight):
    batches = input_rows.shape[0]
    seq_total = input_rows.shape[1]
    rms_scale = lax.rsqrt(lax.optimization_barrier(jnp.mean(input_rows * input_rows, axis=-1, keepdims=True)) + EPSILON)
    normalized = low(input_rows * rms_scale * norm_gain)
    gate_projected = lower_backward(jnp.einsum('pfn,nv->pfv', normalized, gate_weight, precision=FULL_PRECISION))
    value_projected = lower_backward(jnp.einsum('pfn,nv->pfv', normalized, value_weight, precision=FULL_PRECISION))
    shared_projected = lower_backward(jnp.einsum('pfn,nv->pfv', normalized, shared_weight, precision=FULL_PRECISION))
    unscaled_step = lower_backward(jnp.einsum('pfn,nv->pfv', normalized, step_weight, precision=FULL_PRECISION))
    mixed_value = low(silu_act(causal_conv(value_projected, conv_value, conv_value_bias)))
    mixed_shared = low(silu_act(causal_conv(shared_projected, conv_shared, conv_shared_bias)))
    steps = jax.nn.softplus(unscaled_step + step_bias)
    logdecay = -steps * decay_rate
    group_count = seq_total // GROUP

    def blocks(array):
        shaped = array.reshape((batches, group_count, GROUP) + array.shape[2:])
        return jnp.moveaxis(shaped, 1, 0)
    values = blocks(mixed_value.reshape(batches, seq_total, HEADS, HEADDIM))
    keys_state = blocks(mixed_shared[:, :, :STATE])
    reads_state = blocks(mixed_shared[:, :, STATE:])
    skip_rows = jnp.broadcast_to(skip_weight, (group_count, HEADS))
    start_state = jnp.zeros((batches, HEADS, HEADDIM, STATE), jnp.float32)
    _, outputs = lax.scan(jax.checkpoint(group_core), start_state, (values, keys_state, reads_state, blocks(logdecay), blocks(steps), skip_rows))
    ssd_out = jnp.moveaxis(outputs, 0, 1).reshape(batches, seq_total, INNER)
    gated = ssd_out * silu_act(gate_projected)
    gate_scale = lax.rsqrt(lax.optimization_barrier(jnp.mean(gated * gated, axis=-1, keepdims=True)) + EPSILON)
    normalized_output = low(gated * gate_scale * out_gain)
    return input_rows + jnp.einsum('ufc,cq->ufq', normalized_output, output_weight, precision=FULL_PRECISION)

def reference(tokens, norm_gain, gate_weight, value_weight, shared_weight, step_weight, conv_value, conv_value_bias, conv_shared, conv_shared_bias, step_bias, decay_rate, skip_weight, out_gain, output_weight, cotangent):
    params = (tokens.astype(jnp.float32), norm_gain, gate_weight.astype(jnp.float32), value_weight.astype(jnp.float32), shared_weight.astype(jnp.float32), step_weight.astype(jnp.float32), conv_value, conv_value_bias, conv_shared, conv_shared_bias, step_bias, decay_rate, skip_weight, out_gain, output_weight.astype(jnp.float32))
    primal, pullback = jax.vjp(forward, *params)
    grads = pullback(cotangent.astype(jnp.float32))
    return (primal.astype(jnp.bfloat16), grads[0], grads[1], grads[2], grads[3], grads[4], grads[5], grads[6], grads[7], grads[8], grads[9], grads[10], grads[11], grads[12], grads[13], grads[14])
```

```python
import jax
import jax.numpy as jnp
from jax import lax
from jax.experimental import pallas as pl
from jax.experimental.pallas import tpu as pltpu
from jax.sharding import PartitionSpec as P

EPSILON = 1e-05
F32 = jnp.float32
BF = jnp.bfloat16
MESH = pl.DeviceIdType.MESH
LANES = 128


def mm(a, b):
    return lax.dot_general(a, b, (((1,), (0,)), ((), ())), preferred_element_type=F32)


def nt(a, b):
    return lax.dot_general(a, b, (((1,), (1,)), ((), ())), preferred_element_type=F32)


def tn(a, b):
    return lax.dot_general(a, b, (((0,), (0,)), ((), ())), preferred_element_type=F32)


def split(x):
    high = x.astype(BF)
    return high, (x - high.astype(F32)).astype(BF)


def mm_exact_left(a, x):
    high, rest = x.astype(BF), x - x.astype(BF).astype(F32)
    mid, low = split(rest)
    return mm(a, high) + (mm(a, mid) + mm(a, low))


def sigmoid(x):
    return 1.0 / (1.0 + jnp.exp(-x))


def loop(count, body):
    def step(i, carry):
        body(i)
        return carry

    lax.fori_loop(0, count, step, 0)


class Reduced:
    def __init__(self, buf, base, rows, inbox, inbase, levels, sems, first):
        self.buf, self.inbox, self.levels = buf, inbox, levels
        self.send, self.recv, self.free = sems
        self.first = first
        self.lo, self.size, self.stack, self.offset = base, rows, [], inbase
        self.copies = {}

    def copy(self, src, dst, slot, partner):
        return pltpu.make_async_remote_copy(
            src_ref=src,
            dst_ref=dst,
            send_sem=self.send.at[slot],
            recv_sem=self.recv.at[slot],
            device_id=partner,
            device_id_type=MESH,
        )

    def start(self, level):
        partner, bit = self.levels[level]
        halved = self.size // 2 >= 16
        part = self.size // 2 if halved else self.size
        theirs = self.lo + (1 - bit) * part if halved else self.lo
        mine = self.lo + bit * part if halved else self.lo
        copy = self.copy(
            self.buf.at[pl.ds(pl.multiple_of(theirs, 16), part), :],
            self.inbox.at[pl.ds(self.offset, part), :],
            self.first + level,
            partner,
        )
        copy.start()
        self.copies[level] = (copy, mine, part, self.offset, halved)
        self.offset += part

    def finish(self, level):
        copy, mine, part, offset, halved = self.copies[level]
        copy.wait()
        if halved:
            pl.semaphore_signal(
                self.free.at[self.first + level],
                inc=1,
                device_id=self.levels[level][0],
                device_id_type=MESH,
            )
        block = min(part, 64)

        def add(i):
            rows = pl.ds(pl.multiple_of(mine + i * block, 16), block)
            got = self.inbox[pl.ds(pl.multiple_of(offset + i * block, 16), block), :]
            self.buf[rows, :] = (self.buf[rows, :].astype(F32) + got.astype(F32)).astype(BF)

        loop(part // block, add)
        self.stack.append((self.lo, self.size, halved))
        self.lo, self.size = mine, part

    def spread_start(self, level):
        slot = self.first + len(self.levels) + level
        rows = pl.ds(pl.multiple_of(self.lo, 16), self.size)
        pl.semaphore_wait(self.free.at[self.first + level], 1)
        self.copies[level] = self.copy(self.buf.at[rows, :], self.buf.at[rows, :], slot, self.levels[level][0])
        self.copies[level].start()

    def steps(self):
        count = len(self.levels)
        for level in range(count):
            self.start(level)
            yield
            self.finish(level)
        for level in range(count - 1, -1, -1):
            lo, size, halved = self.stack[level]
            if halved:
                self.spread_start(level)
                yield
                self.copies[level].wait()
            self.lo, self.size = lo, size


def kernel(dims, *refs):
    n, S, T, D, C, H, N, F = dims
    PW = C // H
    Sh = S // 2
    R = Sh * C // n
    q = n // Sh
    groups = max(1, R // PW)
    span = R // groups
    names = dims_names(dims)
    ref = dict(zip(names, refs))

    class A:
        pass

    a = A()
    a.__dict__.update(ref)
    me = lax.axis_index("seq")
    head = lax.axis_index("head")
    flip = lambda value, bit: value + bit - 2 * bit * lax.rem(value // bit, 2)
    core_peer = (me, flip(head, 1))
    x_peer = (me, flip(head, 2))
    diag = (me, flip(flip(head, 1), 2))
    barrier = pltpu.get_barrier_semaphore()
    for peer in (core_peer, x_peer, diag):
        pl.semaphore_signal(barrier, inc=1, device_id=peer, device_id_type=MESH)

    def greet(i):
        peer = (lax.rem(me + i + 1, n), head)
        pl.semaphore_signal(barrier, inc=1, device_id=peer, device_id_type=MESH)

    loop(n - 1, greet)

    lane = lax.broadcasted_iota(jnp.int32, (T, LANES), 1)
    first_half = lane < PW

    rows_i = lax.broadcasted_iota(jnp.int32, (T, T), 0)
    cols_i = lax.broadcasted_iota(jnp.int32, (T, T), 1)
    a.tri[...] = jnp.where(rows_i >= cols_i, 1.0, 0.0).astype(BF)
    a.triT[...] = jnp.where(rows_i <= cols_i, 1.0, 0.0).astype(BF)
    er = lax.broadcasted_iota(jnp.int32, (2 * LANES, C), 0)
    ec_ = lax.broadcasted_iota(jnp.int32, (2 * LANES, C), 1)
    a.E2[...] = jnp.where(lax.rem(er, LANES) == ec_ // PW, 1.0, 0.0).astype(BF)
    tr = lax.broadcasted_iota(jnp.int32, (C, LANES), 0)
    tc = lax.broadcasted_iota(jnp.int32, (C, LANES), 1)
    a.ET[...] = jnp.where(tr // PW == tc, 1.0, 0.0).astype(BF)
    a.stT[...] = jnp.zeros(a.stT.shape, BF)
    a.stT[0:H, :] = a.step_weight[...]
    a.small[...] = jnp.zeros(a.small.shape, F32)
    a.heads_sm[...] = jnp.zeros(a.heads_sm.shape, F32)
    a.shsm[...] = jnp.zeros(a.shsm.shape, F32)
    a.hrow[...] = jnp.zeros(a.hrow.shape, F32)
    a.hrow[0:1, 0:H] = a.step_bias[...]
    a.hrow[1:2, 0:H] = a.decay_rate[...]
    a.hrow[2:3, 0:H] = a.skip_weight[...]
    bias_row = a.hrow[0:1, :]
    rate_row = a.hrow[1:2, :]

    def expand(x):
        high, low = split(x)
        return mm(jnp.concatenate([high, low], axis=1), a.E2[...])

    a.skipE[...] = expand(jnp.broadcast_to(a.hrow[2:3, :], (8, LANES)))
    skip_row = a.skipE[0:1, :]
    gain = a.norm_gain[...]

    def norm_rows(x):
        scale = lax.rsqrt(jnp.mean(x * x, axis=-1, keepdims=True) + EPSILON)
        return (x * scale * gain).astype(BF), scale

    def norm_block(b):
        s, r = b // 4, pl.multiple_of(lax.rem(b, 4) * (T // 4), T // 4)
        rows = pl.ds(r, T // 4)
        x = a.tokens[s, rows, :].astype(F32)
        low, scale = norm_rows(x)
        a.normed[s, rows, :] = low
        a.rms[s, rows, :] = jnp.broadcast_to(scale, (T // 4, LANES))

    pl.semaphore_wait(barrier, n - 1 + 3)

    def halo_copy():
        return pltpu.make_async_remote_copy(
            src_ref=a.tokens.at[:, pl.ds(T - 16, 16), :],
            dst_ref=a.halo,
            send_sem=a.ssem.at[0],
            recv_sem=a.rsem.at[0],
            device_id=(lax.rem(me + 1, n), head),
            device_id_type=MESH,
        )

    @pl.when(me < n - 1)
    def _():
        halo_copy().start()

    def cot_copy(src, slot, sem, peer):
        return pltpu.make_async_remote_copy(
            src_ref=src,
            dst_ref=a.cotf.at[slot],
            send_sem=a.ssem.at[sem],
            recv_sem=a.rsem.at[sem],
            device_id=peer,
            device_id_type=MESH,
        )

    cot_x = cot_copy(a.cotangent, head, 1, x_peer)
    cot_x.start()
    cot_c = cot_copy(a.cotangent, head, 2, core_peer)
    cot_c.start()
    cot_own = pltpu.make_async_copy(a.cotangent, a.cotf.at[head], a.lsem.at[0])
    cot_own.start()

    def half(which, f):
        loop(Sh, lambda i: f(which * Sh + i))

    loop(4 * Sh, norm_block)

    def project_b(s):
        x = a.normed[s]
        a.vext[s, 8 : 8 + T, :] = mm(x, a.value_weight[...])
        a.sext[s, 8 : 8 + T, :] = mm(x, a.shared_weight[...])
        a.raw[s] = nt(x, a.stT[...]) + bias_row

    half(0, project_b)

    @pl.when(me > 0)
    def _():
        halo_copy().wait_recv()

    @pl.when(me == 0)
    def _():
        a.halo[...] = jnp.zeros(a.halo.shape, BF)

    @pl.when(me < n - 1)
    def _():
        halo_copy().wait_send()

    hx = jnp.concatenate([a.halo[s] for s in range(S)], axis=0).astype(F32)
    hlow, _ = norm_rows(hx)
    vh = mm(hlow, a.value_weight[...])
    sh = mm(hlow, a.shared_weight[...])
    for s in range(S):
        a.vext[s, 0:8, :] = vh[s * 16 + 8 : s * 16 + 16, :]
        a.sext[s, 0:8, :] = sh[s * 16 + 8 : s * 16 + 16, :]

    def conv(ext, w, b, s, c):
        running = b[0:1, c : c + LANES] + jnp.zeros((T, LANES), F32)
        for k in range(4):
            running = running + w[k : k + 1, c : c + LANES] * ext[s, pl.ds(5 + k, T), c : c + LANES]
        sig = sigmoid(running)
        return running * sig, sig * (1.0 + running * (1.0 - sig))

    def states(tag, reverse):
        m1, o2 = a.__dict__["m1" + tag[1]], a.__dict__["o2" + tag[1]]
        i1, i2 = (a.__dict__[k + tag] for k in ("i1", "i2"))
        s1, r1, s2, r2 = (a.__dict__[k + tag] for k in ("s1", "r1", "s2", "r2"))

        def first(k):
            return pltpu.make_async_remote_copy(
                src_ref=m1.at[k],
                dst_ref=i1.at[me],
                send_sem=s1.at[k],
                recv_sem=r1.at[me],
                device_id=(k, head),
                device_id_type=MESH,
            )

        def first_wait(k):
            return pltpu.make_async_remote_copy(
                src_ref=m1.at[k],
                dst_ref=i1.at[k],
                send_sem=s1.at[k],
                recv_sem=r1.at[k],
                device_id=(k, head),
                device_id_type=MESH,
            )

        def second(k):
            return pltpu.make_async_remote_copy(
                src_ref=o2.at[k],
                dst_ref=i2.at[me],
                send_sem=s2.at[k],
                recv_sem=r2.at[me],
                device_id=(k, head),
                device_id_type=MESH,
            )

        def second_wait(k):
            return pltpu.make_async_remote_copy(
                src_ref=o2.at[k],
                dst_ref=i2.at[k],
                send_sem=s2.at[k],
                recv_sem=r2.at[k],
                device_id=(k, head),
                device_id_type=MESH,
            )

        none = n - 1 if reverse else 0

        def pack(i, state, decay):
            high, low = split(decay)
            hf, lf = high.astype(F32), low.astype(F32)
            for j in range(q):
                h0 = j * R // PW
                k = i * q + j
                m1[k, 0:R, :] = state[j * R : (j + 1) * R, :].astype(BF)
                both = [hf[h0:], hf[:h0], lf[h0:], lf[:h0]] if h0 else [hf, lf]
                m1[k, R : R + 16, :] = jnp.concatenate(both, axis=0).astype(BF)

                @pl.when(k != me)
                def _():
                    first(k).start()

                @pl.when(k == me)
                def _():
                    i1[k] = m1[k]

        group_row = lax.broadcasted_iota(jnp.int32, (8, LANES), 0)
        group_lane = lax.broadcasted_iota(jnp.int32, (8, LANES), 1) // span

        def join():
            def wait(k):
                @pl.when(k != me)
                def _():
                    first_wait(k).wait()

            loop(n, wait)

            def one(step):
                j = n - 1 - step if reverse else step
                tail = i1[j, R : R + 16, :].astype(F32)
                decay = tail[0:8] + tail[8:16]
                now = a.joined[step % 2 if isinstance(step, int) else lax.rem(step, 2)]
                means = [jnp.mean(now[g * span : (g + 1) * span], axis=0, keepdims=True) for g in range(groups)]
                means = jnp.concatenate(means + [jnp.zeros((8 - groups, LANES), F32)], axis=0)
                size = jnp.sum(means * means, axis=1, keepdims=True) + 1e-30
                along = nt(means.astype(BF), now.astype(BF)) / size
                along = jnp.where(group_row == group_lane, along, 0.0)
                ah, mh = along.astype(BF).astype(F32), means.astype(BF).astype(F32)
                al, ml = (along - ah).astype(BF).astype(F32), (means - mh).astype(BF).astype(F32)
                left, right = [], []
                for g in range(groups):
                    row = slice(g, g + 1)
                    left += [ah[row], ah[row], al[row]]
                    right += [mh[row], ml[row], mh[row]]
                rest = [jnp.zeros((8 - 3 * groups, LANES), F32)]
                left, right = jnp.concatenate(left + rest, axis=0), jnp.concatenate(right + rest, axis=0)
                o2[j, 0:R, :] = (now - tn(left, right))[0:R].astype(BF)
                o2[j, R : R + 16, :] = jnp.concatenate([left, right], axis=0).astype(BF)
                after = [
                    decay[g : g + 1, :] * now[g * span : (g + 1) * span]
                    + i1[j, g * span : (g + 1) * span, :].astype(F32)
                    for g in range(groups)
                ]
                if R < LANES:
                    after.append(jnp.zeros((LANES - R, N), F32))
                a.joined[(step + 1) % 2 if isinstance(step, int) else lax.rem(step + 1, 2)] = jnp.concatenate(after, axis=0)

                @pl.when((j != me) & (j != none))
                def _():
                    second(j).start()

                @pl.when((j == me) & (j != none))
                def _():
                    i2[j] = o2[j]

            a.joined[0] = jnp.zeros((LANES, N), F32)
            if n <= 8:
                for step in range(n):
                    one(step)
            else:
                loop(n, one)

        def collect(out, base):
            def wait(k):
                @pl.when((k != me) & (me != none))
                def _():
                    second_wait(k).wait_recv()

                @pl.when((k != me) & (k != none))
                def _():
                    second_wait(k).wait_send()

            loop(n, wait)

            @pl.when(me != none)
            def _():
                def one(k):
                    tail = i2[k, R : R + 16, :].astype(F32)
                    got = i2[k, 0:R, :].astype(F32) + tn(tail[0:8], tail[8:16])[0:R]
                    out[pl.ds(pl.multiple_of(base + k * R, 16), R), :] = got

                if n <= 8:
                    for k in range(n):
                        one(k)
                else:
                    loop(n, one)

            @pl.when(me == none)
            def _():
                out[base : base + Sh * C, :] = jnp.zeros((Sh * C, N), F32)

        return pack, join, collect

    forward = [states("f" + x, False) for x in "01"]
    backward = [states("b" + x, True) for x in "01"]

    def scan_inputs(s, i, pack):
        for c in range(0, C, LANES):
            v, d = conv(a.vext, a.conv_value, a.conv_value_bias, s, c)
            a.V[s, :, c : c + LANES] = v.astype(BF)
            a.dsv[s, :, c : c + LANES] = d.astype(BF)
        for c in range(0, 2 * N, LANES):
            v, d = conv(a.sext, a.conv_shared, a.conv_shared_bias, s, c)
            a.KR[s, :, c : c + LANES] = v.astype(BF)
            a.dss[s, :, c : c + LANES] = d.astype(BF)
        raw = a.raw[s]
        steps = jnp.maximum(raw, 0.0) + jnp.log1p(jnp.exp(-jnp.abs(raw)))
        a.steps[s] = steps
        cum = mm_exact_left(a.tri[...], -steps * rate_row)
        a.cum[s] = cum
        cumT = cum.T[0:8]
        a.cumT[s] = cumT
        last = cum[T - 1 : T, :]
        tail = jnp.exp(last - cum)
        V = a.V[s].astype(F32)
        a.U[s] = (expand(steps) * V).astype(BF)
        tU = (expand(steps * tail) * V).astype(BF)
        a.tU[s] = tU
        state = tn(tU, a.KR[s, :, 0:N])
        a.sp[pl.ds(pl.multiple_of(s * C, C), C), :] = state
        decay = jnp.broadcast_to(jnp.exp(cumT[:, T - 1 : T]), (8, LANES))
        a.decay[s] = decay
        pack(i, state, decay)

    def scan_half(which):
        loop(Sh, lambda i: scan_inputs(which * Sh + i, i, forward[which][0]))

    scan_half(0)
    loop(4 * Sh, lambda b: norm_block(4 * Sh + b))
    half(1, project_b)
    scan_half(1)

    def project_gate(s):
        a.gate[s] = mm(a.normed[s], a.gate_weight[...])

    def intra_forward(s):
        K, Rm = a.KR[s, :, 0:N], a.KR[s, :, N : 2 * N]
        G = jnp.where(rows_i >= cols_i, nt(Rm, K), 0.0)
        for p in range(H // 2):
            pair = slice(p * LANES, (p + 1) * LANES)
            U2 = a.U[s, :, pair]
            z = []
            for h in (2 * p, 2 * p + 1):
                gap = a.cum[s, :, h : h + 1] - a.cumT[s, h : h + 1, :]
                M = (jnp.exp(jnp.minimum(gap, 0.0)) * G).astype(BF)
                z.append(mm(M, U2))
            a.Y[s, :, pair] = jnp.where(first_half, z[0], z[1])

    loop(S, project_gate)
    half(0, intra_forward)
    forward[0][1]()
    half(1, intra_forward)

    cot_x.wait()
    cot_f = cot_copy(a.cotf.at[flip(head, 2)], flip(head, 2), 3, core_peer)
    cot_f.start()
    cot_c.wait()
    cot_f.wait()
    cot_own.wait()

    def back_out(s):
        total = nt(a.cotf[0, s], a.output_weight[:, 0:F])
        for f in range(1, D // F):
            total = total + nt(a.cotf[f, s], a.output_weight[:, f * F : (f + 1) * F])
        a.dext[s, 0:T, :] = total

    loop(S, back_out)
    forward[1][1]()

    def transposed(s):
        rows = pl.ds(pl.multiple_of(s * T, T), T)
        for c in range(0, D, 256):
            a.normT[c : c + 256, rows] = a.normed[s, :, c : c + 256].T

    loop(S, transposed)

    def outputs(s, i, stat):
        rows = pl.ds(pl.multiple_of(s * C, C), C)
        high, low = split(a.Sin[rows, :])
        Rm = a.KR[s, :, N : 2 * N]
        reach = expand(jnp.exp(a.cum[s]))
        outer = reach * (nt(Rm, high) + nt(Rm, low))
        Y = a.Y[s] + outer + skip_row * a.V[s].astype(F32)
        a.Y[s] = Y
        g = a.gate[s]
        gated = Y * (g * sigmoid(g))
        dots = a.dext[s, 0:T, :] * a.out_gain[...] * gated
        ones = jnp.ones((8, C), BF)
        sq = nt(ones, (gated * gated).astype(BF))
        dt = nt(ones, dots.astype(BF))
        row8 = lax.broadcasted_iota(jnp.int32, (8, T), 0)
        part = jnp.where(row8 == 2 * i, sq, 0.0) + jnp.where(row8 == 2 * i + 1, dt, 0.0)
        stat[...] = part + jnp.where(row8 < 2 * i, stat[...], 0.0)

    def head_sums(stat, inbox, first):
        return [
            pltpu.make_async_remote_copy(
                src_ref=stat,
                dst_ref=inbox.at[i],
                send_sem=a.ssem.at[first + i],
                recv_sem=a.rsem.at[first + i],
                device_id=peer,
                device_id_type=MESH,
            )
            for i, peer in enumerate((x_peer, diag, core_peer))
        ]

    stats = [head_sums(a.stat.at[w], a.stin.at[w], 9 + 3 * w) for w in range(2)]
    inner = C * lax.axis_size("head")

    def output_half(w):
        a.stat[w] = jnp.zeros((8, T), F32)
        loop(Sh, lambda i: outputs(w * Sh + i, i, a.stat.at[w]))
        for copy in stats[w]:
            copy.start()

    def stat_half(w):
        for copy in stats[w]:
            copy.wait()
        total = a.stat[w] + (a.stin[w, 0] + a.stin[w, 1]) + a.stin[w, 2]
        columns = []
        for i in range(Sh):
            scale = lax.rsqrt(total[2 * i : 2 * i + 1] / inner + EPSILON)
            columns += [scale, total[2 * i + 1 : 2 * i + 2] * scale / inner]
        stacked = jnp.concatenate(columns + [jnp.zeros((LANES - 2 * Sh, T), F32)], axis=0).T
        for i in range(Sh):
            a.gscale[i] = jnp.broadcast_to(stacked[:, 2 * i : 2 * i + 1], (T, LANES))
            a.gmean[i] = jnp.broadcast_to(stacked[:, 2 * i + 1 : 2 * i + 2], (T, LANES))

    def gate_back(s, i, pack):
        reach = expand(jnp.exp(a.cum[s]))
        scale, mean = a.gscale[i], a.gmean[i]
        cols = pl.ds(pl.multiple_of(s * T, T), T)
        for c in range(0, C, LANES):
            ch = slice(c, c + LANES)
            g, Y = a.gate[s, :, ch], a.Y[s, :, ch]
            sig = sigmoid(g)
            act = g * sig
            gu = Y * act * scale
            og = a.out_gain[0:1, ch]
            ny = gu * og
            a.ny[s, :, ch] = ny.astype(BF)
            a.nyT[ch, cols] = ny.T.astype(BF)
            dn = a.dext[s, 0:T, ch]
            a.small[5:6, ch] += jnp.sum(dn * gu, axis=0, keepdims=True)
            dg = scale * (dn * og - gu * mean)
            dY = (dg * act).astype(BF)
            a.dY[s, :, ch] = dY
            a.ecdY[s, :, ch] = (reach[:, ch] * dY.astype(F32)).astype(BF)
            a.normed[s, :, ch] = (dg * Y * sig * (1.0 + g * (1.0 - sig))).astype(BF)
        state = tn(a.ecdY[s], a.KR[s, :, N : 2 * N])
        pack(i, state, a.decay[s])

    for w in range(2):
        forward[w][2](a.Sin, w * Sh * C)
        output_half(w)
    for w in range(2):
        stat_half(w)
        loop(Sh, lambda i: gate_back(w * Sh + i, i, backward[w][0]))

    levels = []
    bit = 1
    while bit < n:
        levels.append(((flip(me, bit), head), lax.rem(me // bit, 2)))
        bit *= 2
    L = len(levels)
    sems = (a.asend, a.arecv, a.afree)
    head_levels = [(core_peer, lax.rem(head, 2)), (x_peer, lax.rem(head // 2, 2))]
    tasks, used = {}, 0
    for name, buf, inbox, count, order in (
        ("O", a.gwo, a.gwo_in, 2, levels),
        ("G", a.gwg, a.gwg_in, 2, levels),
        ("V", a.gwv, a.gwv_in, 4, levels),
        ("S", a.gws, a.gws_in, 1, head_levels + levels),
    ):
        rows = buf.shape[0] // count
        for c in range(count):
            inbase = c * inbox_rows(rows, len(order))
            red = Reduced(buf, c * rows, rows, inbox, inbase, order, sems, used)
            tasks[name + str(c)] = red.steps()
            used += 2 * len(order)

    def pump(*names):
        for name in names:
            next(tasks[name], None)

    def feature_sum(tag, block):
        sb1, sb2 = a.sb1, a.sb2
        rb1, rb2 = (a.__dict__[k + tag] for k in ("rb1", "rb2"))
        sem = a.__dict__["fsem" + tag]

        def copy1(s):
            return pltpu.make_async_remote_copy(
                src_ref=sb1.at[s],
                dst_ref=rb1.at[s],
                send_sem=sem.at[0, s],
                recv_sem=sem.at[1, s],
                device_id=core_peer,
                device_id_type=MESH,
            )

        def copy2(s):
            return pltpu.make_async_remote_copy(
                src_ref=sb2.at[s],
                dst_ref=rb2.at[s],
                send_sem=sem.at[2, s],
                recv_sem=sem.at[3, s],
                device_id=x_peer,
                device_id_type=MESH,
            )

        def one(s):
            sb1[s, 0] = block(s, flip(head, 1)).astype(BF)
            sb1[s, 1] = block(s, flip(flip(head, 1), 2)).astype(BF)
            copy1(s).start()

        def two(s):
            far = block(s, flip(head, 2))
            copy1(s).wait()
            sb2[s] = (far + rb1[s, 1].astype(F32)).astype(BF)
            copy2(s).start()

        def three(s):
            near = block(s, head)
            copy2(s).wait()
            return near + rb1[s, 0].astype(F32) + rb2[s].astype(F32)

        return one, two, three

    def features(f):
        return pl.ds(pl.multiple_of(f * F, F), F)

    o_one, o_two, o_three = feature_sum("o", lambda s, f: mm(a.ny[s], a.output_weight[:, features(f)]))

    def grad_out_weight(half_index):
        for g in range(D // F // 2):
            f = half_index * (D // F // 2) + g
            x = mm(a.nyT[...], a.cotf[f].reshape(S * T, F))
            a.gwo[half_index * C : (half_index + 1) * C, g * F : (g + 1) * F] = x.astype(BF)

    def weight_grad(out, r, rows, columns):
        out[r : r + rows, :] = mm(a.normT[r : r + rows, :], columns()).astype(BF)

    grad_out_weight(0)
    pump("O0")
    grad_out_weight(1)
    pump("O1")
    backward[0][1]()
    loop(S, o_one)
    weight_grad(a.gwg, 0, D // 2, lambda: a.normed[:, :, 0:C].reshape(S * T, C))
    pump("G0")
    weight_grad(a.gwg, D // 2, D // 2, lambda: a.normed[:, :, 0:C].reshape(S * T, C))
    backward[1][1]()
    pump("O0", "G1")
    loop(S, o_two)
    pump("O1")

    def intra_backward(s):
        K, Rm = a.KR[s, :, 0:N], a.KR[s, :, N : 2 * N]
        GT = jnp.where(rows_i <= cols_i, nt(K, Rm), 0.0)
        dGT = jnp.zeros((T, T), F32)
        for p in range(H // 2):
            pair = slice(p * LANES, (p + 1) * LANES)
            dY2, U2 = a.dY[s, :, pair], a.U[s, :, pair]
            z = []
            for h in (2 * p, 2 * p + 1):
                gap = a.cumT[s, h : h + 1, :] - a.cum[s, :, h : h + 1]
                LT = jnp.exp(jnp.minimum(gap, 0.0))
                mine = first_half if h == 2 * p else jnp.logical_not(first_half)
                Um = jnp.where(mine, U2.astype(F32), 0.0).astype(BF)
                dGT = dGT + nt(Um, dY2) * LT
                z.append(mm((LT * GT).astype(BF), dY2))
            a.dext[s, 0:T, pair] = jnp.where(first_half, z[0], z[1])
        a.dGT[s] = jnp.where(rows_i <= cols_i, dGT, 0.0).astype(BF)

    def out_rows(s):
        total = o_three(s)
        own = a.tokens[s, :, features(head)].astype(F32)
        a.mixed[s] = (own + total).astype(BF)

    half(0, intra_backward)
    pump("O0", "O1")
    half(1, intra_backward)
    pump("G0", "O0", "O1")
    loop(S, out_rows)
    pump("G1", "O0")

    def state_back(s):
        rows = pl.ds(pl.multiple_of(s * C, C), C)
        K, Rm = a.KR[s, :, 0:N], a.KR[s, :, N : 2 * N]
        gout, Sin = a.gout[rows, :], a.Sin[rows, :]
        gob = gout.astype(BF)
        cum, steps = a.cum[s], a.steps[s]
        tail = expand(jnp.exp(cum[T - 1 : T, :] - cum))
        V = a.V[s].astype(F32)
        dY = a.dY[s].astype(F32)
        dU = a.dext[s, 0:T, :] + tail * nt(K, gob)
        skipV = skip_row * V
        dV = expand(steps) * dU + skip_row * dY
        a.small[6:7, :] += jnp.sum(dY * V, axis=0, keepdims=True)
        ph, plo = split(dU * V)
        dsd = mm(ph, a.ET[...]) + mm(plo, a.ET[...])
        ph, plo = split(dY * (a.Y[s] - skipV))
        row = mm(ph, a.ET[...]) + mm(plo, a.ET[...])
        dcv = dV * a.dsv[s].astype(F32)
        a.dext[s, 0:T, :] = dcv
        dGT = a.dGT[s]
        sh, sl = split(Sin)
        dK = mm(dGT, Rm) + mm(a.tU[s], gob)
        dR = tn(dGT, K) + (mm(a.ecdY[s], sh) + mm(a.ecdY[s], sl))
        a.dsext[s, 0:T, 0:N] = dK * a.dss[s, :, 0:N].astype(F32)
        a.dsext[s, 0:T, N : 2 * N] = dR * a.dss[s, :, N : 2 * N].astype(F32)
        decay = a.decay[s]
        sums = []
        for h in range(H):
            hs = slice(h * PW, (h + 1) * PW)
            sp = a.sp[pl.ds(pl.multiple_of(s * C + h * PW, PW), PW), :]
            sums.append(jnp.sum(gout[hs] * (decay[h : h + 1] * Sin[hs] + sp), axis=0, keepdims=True))
        sums = jnp.concatenate(sums + [jnp.zeros((LANES - H, LANES), F32)], axis=0)
        ones = jnp.ones((8, LANES), BF)
        lh, ll = split(sums)
        end = (nt(ones, lh) + nt(ones, ll))[0:1]
        dld = mm_exact_left(a.triT[...], row - steps * dsd) + end
        draw = (dsd - rate_row * dld) * sigmoid(a.raw[s])
        a.heads_sm[0:1, :] += jnp.sum(draw, axis=0, keepdims=True)
        a.heads_sm[1:2, :] -= jnp.sum(steps * dld, axis=0, keepdims=True)
        a.dst[s] = draw.astype(BF)
        a.dstT[:, pl.ds(pl.multiple_of(s * T, T), T)] = draw.T[0:16].astype(BF)

    backward[0][2](a.gout, 0)
    half(0, state_back)
    pump("O1", "G0", "G1")
    backward[1][2](a.gout, Sh * C)
    half(1, state_back)
    a.stepsum[...] = nt(a.dstT[...], a.normT[...])[0:8]

    def edge_copy(src, dst, sem):
        return pltpu.make_async_remote_copy(
            src_ref=src.at[:, pl.ds(0, 8), :],
            dst_ref=dst,
            send_sem=a.ssem.at[sem],
            recv_sem=a.rsem.at[sem],
            device_id=(lax.rem(me + n - 1, n), head),
            device_id_type=MESH,
        )

    edges = [edge_copy(a.dext, a.ev, 7), edge_copy(a.dsext, a.es, 8)]

    @pl.when(me > 0)
    def _():
        for copy in edges:
            copy.start()

    pump("O0", "G0", "G1")

    def conv_grads(s):
        for ext, grad, out, base, width in (
            (a.vext, a.dext, a.small, 0, C),
            (a.sext, a.dsext, a.shsm, 0, 2 * N),
        ):
            for c in range(0, width, LANES):
                ch = slice(c, c + LANES)
                d = grad[s, 0:T, ch]
                for k in range(4):
                    x = ext[s, pl.ds(5 + k, T), ch]
                    out[base + k : base + k + 1, ch] += jnp.sum(d * x, axis=0, keepdims=True)
                out[base + 4 : base + 5, ch] += jnp.sum(d, axis=0, keepdims=True)

    loop(S, conv_grads)
    a.pack[...] = jnp.zeros(a.pack.shape, F32)
    a.pack[0:7, 0:C] = a.small[0:7, :]
    a.pack[0:2, C : C + LANES] = a.heads_sm[0:2, :]
    a.pack[8:16, :] = a.stepsum[...]
    a.pack[16:21, 0 : 2 * N] = a.shsm[0:5, :]

    def whole_sum(buf, inbox, partners, first):
        for i, partner in enumerate(partners):
            copy = pltpu.make_async_remote_copy(
                src_ref=buf,
                dst_ref=inbox.at[i],
                send_sem=a.psend.at[first + i],
                recv_sem=a.precv.at[first + i],
                device_id=partner,
                device_id_type=MESH,
            )
            copy.start()
            yield
            copy.wait()
            buf[...] = buf[...] + inbox[i]

    def small_sums():
        partners = [partner for partner, _ in levels]
        yield from whole_sum(a.pack, a.packin, partners, 0)
        yield from whole_sum(a.pack.at[pl.ds(16, 8), :], a.shin, [x_peer, core_peer], L)

    tasks["P"] = small_sums()
    tasks["N"] = whole_sum(a.ngain, a.ngin, [partner for partner, _ in levels], L + 2)
    pump("P", "O1")

    @pl.when(me < n - 1)
    def _():
        for copy in edges:
            copy.wait_recv()
        for s in range(S):
            a.dext[s, T : T + 8, :] = a.ev[s]
            a.dsext[s, T : T + 8, :] = a.es[s]

    @pl.when(me == n - 1)
    def _():
        for s in range(S):
            a.dext[s, T : T + 8, :] = jnp.zeros((8, C), F32)
            a.dsext[s, T : T + 8, :] = jnp.zeros((8, 2 * N), F32)

    @pl.when(me > 0)
    def _():
        for copy in edges:
            copy.wait_send()

    def conv_back(s):
        for grad, w, out, shift, width in (
            (a.dext, a.conv_value, a.normed, C, C),
            (a.dsext, a.conv_shared, a.dsl, 0, 2 * N),
        ):
            for c in range(0, width, LANES):
                ch = slice(c, c + LANES)
                total = w[3:4, ch] * grad[s, 0:T, ch]
                for k in range(3):
                    total = total + w[k : k + 1, ch] * grad[s, pl.ds(3 - k, T), ch]
                out[s, :, shift + c : shift + c + LANES] = total.astype(BF)

    loop(S, conv_back)

    weight_grad(a.gws, 0, D, lambda: a.dsl[...].reshape(S * T, 2 * N))
    pump("S0")
    for c in range(4):
        weight_grad(a.gwv, c * D // 4, D // 4, lambda: a.normed[:, :, C : 2 * C].reshape(S * T, C))
        pump("V" + str(c))
        if c == 1:
            pump("S0", "P")
    pump("O0", "O1", "G0", "G1")

    def d_normed(s, f):
        rows = features(f)
        return (
            nt(a.normed[s, :, 0:C], a.gate_weight[rows, :])
            + nt(a.normed[s, :, C : 2 * C], a.value_weight[rows, :])
            + nt(a.dsl[s], a.shared_weight[rows, :])
            + mm(a.dst[s], a.stT[:, rows])
        )

    d_one, d_two, d_three = feature_sum("d", d_normed)
    half(0, d_one)
    pump("V0", "S0", "P")
    half(1, d_one)
    pump("V1", "V0", "O1", "S0")
    half(0, d_two)
    pump("V2", "V1", "V0", "P")
    half(1, d_two)
    pump("V3", "V2", "V1", "V0", "S0", "P")

    own_gain = a.norm_gain[0:1, features(head)]

    def feature_rows(s):
        d = d_three(s)
        a.dfeat[s] = d
        unit = a.tokens[s, :, features(head)].astype(F32) * a.rms[s][:, 0:1]
        a.ngain[0:1, :] += jnp.sum(d * unit, axis=0, keepdims=True)
        ones = jnp.ones((8, F), BF)
        dh, dl = split(d * own_gain * unit)
        dot = nt(ones, dh) + nt(ones, dl)
        row8 = lax.broadcasted_iota(jnp.int32, (8, T), 0)
        a.stat2[...] = jnp.where(row8 == s, dot, 0.0) + jnp.where(row8 < s, a.stat2[...], 0.0)

    a.ngain[...] = jnp.zeros(a.ngain.shape, F32)
    a.stat2[...] = jnp.zeros(a.stat2.shape, F32)
    half(0, feature_rows)
    pump("V3", "V2", "V1", "S0")
    half(1, feature_rows)
    stats2 = head_sums(a.stat2, a.stin2, 15)
    for copy in stats2:
        copy.start()
    pump("N", "V3", "V2", "P", "V0", "S0")
    for copy in stats2:
        copy.wait()
    total2 = a.stat2[...] + (a.stin2[0] + a.stin2[1]) + a.stin2[2]
    cols2 = jnp.concatenate([total2 / D, jnp.zeros((LANES - 8, T), F32)], axis=0).T
    for s in range(S):
        unit = a.tokens[s, :, features(head)].astype(F32) * a.rms[s][:, 0:1]
        inner_part = a.dfeat[s] * own_gain - unit * cols2[:, s : s + 1]
        a.gtok[s] = a.cotangent[s].astype(F32) + a.rms[s][:, 0:1] * inner_part
    order = ("N", "V3", "V1", "V0", "S0", "P", "O0", "O1", "G0", "G1", "V2")
    for _ in range(4 * (L + 3)):
        pump(*order)
    done = [
        pltpu.make_async_copy(a.gwo, a.out_gwo, a.lsem.at[1]),
        pltpu.make_async_copy(a.gwg, a.out_gwg, a.lsem.at[2]),
        pltpu.make_async_copy(a.gwv, a.out_gwv, a.lsem.at[3]),
        pltpu.make_async_copy(a.gws, a.out_gws, a.lsem.at[4]),
    ]
    for copy in done:
        copy.start()
    a.o_small[...] = a.pack[...]
    a.o_ngain[...] = a.ngain[...]
    for copy in done:
        copy.wait()


INPUTS = [
    "tokens",
    "norm_gain",
    "gate_weight",
    "value_weight",
    "shared_weight",
    "step_weight",
    "conv_value",
    "conv_value_bias",
    "conv_shared",
    "conv_shared_bias",
    "step_bias",
    "decay_rate",
    "skip_weight",
    "out_gain",
    "output_weight",
    "cotangent",
]
OUTPUTS = ["mixed", "gtok", "out_gwg", "out_gwv", "out_gws", "out_gwo", "o_small", "o_ngain"]


def inbox_rows(size, count):
    total = 0
    for _ in range(count):
        size = size // 2 if size // 2 >= 16 else size
        total += size
    return total


def scratch(dims):
    n, S, T, D, C, H, N, F = dims
    R = S // 2 * C // n
    L = n.bit_length() - 1
    vm = pltpu.VMEM
    dma = pltpu.SemaphoreType.DMA
    items = dict(
        tri=vm((T, T), BF),
        triT=vm((T, T), BF),
        E2=vm((2 * LANES, C), BF),
        ET=vm((C, LANES), BF),
        stT=vm((LANES, D), BF),
        skipE=vm((8, C), F32),
        hrow=vm((8, LANES), F32),
        small=vm((8, C), F32),
        heads_sm=vm((8, LANES), F32),
        shsm=vm((8, 2 * N), F32),
        normed=vm((S, T, D), BF),
        normT=vm((D, S * T), BF),
        rms=vm((S, T, LANES), F32),
        halo=vm((S, 16, D), BF),
        cotf=vm((D // F, S, T, F), BF),
        vext=vm((S, T + 8, C), F32),
        sext=vm((S, T + 8, 2 * N), F32),
        raw=vm((S, T, LANES), F32),
        steps=vm((S, T, LANES), F32),
        cum=vm((S, T, LANES), F32),
        cumT=vm((S, 8, T), F32),
        decay=vm((S, 8, LANES), F32),
        V=vm((S, T, C), BF),
        KR=vm((S, T, 2 * N), BF),
        dsv=vm((S, T, C), BF),
        dss=vm((S, T, 2 * N), BF),
        U=vm((S, T, C), BF),
        tU=vm((S, T, C), BF),
        sp=vm((S * C, N), F32),
        Sin=vm((S * C, N), F32),
        gout=vm((S * C, N), F32),
        joined=vm((2, LANES, N), F32),
        gate=vm((S, T, C), F32),
        Y=vm((S, T, C), F32),
        stat=vm((2, 8, T), F32),
        stin=vm((2, 3, 8, T), F32),
        stat2=vm((8, T), F32),
        stin2=vm((3, 8, T), F32),
        gscale=vm((S // 2, T, LANES), F32),
        gmean=vm((S // 2, T, LANES), F32),
        ny=vm((S, T, C), BF),
        nyT=vm((C, S * T), BF),
        dY=vm((S, T, C), BF),
        ecdY=vm((S, T, C), BF),
        dGT=vm((S, T, T), BF),
        dext=vm((S, T + 8, C), F32),
        dsext=vm((S, T + 8, 2 * N), F32),
        ev=vm((S, 8, C), F32),
        es=vm((S, 8, 2 * N), F32),
        dsl=vm((S, T, 2 * N), BF),
        dst=vm((S, T, LANES), BF),
        dstT=vm((16, S * T), BF),
        stepsum=vm((8, D), F32),
        gwo=vm((2 * C, D // 2), BF),
        gwo_in=vm((2 * inbox_rows(C, L), D // 2), BF),
        gwg=vm((D, C), BF),
        gwg_in=vm((2 * inbox_rows(D // 2, L), C), BF),
        gwv=vm((D, C), BF),
        gwv_in=vm((4 * inbox_rows(D // 4, L), C), BF),
        gws=vm((D, 2 * N), BF),
        gws_in=vm((inbox_rows(D, L + 2), 2 * N), BF),
        dfeat=vm((S, T, F), F32),
        ngain=vm((8, F), F32),
        pack=vm((24, D), F32),
        packin=vm((L, 24, D), F32),
        shin=vm((2, 8, D), F32),
        ngin=vm((L, 8, F), F32),
        ssem=dma((18,)),
        rsem=dma((18,)),
        lsem=dma((5,)),
        asend=dma((16 * L + 2 * (L + 2),)),
        arecv=dma((16 * L + 2 * (L + 2),)),
        afree=pltpu.SemaphoreType.REGULAR((16 * L + 2 * (L + 2),)),
        psend=dma((2 * L + 2,)),
        precv=dma((2 * L + 2,)),
    )
    for key in ("m10", "m11", "o20", "o21"):
        items[key] = vm((n, R + 16, N), BF)
    items["sb1"] = vm((S, 2, T, F), BF)
    items["sb2"] = vm((S, T, F), BF)
    for tag in ("f0", "f1", "b0", "b1"):
        for key in ("i1", "i2"):
            items[key + tag] = vm((n, R + 16, N), BF)
        for key in ("s1", "r1", "s2", "r2"):
            items[key + tag] = dma((n,))
    for tag in "od":
        items["rb1" + tag] = vm((S, 2, T, F), BF)
        items["rb2" + tag] = vm((S, T, F), BF)
        items["fsem" + tag] = dma((4, S))
    return items


def dims_names(dims):
    return INPUTS + OUTPUTS + list(scratch(dims))


def finish(dims, mixed, gtok, gwg, gwv, gws, left, right, small, ngain, *outs):
    n, S, T, D, C, H, N, F = dims
    PW = C // H
    outs[0][...] = mixed[...]
    outs[1][...] = gtok[...]
    outs[3][...] = gwg[...].astype(F32)
    outs[4][...] = gwv[...].astype(F32)
    outs[5][...] = gws[...].astype(F32)
    outs[15][:, 0 : D // 2] = left[...].astype(F32)
    outs[15][:, D // 2 : D] = right[...].astype(F32)

    @pl.when(pl.program_id(0) == 0)
    def _():
        outs[2][...] = ngain[0:1, :]
        outs[6][...] = small[8 : 8 + H, :]
        outs[7][...] = small[0:4, 0:C]
        outs[8][...] = small[4:5, 0:C]
        outs[9][...] = small[16:20, 0 : 2 * N]
        outs[10][...] = small[20:21, 0 : 2 * N]
        outs[11][...] = small[0:1, C : C + H]
        outs[12][...] = small[1:2, C : C + H]
        sums = [jnp.sum(small[6:7, h * PW : (h + 1) * PW], axis=1, keepdims=True) for h in range(H)]
        outs[13][...] = jnp.concatenate(sums, axis=1)
        outs[14][...] = small[5:6, 0:C]


def shards(*args):
    tokens, gate_weight, step_weight, shared_weight = args[0], args[2], args[5], args[4]
    cotangent = args[15]
    S, T, D = tokens.shape
    C, H, N, F = gate_weight.shape[1], step_weight.shape[1], shared_weight.shape[1] // 2, cotangent.shape[2]
    n = lax.axis_size("seq")
    dims = (n, S, T, D, C, H, N, F)
    args = [x.reshape(1, -1) if x.ndim == 1 else x for x in args]
    args[5] = step_weight.T
    items = scratch(dims)
    whole = pl.BlockSpec(memory_space=pltpu.VMEM)
    hbm = pl.BlockSpec(memory_space=pl.ANY)
    struct = jax.ShapeDtypeStruct
    mixed, gtok, gwg, gwv, gws, gwo, small, ngain = pl.pallas_call(
        lambda *refs: kernel(dims, *refs),
        out_shape=(
            struct((S, T, F), BF),
            struct((S, T, F), F32),
            struct((D, C), BF),
            struct((D, C), BF),
            struct((D, 2 * N), BF),
            struct((2 * C, D // 2), BF),
            struct((24, D), F32),
            struct((8, F), F32),
        ),
        in_specs=[whole] * len(args),
        out_specs=(whole, whole, hbm, hbm, hbm, hbm, whole, whole),
        scratch_shapes=list(items.values()),
        compiler_params=pltpu.CompilerParams(
            collective_id=0, has_side_effects=True, vmem_limit_bytes=63 * 2**20
        ),
        name="block",
    )(*args)
    outs = pl.pallas_call(
        lambda *refs: finish(dims, *refs),
        grid=(S,),
        out_shape=(
            struct((S, T, F), BF),
            struct((S, T, F), F32),
            struct((1, F), F32),
            struct((D, C), F32),
            struct((D, C), F32),
            struct((D, 2 * N), F32),
            struct((H, D), F32),
            struct((4, C), F32),
            struct((1, C), F32),
            struct((4, 2 * N), F32),
            struct((1, 2 * N), F32),
            struct((1, H), F32),
            struct((1, H), F32),
            struct((1, H), F32),
            struct((1, C), F32),
            struct((C, D), F32),
        ),
        in_specs=[
            pl.BlockSpec((1, T, F), lambda i: (i, 0, 0)),
            pl.BlockSpec((1, T, F), lambda i: (i, 0, 0)),
            pl.BlockSpec((D // S, C), lambda i: (i, 0)),
            pl.BlockSpec((D // S, C), lambda i: (i, 0)),
            pl.BlockSpec((D // S, 2 * N), lambda i: (i, 0)),
            pl.BlockSpec((C // S, D // 2), lambda i: (i, 0)),
            pl.BlockSpec((C // S, D // 2), lambda i: (i + S, 0)),
            pl.BlockSpec((24, D), lambda i: (0, 0)),
            pl.BlockSpec((8, F), lambda i: (0, 0)),
        ],
        out_specs=(
            pl.BlockSpec((1, T, F), lambda i: (i, 0, 0)),
            pl.BlockSpec((1, T, F), lambda i: (i, 0, 0)),
            pl.BlockSpec((1, F), lambda i: (0, 0)),
            pl.BlockSpec((D // S, C), lambda i: (i, 0)),
            pl.BlockSpec((D // S, C), lambda i: (i, 0)),
            pl.BlockSpec((D // S, 2 * N), lambda i: (i, 0)),
            pl.BlockSpec((H, D), lambda i: (0, 0)),
            pl.BlockSpec((4, C), lambda i: (0, 0)),
            pl.BlockSpec((1, C), lambda i: (0, 0)),
            pl.BlockSpec((4, 2 * N), lambda i: (0, 0)),
            pl.BlockSpec((1, 2 * N), lambda i: (0, 0)),
            pl.BlockSpec((1, H), lambda i: (0, 0)),
            pl.BlockSpec((1, H), lambda i: (0, 0)),
            pl.BlockSpec((1, H), lambda i: (0, 0)),
            pl.BlockSpec((1, C), lambda i: (0, 0)),
            pl.BlockSpec((C // S, D), lambda i: (i, 0)),
        ),
        name="finish",
    )(mixed, gtok, gwg, gwv, gws, gwo, gwo, small, ngain)
    outs = list(outs)
    outs[6] = outs[6].T
    for i in (2, 8, 10, 11, 12, 13, 14):
        outs[i] = outs[i].reshape(-1)
    return tuple(outs)


def solution(mesh):
    head = P("head")
    return jax.shard_map(
        shards,
        mesh=mesh,
        in_specs=(
            P(None, "seq", None),
            P(),
            P(None, "head"),
            P(None, "head"),
            P(),
            P(None, "head"),
            P(None, "head"),
            head,
            P(),
            P(),
            head,
            head,
            head,
            head,
            P("head", None),
            P(None, "seq", "head"),
        ),
        out_specs=(
            P(None, "seq", "head"),
            P(None, "seq", "head"),
            head,
            P(None, "head"),
            P(None, "head"),
            P(),
            P(None, "head"),
            P(None, "head"),
            head,
            P(),
            P(),
            head,
            head,
            head,
            head,
            P("head", None),
        ),
        check_vma=False,
    )
```

```python
import jax
import jax.numpy as jnp
from jax import lax
from jax.experimental import pallas as pl
from jax.experimental.pallas import tpu as pltpu
from jax.sharding import PartitionSpec as P

EPSILON = 1e-05
F32 = jnp.float32
BF = jnp.bfloat16
MESH = pl.DeviceIdType.MESH
LANES = 128


def mm(a, b):
    return lax.dot_general(a, b, (((1,), (0,)), ((), ())), preferred_element_type=F32)


def nt(a, b):
    return lax.dot_general(a, b, (((1,), (1,)), ((), ())), preferred_element_type=F32)


def tn(a, b):
    return lax.dot_general(a, b, (((0,), (0,)), ((), ())), preferred_element_type=F32)


def split(x):
    high = x.astype(BF)
    return high, (x - high.astype(F32)).astype(BF)


def mm_exact_left(a, x):
    high, rest = x.astype(BF), x - x.astype(BF).astype(F32)
    mid, low = split(rest)
    return mm(a, high) + (mm(a, mid) + mm(a, low))


def sigmoid(x):
    return 0.5 * jnp.tanh(0.5 * x) + 0.5


def softplus(x):
    return jnp.maximum(x, 0.0) + jnp.log1p(jnp.exp(-jnp.abs(x)))


def loop(count, body):
    def step(i, carry):
        body(i)
        return carry

    lax.fori_loop(0, count, step, 0)


def can_halve(size):
    return size % 32 == 0


ORDERS = {"O0": 0, "O1": 0, "G0": 0, "G1": 1, "V0": 0, "V1": 0, "V2": 0, "V3": 0}
PLAN = {
    "wa1": ("O0",),
    "wb0": ("O1", "G1", "O0", "G0",),
    "s1": ("O1",),
    "s2": ("G1",),
    "s3": ("O0",),
    "c0": ("G1", "G0",),
    "c1": ("O1",),
    "we": ("O0",),
    "v": ("G1", "P", "G0",),
    "v1": ("O1", "V3", "O0",),
    "d0": ("V0", "P", "G1", "V3", "V1",),
    "d1": ("G0", "O1",),
    "d2": ("V0",),
    "d3": ("P", "O0",),
    "e2": ("P", "V2",),
    "o0": ("P", "G1",),
    "o1": ("V1", "V3",),
    "f0": ("G0", "V0",),
    "f1": ("V2", "V1", "O1",),
    "f2": ("V3", "V0", "V2",),
    "f3": ("V1",),
    "n1": ("G0", "V3", "V0",),
    "n2": ("V2",),
    "n3": ("V1", "N",),
    "wst": ("V3", "V2", "V0", "V1", "V3", "V2",),
    "x2": ("V3",),
    "end": ("V3", "V3",),
}


class Reduced:
    def __init__(self, buf, base, rows, inbox, inbase, levels, sems, first):
        self.buf, self.inbox, self.levels = buf, inbox, levels
        self.send, self.recv, self.free = sems
        self.first = first
        self.lo, self.size, self.stack, self.offset = base, rows, [], inbase
        self.copies = {}

    def copy(self, src, dst, slot, partner):
        return pltpu.make_async_remote_copy(
            src_ref=src,
            dst_ref=dst,
            send_sem=self.send.at[slot],
            recv_sem=self.recv.at[slot],
            device_id=partner,
            device_id_type=MESH,
        )

    def start(self, level):
        partner, bit = self.levels[level]
        halved = can_halve(self.size)
        part = self.size // 2 if halved else self.size
        theirs = self.lo + (1 - bit) * part if halved else self.lo
        mine = self.lo + bit * part if halved else self.lo
        copy = self.copy(
            self.buf.at[pl.ds(pl.multiple_of(theirs, 16), part), :],
            self.inbox.at[pl.ds(self.offset, part), :],
            self.first + level,
            partner,
        )
        copy.start()
        self.copies[level] = (copy, mine, part, self.offset, halved)
        self.offset += part

    def finish(self, level):
        copy, mine, part, offset, halved = self.copies[level]
        copy.wait()
        if halved:
            pl.semaphore_signal(
                self.free.at[self.first + level],
                inc=1,
                device_id=self.levels[level][0],
                device_id_type=MESH,
            )
        block = 64 if part % 64 == 0 else part

        def add(i):
            rows = pl.ds(pl.multiple_of(mine + i * block, 16), block)
            got = self.inbox[pl.ds(pl.multiple_of(offset + i * block, 16), block), :]
            self.buf[rows, :] = (self.buf[rows, :].astype(F32) + got.astype(F32)).astype(BF)

        loop(part // block, add)
        self.stack.append((self.lo, self.size, halved))
        self.lo, self.size = mine, part

    def spread_start(self, level):
        slot = self.first + len(self.levels) + level
        rows = pl.ds(pl.multiple_of(self.lo, 16), self.size)
        pl.semaphore_wait(self.free.at[self.first + level], 1)
        self.copies[level] = self.copy(self.buf.at[rows, :], self.buf.at[rows, :], slot, self.levels[level][0])
        self.copies[level].start()

    def halves(self):
        for level in range(len(self.levels)):
            self.start(level)
            yield
            self.finish(level)

    def spread(self):
        for level in range(len(self.levels) - 1, -1, -1):
            lo, size, halved = self.stack[level]
            if halved:
                self.spread_start(level)
                yield
                self.copies[level].wait()
            self.lo, self.size = lo, size

    def steps(self):
        yield from self.halves()
        yield from self.spread()


def kernel(dims, *refs):
    n, S, T, D, C, H, N, F = dims
    PW = C // H
    Sh = S // 2
    R = Sh * C // n
    q = n // Sh
    groups = max(1, R // PW)
    span = R // groups
    names = dims_names(dims)
    ref = dict(zip(names, refs))

    class A:
        pass

    a = A()
    a.__dict__.update(ref)
    me = lax.axis_index("seq")
    head = lax.axis_index("head")
    flip = lambda value, bit: value + bit - 2 * bit * lax.rem(value // bit, 2)
    core_peer = (me, flip(head, 1))
    x_peer = (me, flip(head, 2))
    diag = (me, flip(flip(head, 1), 2))
    barrier = pltpu.get_barrier_semaphore()
    for peer in (core_peer, x_peer, diag):
        pl.semaphore_signal(barrier, inc=1, device_id=peer, device_id_type=MESH)

    def greet(i):
        peer = (lax.rem(me + i + 1, n), head)
        pl.semaphore_signal(barrier, inc=1, device_id=peer, device_id_type=MESH)

    loop(n - 1, greet)

    lane = lax.broadcasted_iota(jnp.int32, (T, LANES), 1)
    first_half = lane < PW

    rows_i = lax.broadcasted_iota(jnp.int32, (T, T), 0)
    cols_i = lax.broadcasted_iota(jnp.int32, (T, T), 1)
    a.tri[...] = jnp.where(rows_i >= cols_i, 1.0, 0.0).astype(BF)
    a.triT[...] = jnp.where(rows_i <= cols_i, 1.0, 0.0).astype(BF)
    er = lax.broadcasted_iota(jnp.int32, (2 * LANES, C), 0)
    ec_ = lax.broadcasted_iota(jnp.int32, (2 * LANES, C), 1)
    a.E2[...] = jnp.where(lax.rem(er, LANES) == ec_ // PW, 1.0, 0.0).astype(BF)
    tr = lax.broadcasted_iota(jnp.int32, (C, LANES), 0)
    tc = lax.broadcasted_iota(jnp.int32, (C, LANES), 1)
    a.ET[...] = jnp.where(tr // PW == tc, 1.0, 0.0).astype(BF)
    a.stT[...] = jnp.zeros(a.stT.shape, BF)
    a.stT[0:H, :] = a.step_weight[...]
    a.small[...] = jnp.zeros(a.small.shape, F32)
    a.heads_sm[...] = jnp.zeros(a.heads_sm.shape, F32)
    a.shsm[...] = jnp.zeros(a.shsm.shape, F32)
    a.hrow[...] = jnp.zeros(a.hrow.shape, F32)
    a.hrow[0:1, 0:H] = a.step_bias[...]
    a.hrow[1:2, 0:H] = a.decay_rate[...]
    a.hrow[2:3, 0:H] = a.skip_weight[...]
    bias_row = a.hrow[0:1, :]
    rate_row = a.hrow[1:2, :]

    def expand(x):
        high, low = split(x)
        return mm(jnp.concatenate([high, low], axis=1), a.E2[...])

    a.skipE[...] = expand(jnp.broadcast_to(a.hrow[2:3, :], (8, LANES)))
    skip_row = a.skipE[0:1, :]
    gain = a.norm_gain[...]

    def norm_rows(x):
        scale = lax.rsqrt(jnp.mean(x * x, axis=-1, keepdims=True) + EPSILON)
        return (x * scale * gain).astype(BF), scale

    def norm_block(b):
        s, r = b // 4, pl.multiple_of(lax.rem(b, 4) * (T // 4), T // 4)
        rows = pl.ds(r, T // 4)
        x = a.tokens[s, rows, :].astype(F32)
        low, scale = norm_rows(x)
        a.normed[s, rows, :] = low
        a.raw[s, rows, :] = jnp.broadcast_to(scale, (T // 4, LANES))

    pl.semaphore_wait(barrier, n - 1 + 3)

    def halo_copy():
        return pltpu.make_async_remote_copy(
            src_ref=a.tokens.at[:, pl.ds(T - 16, 16), :],
            dst_ref=a.halo,
            send_sem=a.ssem.at[0],
            recv_sem=a.rsem.at[0],
            device_id=(lax.rem(me + 1, n), head),
            device_id_type=MESH,
        )

    @pl.when(me < n - 1)
    def _():
        halo_copy().start()

    def cot_copy(src, slot, sem, peer):
        return pltpu.make_async_remote_copy(
            src_ref=src,
            dst_ref=a.cotf.at[slot],
            send_sem=a.ssem.at[sem],
            recv_sem=a.rsem.at[sem],
            device_id=peer,
            device_id_type=MESH,
        )

    cot_x = cot_copy(a.cotangent, head, 1, x_peer)
    cot_x.start()
    cot_c = cot_copy(a.cotangent, head, 2, core_peer)
    cot_c.start()
    cot_own = pltpu.make_async_copy(a.cotangent, a.cotf.at[head], a.lsem.at[0])
    cot_own.start()

    def half(which, f):
        loop(Sh, lambda i: f(which * Sh + i))

    loop(4 * Sh, norm_block)

    def project_b(s):
        x = a.normed[s]
        a.vext[s, 8 : 8 + T, :] = mm(x, a.value_weight[...])
        a.sext[s, 8 : 8 + T, :] = mm(x, a.shared_weight[...])
        a.raw[s] = jnp.where(lane == H, a.raw[s], nt(x, a.stT[...]) + bias_row)

    half(0, project_b)

    @pl.when(me > 0)
    def _():
        halo_copy().wait_recv()

    @pl.when(me == 0)
    def _():
        a.halo[...] = jnp.zeros(a.halo.shape, BF)

    @pl.when(me < n - 1)
    def _():
        halo_copy().wait_send()

    hx = jnp.concatenate([a.halo[s] for s in range(S)], axis=0).astype(F32)
    hlow, _ = norm_rows(hx)
    vh = mm(hlow, a.value_weight[...])
    sh = mm(hlow, a.shared_weight[...])
    for s in range(S):
        a.vext[s, 0:8, :] = vh[s * 16 + 8 : s * 16 + 16, :]
        a.sext[s, 0:8, :] = sh[s * 16 + 8 : s * 16 + 16, :]

    def conv(ext, w, b, s, c):
        running = b[0:1, c : c + LANES] + jnp.zeros((T, LANES), F32)
        for k in range(4):
            running = running + w[k : k + 1, c : c + LANES] * ext[s, pl.ds(5 + k, T), c : c + LANES]
        sig = sigmoid(running)
        return running * sig, sig * (1.0 + running * (1.0 - sig))

    def states(tag, reverse):
        m1, o2 = a.__dict__["m1" + tag[1]], a.__dict__["o2" + tag[1]]
        i1, i2 = (a.__dict__[k + tag] for k in ("i1", "i2"))
        s1, r1, s2, r2 = (a.__dict__[k + tag] for k in ("s1", "r1", "s2", "r2"))

        def first(k):
            return pltpu.make_async_remote_copy(
                src_ref=m1.at[k],
                dst_ref=i1.at[me],
                send_sem=s1.at[k],
                recv_sem=r1.at[me],
                device_id=(k, head),
                device_id_type=MESH,
            )

        def first_wait(k):
            return pltpu.make_async_remote_copy(
                src_ref=m1.at[k],
                dst_ref=i1.at[k],
                send_sem=s1.at[k],
                recv_sem=r1.at[k],
                device_id=(k, head),
                device_id_type=MESH,
            )

        def second(k):
            return pltpu.make_async_remote_copy(
                src_ref=o2.at[k, pl.ds(0, back_rows)],
                dst_ref=i2.at[me, pl.ds(0, back_rows)],
                send_sem=s2.at[k],
                recv_sem=r2.at[me],
                device_id=(k, head),
                device_id_type=MESH,
            )

        def second_wait(k):
            return pltpu.make_async_remote_copy(
                src_ref=o2.at[k, pl.ds(0, back_rows)],
                dst_ref=i2.at[k, pl.ds(0, back_rows)],
                send_sem=s2.at[k],
                recv_sem=r2.at[k],
                device_id=(k, head),
                device_id_type=MESH,
            )

        none = n - 1 if reverse else 0
        back_rows = R if reverse else R + 16

        def pack(i, state, decay):
            high, low = split(decay)
            hf, lf = high.astype(F32), low.astype(F32)
            for j in range(q):
                h0 = j * R // PW
                k = i * q + j
                m1[k, 0:R, :] = state[j * R : (j + 1) * R, :].astype(BF)
                both = [hf[h0:], hf[:h0], lf[h0:], lf[:h0]] if h0 else [hf, lf]
                m1[k, R : R + 16, :] = jnp.concatenate(both, axis=0).astype(BF)

                @pl.when(k != me)
                def _():
                    first(k).start()

                @pl.when(k == me)
                def _():
                    i1[k] = m1[k]

        group_row = lax.broadcasted_iota(jnp.int32, (8, LANES), 0)
        group_lane = lax.broadcasted_iota(jnp.int32, (8, LANES), 1) // span

        def join():
            def wait(k):
                @pl.when(k != me)
                def _():
                    first_wait(k).wait()

            loop(n, wait)

            def one(step):
                j = n - 1 - step if reverse else step
                tail = i1[j, R : R + 16, :].astype(F32)
                decay = tail[0:8] + tail[8:16]
                now = a.joined[step % 2 if isinstance(step, int) else lax.rem(step, 2)]
                if reverse:
                    o2[j, 0:R, :] = now[0:R].astype(BF)
                else:
                    means = [jnp.mean(now[g * span : (g + 1) * span], axis=0, keepdims=True) for g in range(groups)]
                    means = jnp.concatenate(means + [jnp.zeros((8 - groups, LANES), F32)], axis=0)
                    size = jnp.sum(means * means, axis=1, keepdims=True) + 1e-30
                    along = nt(means.astype(BF), now.astype(BF)) / size
                    along = jnp.where(group_row == group_lane, along, 0.0)
                    ah, mh = along.astype(BF).astype(F32), means.astype(BF).astype(F32)
                    al, ml = (along - ah).astype(BF).astype(F32), (means - mh).astype(BF).astype(F32)
                    left, right = [], []
                    for g in range(groups):
                        row = slice(g, g + 1)
                        left += [ah[row], ah[row], al[row]]
                        right += [mh[row], ml[row], mh[row]]
                    rest = [jnp.zeros((8 - 3 * groups, LANES), F32)]
                    left, right = jnp.concatenate(left + rest, axis=0), jnp.concatenate(right + rest, axis=0)
                    o2[j, 0:R, :] = (now - tn(left, right))[0:R].astype(BF)
                    o2[j, R : R + 16, :] = jnp.concatenate([left, right], axis=0).astype(BF)
                after = [
                    decay[g : g + 1, :] * now[g * span : (g + 1) * span]
                    + i1[j, g * span : (g + 1) * span, :].astype(F32)
                    for g in range(groups)
                ]
                if R < LANES:
                    after.append(jnp.zeros((LANES - R, N), F32))
                a.joined[(step + 1) % 2 if isinstance(step, int) else lax.rem(step + 1, 2)] = jnp.concatenate(after, axis=0)

                @pl.when((j != me) & (j != none))
                def _():
                    second(j).start()

                @pl.when((j == me) & (j != none))
                def _():
                    i2[j, 0:back_rows, :] = o2[j, 0:back_rows, :]

            a.joined[0] = jnp.zeros((LANES, N), F32)
            if n <= 8:
                for step in range(n):
                    one(step)
            else:
                loop(n, one)

        def collect(out, base):
            def wait(k):
                @pl.when((k != me) & (me != none))
                def _():
                    second_wait(k).wait_recv()

                @pl.when((k != me) & (k != none))
                def _():
                    second_wait(k).wait_send()

            loop(n, wait)

            @pl.when(me != none)
            def _():
                def one(k):
                    got = i2[k, 0:R, :].astype(F32)
                    if not reverse:
                        tail = i2[k, R : R + 16, :].astype(F32)
                        got = got + tn(tail[0:8], tail[8:16])[0:R]
                    out[pl.ds(pl.multiple_of(base + k * R, 16), R), :] = got

                if n <= 8:
                    for k in range(n):
                        one(k)
                else:
                    loop(n, one)

            @pl.when(me == none)
            def _():
                out[base : base + Sh * C, :] = jnp.zeros((Sh * C, N), F32)

        return pack, join, collect

    forward = [states("f" + x, False) for x in "01"]
    backward = [states("b" + x, True) for x in "01"]

    def scan_inputs(s, i, pack):
        for c in range(0, C, LANES):
            v, d = conv(a.vext, a.conv_value, a.conv_value_bias, s, c)
            a.V[s, :, c : c + LANES] = v.astype(BF)
            a.dsv[s, :, c : c + LANES] = d.astype(BF)
        for c in range(0, 2 * N, LANES):
            v, d = conv(a.sext, a.conv_shared, a.conv_shared_bias, s, c)
            a.KR[s, :, c : c + LANES] = v.astype(BF)
            a.dss[s, :, c : c + LANES] = d.astype(BF)
        raw = a.raw[s]
        steps = softplus(raw)
        cum = mm_exact_left(a.tri[...], -steps * rate_row)
        a.cum[s] = cum
        cumT = cum.T[0:8]
        a.cumT[s] = cumT
        last = cum[T - 1 : T, :]
        tail = jnp.exp(last - cum)
        V = a.V[s].astype(F32)
        a.U[s] = (expand(steps) * V).astype(BF)
        tU = (expand(steps * tail) * V).astype(BF)
        a.tU[s] = tU
        state = tn(tU, a.KR[s, :, 0:N])
        a.sp[pl.ds(pl.multiple_of(s * C, C), C), :] = state
        decay = jnp.broadcast_to(jnp.exp(cumT[:, T - 1 : T]), (8, LANES))
        a.decay[s] = decay
        pack(i, state, decay)

    def scan_half(which):
        loop(Sh, lambda i: scan_inputs(which * Sh + i, i, forward[which][0]))

    scan_half(0)
    loop(4 * Sh, lambda b: norm_block(4 * Sh + b))
    half(1, project_b)
    scan_half(1)

    def project_gate(s):
        a.gate[s] = mm(a.normed[s], a.gate_weight[...])

    def intra_forward(s):
        K, Rm = a.KR[s, :, 0:N], a.KR[s, :, N : 2 * N]
        G = jnp.where(rows_i >= cols_i, nt(Rm, K), 0.0)
        for p in range(H // 2):
            pair = slice(p * LANES, (p + 1) * LANES)
            U2 = a.U[s, :, pair]
            z = []
            for h in (2 * p, 2 * p + 1):
                gap = a.cum[s, :, h : h + 1] - a.cumT[s, h : h + 1, :]
                M = (jnp.exp(jnp.minimum(gap, 0.0)) * G).astype(BF)
                z.append(mm(M, U2))
            a.Y[s, :, pair] = jnp.where(first_half, z[0], z[1])

    loop(S, project_gate)
    half(0, intra_forward)
    forward[0][1]()
    half(1, intra_forward)

    cot_x.wait()
    cot_f = cot_copy(a.cotf.at[flip(head, 2)], flip(head, 2), 3, core_peer)
    cot_f.start()
    cot_c.wait()
    cot_f.wait()
    cot_own.wait()

    def back_out(s):
        total = nt(a.cotf[0, s], a.output_weight[:, 0:F])
        for f in range(1, D // F):
            total = total + nt(a.cotf[f, s], a.output_weight[:, f * F : (f + 1) * F])
        a.dext[s, 0:T, :] = total

    loop(S, back_out)
    forward[1][1]()

    def transposed(s):
        rows = pl.ds(pl.multiple_of(s * T, T), T)
        for c in range(0, D, 256):
            a.normT[c : c + 256, rows] = a.normed[s, :, c : c + 256].T

    loop(S, transposed)

    def outputs(s, i, stat):
        rows = pl.ds(pl.multiple_of(s * C, C), C)
        high, low = split(a.Sin[rows, :])
        Rm = a.KR[s, :, N : 2 * N]
        reach = expand(jnp.exp(a.cum[s]))
        outer = reach * (nt(Rm, high) + nt(Rm, low))
        Y = a.Y[s] + outer + skip_row * a.V[s].astype(F32)
        a.Y[s] = Y
        g = a.gate[s]
        gated = Y * (g * sigmoid(g))
        dots = a.dext[s, 0:T, :] * a.out_gain[...] * gated
        ones = jnp.ones((8, C), BF)
        sq = nt(ones, (gated * gated).astype(BF))
        dt = nt(ones, dots.astype(BF))
        row8 = lax.broadcasted_iota(jnp.int32, (8, T), 0)
        part = jnp.where(row8 == 2 * i, sq, 0.0) + jnp.where(row8 == 2 * i + 1, dt, 0.0)
        stat[...] = part + jnp.where(row8 < 2 * i, stat[...], 0.0)

    def head_sums(stat, inbox, first):
        return [
            pltpu.make_async_remote_copy(
                src_ref=stat,
                dst_ref=inbox.at[i],
                send_sem=a.ssem.at[first + i],
                recv_sem=a.rsem.at[first + i],
                device_id=peer,
                device_id_type=MESH,
            )
            for i, peer in enumerate((x_peer, diag, core_peer))
        ]

    stats = [head_sums(a.stat.at[w], a.stin.at[w], 9 + 3 * w) for w in range(2)]
    inner = C * lax.axis_size("head")

    def output_half(w):
        a.stat[w] = jnp.zeros((8, T), F32)
        loop(Sh, lambda i: outputs(w * Sh + i, i, a.stat.at[w]))
        for copy in stats[w]:
            copy.start()

    def stat_half(w):
        for copy in stats[w]:
            copy.wait()
        total = a.stat[w] + (a.stin[w, 0] + a.stin[w, 1]) + a.stin[w, 2]
        columns = []
        for i in range(Sh):
            scale = lax.rsqrt(total[2 * i : 2 * i + 1] / inner + EPSILON)
            columns += [scale, total[2 * i + 1 : 2 * i + 2] * scale / inner]
        stacked = jnp.concatenate(columns + [jnp.zeros((LANES - 2 * Sh, T), F32)], axis=0).T
        a.gcols[...] = stacked

    def gate_back(s, i, pack):
        reach = expand(jnp.exp(a.cum[s]))
        scale = jnp.broadcast_to(a.gcols[:, 2 * i : 2 * i + 1], (T, LANES))
        mean = jnp.broadcast_to(a.gcols[:, 2 * i + 1 : 2 * i + 2], (T, LANES))
        cols = pl.ds(pl.multiple_of(s * T, T), T)
        for c in range(0, C, LANES):
            ch = slice(c, c + LANES)
            g, Y = a.gate[s, :, ch], a.Y[s, :, ch]
            sig = sigmoid(g)
            act = g * sig
            gu = Y * act * scale
            og = a.out_gain[0:1, ch]
            ny = gu * og
            a.ny[s, :, ch] = ny.astype(BF)
            a.nyT[ch, cols] = ny.T.astype(BF)
            dn = a.dext[s, 0:T, ch]
            a.small[5:6, ch] += jnp.sum(dn * gu, axis=0, keepdims=True)
            dg = scale * (dn * og - gu * mean)
            dY = (dg * act).astype(BF)
            a.dY[s, :, ch] = dY
            a.ecdY[s, :, ch] = (reach[:, ch] * dY.astype(F32)).astype(BF)
            a.normed[s, :, ch] = (dg * Y * sig * (1.0 + g * (1.0 - sig))).astype(BF)
        state = tn(a.ecdY[s], a.KR[s, :, N : 2 * N])
        pack(i, state, a.decay[s])

    for w in range(2):
        forward[w][2](a.Sin, w * Sh * C)
        output_half(w)
    for w in range(2):
        stat_half(w)
        for i in range(Sh):
            gate_back(w * Sh + i, i, backward[w][0])

    levels = []
    bit = 1
    while bit < n:
        levels.append(((flip(me, bit), head), lax.rem(me // bit, 2)))
        bit *= 2
    L = len(levels)
    sems = (a.asend, a.arecv, a.afree)
    head_levels = [(core_peer, lax.rem(head, 2)), (x_peer, lax.rem(head // 2, 2))]
    later = levels[1:] + levels[:1]
    tasks = {}
    used = inbase = 0
    VR = D // 4
    SR = D // 4 // 2
    for name, buf, inbox, base, rows, order in (
        ("O0", a.gwo, a.gwo_in, 0, C, ORDERS["O0"]),
        ("O1", a.gwo, a.gwo_in, C, C, ORDERS["O1"]),
        ("G0", a.gwg, a.gwg_in, 0, D // 2, ORDERS["G0"]),
        ("G1", a.gwg, a.gwg_in, D // 2, D // 2, ORDERS["G1"]),
        ("V0", a.gwv, a.gwv_in, 0, VR, ORDERS["V0"]),
        ("V1", a.gwv, a.gwv_in, VR, VR, ORDERS["V1"]),
        ("V2", a.gwv, a.gwv_in, 2 * VR, VR, ORDERS["V2"]),
        ("W", a.gwv, a.gwv_in, 3 * VR, VR + SR, ORDERS["V3"]),
        ("H", a.gws, a.gws_in, 0, D, None),
    ):
        order = head_levels if order is None else (later if order else levels)
        inbase = 0 if name in ("O0", "G0", "V0", "H") else inbase
        tasks[name] = Reduced(buf, base, rows, inbox, inbase, order, sems, used)
        inbase += inbox_rows(rows, len(order))
        used += 2 * len(order)

    def last_chunk(over_heads, own):
        shared = over_heads.halves()
        yield from shared
        mine = pl.multiple_of(over_heads.lo, 16)
        for i in range(2):
            half = pl.ds(pl.multiple_of(mine + i * SR, 16), SR)
            a.gwv[D : D + SR, i * 2 * N : (i + 1) * 2 * N] = a.gws[half, :]
        yield from own.steps()
        for i in range(2):
            half = pl.ds(pl.multiple_of(mine + i * SR, 16), SR)
            a.gws[half, :] = a.gwv[D : D + SR, i * 2 * N : (i + 1) * 2 * N]
        yield from over_heads.spread()

    tasks["V3"] = last_chunk(tasks.pop("H"), tasks.pop("W"))
    for name in tasks:
        if name != "V3":
            tasks[name] = tasks[name].steps()

    def pump(*names):
        for name in names:
            next(tasks[name], None)

    def at(point):
        pump(*PLAN.get(point, ()))

    def feature_sum(tag, block):
        sb1, sb2 = a.sb1, a.sb2
        rb1, rb2 = (a.__dict__[k + tag] for k in ("rb1", "rb2"))
        sem = a.__dict__["fsem" + tag]

        def copy1(s):
            return pltpu.make_async_remote_copy(
                src_ref=sb1.at[s],
                dst_ref=rb1.at[s],
                send_sem=sem.at[0, s],
                recv_sem=sem.at[1, s],
                device_id=core_peer,
                device_id_type=MESH,
            )

        def copy2(s):
            return pltpu.make_async_remote_copy(
                src_ref=sb2.at[s],
                dst_ref=rb2.at[s],
                send_sem=sem.at[2, s],
                recv_sem=sem.at[3, s],
                device_id=x_peer,
                device_id_type=MESH,
            )

        def one(s):
            sb1[s, 0] = block(s, flip(head, 1)).astype(BF)
            sb1[s, 1] = block(s, flip(flip(head, 1), 2)).astype(BF)
            copy1(s).start()

        def two(s):
            far = block(s, flip(head, 2))
            copy1(s).wait()
            sb2[s] = (far + rb1[s, 1].astype(F32)).astype(BF)
            copy2(s).start()

        def three(s):
            near = block(s, head)
            copy2(s).wait()
            return near + rb1[s, 0].astype(F32) + rb2[s].astype(F32)

        return one, two, three

    def features(f):
        return pl.ds(pl.multiple_of(f * F, F), F)

    o_one, o_two, o_three = feature_sum("o", lambda s, f: mm(a.ny[s], a.output_weight[:, features(f)]))

    def grad_out_weight(half_index):
        for g in range(D // F // 2):
            f = half_index * (D // F // 2) + g
            x = mm(a.nyT[...], a.cotf[f].reshape(S * T, F))
            a.gwo[half_index * C : (half_index + 1) * C, g * F : (g + 1) * F] = x.astype(BF)

    def weight_grad(out, r, rows, columns):
        out[r : r + rows, :] = mm(a.normT[r : r + rows, :], columns()).astype(BF)

    def intra_backward(s):
        K, Rm = a.KR[s, :, 0:N], a.KR[s, :, N : 2 * N]
        GT = jnp.where(rows_i <= cols_i, nt(K, Rm), 0.0)
        dGT = jnp.zeros((T, T), F32)
        for p in range(H // 2):
            pair = slice(p * LANES, (p + 1) * LANES)
            dY2, U2 = a.dY[s, :, pair], a.U[s, :, pair]
            z = []
            for h in (2 * p, 2 * p + 1):
                gap = a.cumT[s, h : h + 1, :] - a.cum[s, :, h : h + 1]
                LT = jnp.exp(jnp.minimum(gap, 0.0))
                mine = first_half if h == 2 * p else jnp.logical_not(first_half)
                Um = jnp.where(mine, U2.astype(F32), 0.0).astype(BF)
                dGT = dGT + nt(Um, dY2) * LT
                z.append(mm((LT * GT).astype(BF), dY2))
            a.dext[s, 0:T, pair] = jnp.where(first_half, z[0], z[1])
        a.dGT[s] = jnp.where(rows_i <= cols_i, dGT, 0.0).astype(BF)

    def out_rows(s):
        total = o_three(s)
        own = a.tokens[s, :, features(head)].astype(F32)
        a.mixed[s] = (own + total).astype(BF)

    def state_back(s):
        rows = pl.ds(pl.multiple_of(s * C, C), C)
        K, Rm = a.KR[s, :, 0:N], a.KR[s, :, N : 2 * N]
        gout, Sin = a.gout[rows, :], a.Sin[rows, :]
        gob = gout.astype(BF)
        cum, steps = a.cum[s], softplus(a.raw[s])
        tail = expand(jnp.exp(cum[T - 1 : T, :] - cum))
        V = a.V[s].astype(F32)
        dY = a.dY[s].astype(F32)
        dU = a.dext[s, 0:T, :] + tail * nt(K, gob)
        skipV = skip_row * V
        dV = expand(steps) * dU + skip_row * dY
        a.small[6:7, :] += jnp.sum(dY * V, axis=0, keepdims=True)
        ph, plo = split(dU * V)
        dsd = mm(ph, a.ET[...]) + mm(plo, a.ET[...])
        ph, plo = split(dY * (a.Y[s] - skipV))
        row = mm(ph, a.ET[...]) + mm(plo, a.ET[...])
        dcv = dV * a.dsv[s].astype(F32)
        a.dext[s, 0:T, :] = dcv
        dGT = a.dGT[s]
        sh, sl = split(Sin)
        dK = mm(dGT, Rm) + mm(a.tU[s], gob)
        dR = tn(dGT, K) + (mm(a.ecdY[s], sh) + mm(a.ecdY[s], sl))
        a.dsext[s, 0:T, 0:N] = dK * a.dss[s, :, 0:N].astype(F32)
        a.dsext[s, 0:T, N : 2 * N] = dR * a.dss[s, :, N : 2 * N].astype(F32)
        decay = a.decay[s]
        sums = []
        for h in range(H):
            hs = slice(h * PW, (h + 1) * PW)
            sp = a.sp[pl.ds(pl.multiple_of(s * C + h * PW, PW), PW), :]
            sums.append(jnp.sum(gout[hs] * (decay[h : h + 1] * Sin[hs] + sp), axis=0, keepdims=True))
        sums = jnp.concatenate(sums + [jnp.zeros((LANES - H, LANES), F32)], axis=0)
        ones = jnp.ones((8, LANES), BF)
        lh, ll = split(sums)
        end = (nt(ones, lh) + nt(ones, ll))[0:1]
        dld = mm_exact_left(a.triT[...], row - steps * dsd) + end
        draw = (dsd - rate_row * dld) * sigmoid(a.raw[s])
        a.heads_sm[0:1, :] += jnp.sum(draw, axis=0, keepdims=True)
        a.heads_sm[1:2, :] -= jnp.sum(steps * dld, axis=0, keepdims=True)
        a.dst[s] = draw.astype(BF)
        a.dstT[:, pl.ds(pl.multiple_of(s * T, T), T)] = draw.T[0:16].astype(BF)

    def gate_grad(r):
        weight_grad(a.gwg, r * D // 2, D // 2, lambda: a.normed[:, :, 0:C].reshape(S * T, C))

    grad_out_weight(0)
    pump("O0")
    grad_out_weight(1)
    pump("O1")
    at("g")
    gate_grad(0)
    pump("G0")
    at("g0")
    intra_backward(0)
    at("i0")
    at("wa0")
    backward[0][1]()
    at("p1")
    gate_grad(1)
    pump("G1")
    at("g1")
    intra_backward(1)
    at("i1")
    at("wa1")
    backward[1][1]()
    at("p4")
    intra_backward(2)
    at("i2")
    intra_backward(3)
    at("i3")
    at("wb0")
    backward[0][2](a.gout, 0)
    for s in range(Sh):
        state_back(s)
        at("s" + str(s))
    at("wb1")
    backward[1][2](a.gout, Sh * C)
    for s in range(Sh, S):
        state_back(s)
        at("s" + str(s))
    a.stepsum[...] = nt(a.dstT[...], a.normT[...])[0:8]

    def edge_copy(src, dst, sem):
        return pltpu.make_async_remote_copy(
            src_ref=src.at[:, pl.ds(0, 8), :],
            dst_ref=dst,
            send_sem=a.ssem.at[sem],
            recv_sem=a.rsem.at[sem],
            device_id=(lax.rem(me + n - 1, n), head),
            device_id_type=MESH,
        )

    edges = [edge_copy(a.dext, a.ev, 7), edge_copy(a.dsext, a.es, 8)]

    @pl.when(me > 0)
    def _():
        for copy in edges:
            copy.start()


    def conv_grads(s):
        for ext, grad, out, base, width in (
            (a.vext, a.dext, a.small, 0, C),
            (a.sext, a.dsext, a.shsm, 0, 2 * N),
        ):
            for c in range(0, width, LANES):
                ch = slice(c, c + LANES)
                d = grad[s, 0:T, ch]
                for k in range(4):
                    x = ext[s, pl.ds(5 + k, T), ch]
                    out[base + k : base + k + 1, ch] += jnp.sum(d * x, axis=0, keepdims=True)
                out[base + 4 : base + 5, ch] += jnp.sum(d, axis=0, keepdims=True)

    half(0, conv_grads)
    at("c0")
    half(1, conv_grads)
    at("c1")
    a.pack[...] = jnp.zeros(a.pack.shape, F32)
    a.pack[0:7, 0:C] = a.small[0:7, :]
    a.pack[0:2, C : C + LANES] = a.heads_sm[0:2, :]
    a.pack[8:16, :] = a.stepsum[...]
    a.pack[16:21, 0 : 2 * N] = a.shsm[0:5, :]

    def whole_sum(buf, inbox, partners, first):
        for i, partner in enumerate(partners):
            copy = pltpu.make_async_remote_copy(
                src_ref=buf,
                dst_ref=inbox.at[i],
                send_sem=a.psend.at[first + i],
                recv_sem=a.precv.at[first + i],
                device_id=partner,
                device_id_type=MESH,
            )
            copy.start()
            yield
            copy.wait()
            buf[...] = buf[...] + inbox[i]

    def small_sums():
        partners = [partner for partner, _ in levels]
        yield from whole_sum(a.pack, a.packin, partners, 0)
        yield from whole_sum(a.pack.at[pl.ds(16, 8), :], a.shin, [x_peer, core_peer], L)

    tasks["P"] = small_sums()

    def gain_sum():
        def copy(j):
            return pltpu.make_async_remote_copy(
                src_ref=a.ngain,
                dst_ref=a.ngin.at[me],
                send_sem=a.nsend.at[j],
                recv_sem=a.nrecv.at[me],
                device_id=(j, head),
                device_id_type=MESH,
            )

        def arrival(j):
            return pltpu.make_async_remote_copy(
                src_ref=a.ngain,
                dst_ref=a.ngin.at[j],
                send_sem=a.nsend.at[j],
                recv_sem=a.nrecv.at[j],
                device_id=(j, head),
                device_id_type=MESH,
            )

        def start(j):
            @pl.when(j != me)
            def _():
                copy(j).start()

        def wait(j):
            @pl.when(j != me)
            def _():
                arrival(j).wait()

        loop(n, start)
        yield
        loop(n, wait)
        a.ngin[me] = a.ngain[...]
        a.ngain[...] = jnp.zeros(a.ngain.shape, F32)

        def add(j):
            a.ngain[...] += a.ngin[j]

        loop(n, add)

    tasks["N"] = gain_sum()

    pump("P")
    at("we")

    @pl.when(me < n - 1)
    def _():
        for copy in edges:
            copy.wait_recv()
        for s in range(S):
            a.dext[s, T : T + 8, :] = a.ev[s]
            a.dsext[s, T : T + 8, :] = a.es[s]

    @pl.when(me == n - 1)
    def _():
        for s in range(S):
            a.dext[s, T : T + 8, :] = jnp.zeros((8, C), F32)
            a.dsext[s, T : T + 8, :] = jnp.zeros((8, 2 * N), F32)

    @pl.when(me > 0)
    def _():
        for copy in edges:
            copy.wait_send()

    def conv_back(grad, w, out, shift, width):
        def one(s):
            for c in range(0, width, LANES):
                ch = slice(c, c + LANES)
                total = w[3:4, ch] * grad[s, 0:T, ch]
                for k in range(3):
                    total = total + w[k : k + 1, ch] * grad[s, pl.ds(3 - k, T), ch]
                out[s, :, shift + c : shift + c + LANES] = total.astype(BF)

        loop(S, one)

    conv_back(a.dsext, a.conv_shared, a.dsl, 0, 2 * N)
    weight_grad(a.gws, 0, D, lambda: a.dsl[...].reshape(S * T, 2 * N))
    pump("V3")
    at("v")
    conv_back(a.dext, a.conv_value, a.normed, C, C)
    at("vv")
    for c in range(4):
        weight_grad(a.gwv, c * D // 4, D // 4, lambda: a.normed[:, :, C : 2 * C].reshape(S * T, C))
        if c < 3:
            pump("V" + str(c))
        at("v" + str(c))

    def d_normed(s, f):
        rows = features(f)
        return (
            nt(a.normed[s, :, 0:C], a.gate_weight[rows, :])
            + nt(a.normed[s, :, C : 2 * C], a.value_weight[rows, :])
            + nt(a.dsl[s], a.shared_weight[rows, :])
            + mm(a.dst[s], a.stT[:, rows])
        )

    d_one, d_two, d_three = feature_sum("d", d_normed)
    for s in range(S):
        d_one(s)
        at("d" + str(s))
    for s in range(S):
        d_two(s)
        at("e" + str(s))
    for s in range(S):
        o_one(s)
        at("o" + str(s))

    own_gain = a.norm_gain[0:1, features(head)]

    def feature_rows(s):
        d = d_three(s)
        a.Y[s, :, 0:F] = d
        unit = a.tokens[s, :, features(head)].astype(F32) * a.raw[s, :, H : H + 1]
        a.ngain[0:1, :] += jnp.sum(d * unit, axis=0, keepdims=True)
        ones = jnp.ones((8, F), BF)
        dh, dl = split(d * own_gain * unit)
        dot = nt(ones, dh) + nt(ones, dl)
        row8 = lax.broadcasted_iota(jnp.int32, (8, T), 0)
        a.stat2[...] = jnp.where(row8 == s, dot, 0.0) + jnp.where(row8 < s, a.stat2[...], 0.0)

    a.ngain[...] = jnp.zeros(a.ngain.shape, F32)
    a.stat2[...] = jnp.zeros(a.stat2.shape, F32)
    for s in range(S):
        at("wf" + str(s))
        feature_rows(s)
        at("f" + str(s))
    pump("N")
    for s in range(S):
        o_two(s)
        at("n" + str(s))
    stats2 = head_sums(a.stat2, a.stin2, 15)
    for copy in stats2:
        copy.start()
    at("wst")
    for copy in stats2:
        copy.wait()
    total2 = a.stat2[...] + (a.stin2[0] + a.stin2[1]) + a.stin2[2]
    cols2 = jnp.concatenate([total2 / D, jnp.zeros((LANES - 8, T), F32)], axis=0).T
    for s in range(S):
        unit = a.tokens[s, :, features(head)].astype(F32) * a.raw[s, :, H : H + 1]
        inner_part = a.Y[s, :, 0:F] * own_gain - unit * cols2[:, s : s + 1]
        a.gtok[s] = a.cotangent[s].astype(F32) + a.raw[s, :, H : H + 1] * inner_part
    at("t")
    for s in range(S):
        at("wx" + str(s))
        out_rows(s)
        at("x" + str(s))
    at("end")
    for _ in range(2 * L + 8):
        pump(*tasks)
    done = [
        pltpu.make_async_copy(a.gwo, a.out_gwo, a.lsem.at[1]),
        pltpu.make_async_copy(a.gwg, a.out_gwg, a.lsem.at[2]),
        pltpu.make_async_copy(a.gwv.at[pl.ds(0, D), :], a.out_gwv, a.lsem.at[3]),
        pltpu.make_async_copy(a.gws, a.out_gws, a.lsem.at[4]),
    ]
    for copy in done:
        copy.start()
    a.o_small[...] = a.pack[...]
    a.o_ngain[...] = a.ngain[...]
    for copy in done:
        copy.wait()


INPUTS = [
    "tokens",
    "norm_gain",
    "gate_weight",
    "value_weight",
    "shared_weight",
    "step_weight",
    "conv_value",
    "conv_value_bias",
    "conv_shared",
    "conv_shared_bias",
    "step_bias",
    "decay_rate",
    "skip_weight",
    "out_gain",
    "output_weight",
    "cotangent",
]
OUTPUTS = ["mixed", "gtok", "out_gwg", "out_gwv", "out_gws", "out_gwo", "o_small", "o_ngain"]


def inbox_rows(size, count):
    total = 0
    for _ in range(count):
        size = size // 2 if can_halve(size) else size
        total += size
    return total


def scratch(dims):
    n, S, T, D, C, H, N, F = dims
    R = S // 2 * C // n
    L = n.bit_length() - 1
    vm = pltpu.VMEM
    dma = pltpu.SemaphoreType.DMA
    items = dict(
        tri=vm((T, T), BF),
        triT=vm((T, T), BF),
        E2=vm((2 * LANES, C), BF),
        ET=vm((C, LANES), BF),
        stT=vm((LANES, D), BF),
        skipE=vm((8, C), F32),
        hrow=vm((8, LANES), F32),
        small=vm((8, C), F32),
        heads_sm=vm((8, LANES), F32),
        shsm=vm((8, 2 * N), F32),
        normed=vm((S, T, D), BF),
        normT=vm((D, S * T), BF),
        halo=vm((S, 16, D), BF),
        cotf=vm((D // F, S, T, F), BF),
        vext=vm((S, T + 8, C), F32),
        sext=vm((S, T + 8, 2 * N), F32),
        raw=vm((S, T, LANES), F32),
        cum=vm((S, T, LANES), F32),
        cumT=vm((S, 8, T), F32),
        decay=vm((S, 8, LANES), F32),
        V=vm((S, T, C), BF),
        KR=vm((S, T, 2 * N), BF),
        dsv=vm((S, T, C), BF),
        dss=vm((S, T, 2 * N), BF),
        U=vm((S, T, C), BF),
        tU=vm((S, T, C), BF),
        sp=vm((S * C, N), F32),
        Sin=vm((S * C, N), F32),
        gout=vm((S * C, N), F32),
        joined=vm((2, LANES, N), F32),
        gate=vm((S, T, C), F32),
        Y=vm((S, T, C), F32),
        stat=vm((2, 8, T), F32),
        stin=vm((2, 3, 8, T), F32),
        stat2=vm((8, T), F32),
        stin2=vm((3, 8, T), F32),
        gcols=vm((T, LANES), F32),
        ny=vm((S, T, C), BF),
        nyT=vm((C, S * T), BF),
        dY=vm((S, T, C), BF),
        ecdY=vm((S, T, C), BF),
        dGT=vm((S, T, T), BF),
        dext=vm((S, T + 8, C), F32),
        dsext=vm((S, T + 8, 2 * N), F32),
        ev=vm((S, 8, C), F32),
        es=vm((S, 8, 2 * N), F32),
        dsl=vm((S, T, 2 * N), BF),
        dst=vm((S, T, LANES), BF),
        dstT=vm((16, S * T), BF),
        stepsum=vm((8, D), F32),
        gwo=vm((2 * C, D // 2), BF),
        gwo_in=vm((2 * inbox_rows(C, L), D // 2), BF),
        gwg=vm((D, C), BF),
        gwg_in=vm((2 * inbox_rows(D // 2, L), C), BF),
        gwv=vm((D + D // 8, C), BF),
        gwv_in=vm((3 * inbox_rows(D // 4, L) + inbox_rows(D // 4 + D // 8, L), C), BF),
        gws=vm((D, 2 * N), BF),
        gws_in=vm((inbox_rows(D, 2), 2 * N), BF),
        ngain=vm((8, F), F32),
        pack=vm((24, D), F32),
        packin=vm((L, 24, D), F32),
        shin=vm((2, 8, D), F32),
        ngin=vm((n, 8, F), F32),
        ssem=dma((18,)),
        rsem=dma((18,)),
        lsem=dma((5,)),
        asend=dma((16 * L + 4,)),
        arecv=dma((16 * L + 4,)),
        afree=pltpu.SemaphoreType.REGULAR((16 * L + 4,)),
        psend=dma((L + 2,)),
        precv=dma((L + 2,)),
        nsend=dma((n,)),
        nrecv=dma((n,)),
    )
    for key in ("m10", "m11", "o20", "o21"):
        items[key] = vm((n, R + 16, N), BF)
    items["sb1"] = vm((S, 2, T, F), BF)
    items["sb2"] = vm((S, T, F), BF)
    for tag in ("f0", "f1", "b0", "b1"):
        for key in ("i1", "i2"):
            items[key + tag] = vm((n, R + 16, N), BF)
        for key in ("s1", "r1", "s2", "r2"):
            items[key + tag] = dma((n,))
    for tag in "od":
        items["rb1" + tag] = vm((S, 2, T, F), BF)
        items["rb2" + tag] = vm((S, T, F), BF)
        items["fsem" + tag] = dma((4, S))
    return items


def dims_names(dims):
    return INPUTS + OUTPUTS + list(scratch(dims))


def finish(dims, mixed, gtok, gwg, gwv, gws, left, right, small, ngain, *outs):
    n, S, T, D, C, H, N, F = dims
    PW = C // H
    outs[0][...] = mixed[...]
    outs[1][...] = gtok[...]
    outs[3][...] = gwg[...].astype(F32)
    outs[4][...] = gwv[...].astype(F32)
    outs[5][...] = gws[...].astype(F32)
    outs[15][:, 0 : D // 2] = left[...].astype(F32)
    outs[15][:, D // 2 : D] = right[...].astype(F32)

    @pl.when(pl.program_id(0) == 0)
    def _():
        outs[2][...] = ngain[0:1, :]
        outs[6][...] = small[8 : 8 + H, :]
        outs[7][...] = small[0:4, 0:C]
        outs[8][...] = small[4:5, 0:C]
        outs[9][...] = small[16:20, 0 : 2 * N]
        outs[10][...] = small[20:21, 0 : 2 * N]
        outs[11][...] = small[0:1, C : C + H]
        outs[12][...] = small[1:2, C : C + H]
        sums = [jnp.sum(small[6:7, h * PW : (h + 1) * PW], axis=1, keepdims=True) for h in range(H)]
        outs[13][...] = jnp.concatenate(sums, axis=1)
        outs[14][...] = small[5:6, 0:C]


def shards(*args):
    tokens, gate_weight, step_weight, shared_weight = args[0], args[2], args[5], args[4]
    cotangent = args[15]
    S, T, D = tokens.shape
    C, H, N, F = gate_weight.shape[1], step_weight.shape[1], shared_weight.shape[1] // 2, cotangent.shape[2]
    n = lax.axis_size("seq")
    dims = (n, S, T, D, C, H, N, F)
    args = [x.reshape(1, -1) if x.ndim == 1 else x for x in args]
    args[5] = step_weight.T
    items = scratch(dims)
    whole = pl.BlockSpec(memory_space=pltpu.VMEM)
    hbm = pl.BlockSpec(memory_space=pl.ANY)
    struct = jax.ShapeDtypeStruct
    mixed, gtok, gwg, gwv, gws, gwo, small, ngain = pl.pallas_call(
        lambda *refs: kernel(dims, *refs),
        out_shape=(
            struct((S, T, F), BF),
            struct((S, T, F), F32),
            struct((D, C), BF),
            struct((D, C), BF),
            struct((D, 2 * N), BF),
            struct((2 * C, D // 2), BF),
            struct((24, D), F32),
            struct((8, F), F32),
        ),
        in_specs=[whole] * len(args),
        out_specs=(whole, whole, hbm, hbm, hbm, hbm, whole, whole),
        scratch_shapes=list(items.values()),
        compiler_params=pltpu.CompilerParams(
            collective_id=0, has_side_effects=True, vmem_limit_bytes=63 * 2**20
        ),
        name="block",
    )(*args)
    outs = pl.pallas_call(
        lambda *refs: finish(dims, *refs),
        grid=(S,),
        out_shape=(
            struct((S, T, F), BF),
            struct((S, T, F), F32),
            struct((1, F), F32),
            struct((D, C), F32),
            struct((D, C), F32),
            struct((D, 2 * N), F32),
            struct((H, D), F32),
            struct((4, C), F32),
            struct((1, C), F32),
            struct((4, 2 * N), F32),
            struct((1, 2 * N), F32),
            struct((1, H), F32),
            struct((1, H), F32),
            struct((1, H), F32),
            struct((1, C), F32),
            struct((C, D), F32),
        ),
        in_specs=[
            pl.BlockSpec((1, T, F), lambda i: (i, 0, 0)),
            pl.BlockSpec((1, T, F), lambda i: (i, 0, 0)),
            pl.BlockSpec((D // S, C), lambda i: (i, 0)),
            pl.BlockSpec((D // S, C), lambda i: (i, 0)),
            pl.BlockSpec((D // S, 2 * N), lambda i: (i, 0)),
            pl.BlockSpec((C // S, D // 2), lambda i: (i, 0)),
            pl.BlockSpec((C // S, D // 2), lambda i: (i + S, 0)),
            pl.BlockSpec((24, D), lambda i: (0, 0)),
            pl.BlockSpec((8, F), lambda i: (0, 0)),
        ],
        out_specs=(
            pl.BlockSpec((1, T, F), lambda i: (i, 0, 0)),
            pl.BlockSpec((1, T, F), lambda i: (i, 0, 0)),
            pl.BlockSpec((1, F), lambda i: (0, 0)),
            pl.BlockSpec((D // S, C), lambda i: (i, 0)),
            pl.BlockSpec((D // S, C), lambda i: (i, 0)),
            pl.BlockSpec((D // S, 2 * N), lambda i: (i, 0)),
            pl.BlockSpec((H, D), lambda i: (0, 0)),
            pl.BlockSpec((4, C), lambda i: (0, 0)),
            pl.BlockSpec((1, C), lambda i: (0, 0)),
            pl.BlockSpec((4, 2 * N), lambda i: (0, 0)),
            pl.BlockSpec((1, 2 * N), lambda i: (0, 0)),
            pl.BlockSpec((1, H), lambda i: (0, 0)),
            pl.BlockSpec((1, H), lambda i: (0, 0)),
            pl.BlockSpec((1, H), lambda i: (0, 0)),
            pl.BlockSpec((1, C), lambda i: (0, 0)),
            pl.BlockSpec((C // S, D), lambda i: (i, 0)),
        ),
        name="finish",
    )(mixed, gtok, gwg, gwv, gws, gwo, gwo, small, ngain)
    outs = list(outs)
    outs[6] = outs[6].T
    for i in (2, 8, 10, 11, 12, 13, 14):
        outs[i] = outs[i].reshape(-1)
    return tuple(outs)


def solution(mesh):
    head = P("head")
    return jax.shard_map(
        shards,
        mesh=mesh,
        in_specs=(
            P(None, "seq", None),
            P(),
            P(None, "head"),
            P(None, "head"),
            P(),
            P(None, "head"),
            P(None, "head"),
            head,
            P(),
            P(),
            head,
            head,
            head,
            head,
            P("head", None),
            P(None, "seq", "head"),
        ),
        out_specs=(
            P(None, "seq", "head"),
            P(None, "seq", "head"),
            head,
            P(None, "head"),
            P(None, "head"),
            P(),
            P(None, "head"),
            P(None, "head"),
            head,
            P(),
            P(),
            head,
            head,
            head,
            head,
            P("head", None),
        ),
        check_vma=False,
    )
```

```python
import jax
import jax.numpy as jnp
from jax import lax
from jax.experimental import pallas as pl
from jax.experimental.pallas import tpu as pltpu
from jax.sharding import PartitionSpec as P

EPSILON = 1e-05
F32 = jnp.float32
BF = jnp.bfloat16
MESH = pl.DeviceIdType.MESH
LANES = 128


def mm(a, b):
    return lax.dot_general(a, b, (((1,), (0,)), ((), ())), preferred_element_type=F32)


def nt(a, b):
    return lax.dot_general(a, b, (((1,), (1,)), ((), ())), preferred_element_type=F32)


def tn(a, b):
    return lax.dot_general(a, b, (((0,), (0,)), ((), ())), preferred_element_type=F32)


def split(x):
    high = x.astype(BF)
    return high, (x - high.astype(F32)).astype(BF)


def mm_exact_left(a, x):
    high, rest = x.astype(BF), x - x.astype(BF).astype(F32)
    mid, low = split(rest)
    return mm(a, high) + (mm(a, mid) + mm(a, low))


def sigmoid(x):
    return 0.5 * jnp.tanh(0.5 * x) + 0.5


def softplus(x):
    return jnp.maximum(x, 0.0) + jnp.log1p(jnp.exp(-jnp.abs(x)))


def loop(count, body):
    def step(i, carry):
        body(i)
        return carry

    lax.fori_loop(0, count, step, 0)


def can_halve(size):
    return size % 32 == 0


ORDERS = {"O0": 0, "O1": 0, "G0": 0, "G1": 1, "V0": 0, "V1": 0, "V2": 0, "V3": 0}
PLAN = {
    "wa1": ("O0",),
    "wb0": ("O1", "G1", "O0", "G0",),
    "s1": ("O1",),
    "s3": ("G1", "O0",),
    "c1": ("G0",),
    "we": ("G1", "O1", "O0",),
    "v": ("P",),
    "vv": ("G0", "G1",),
    "v2": ("O1", "V3", "O0",),
    "d1": ("P", "G0",),
    "d3": ("V0", "V3", "V1",),
    "o3": ("G1", "O1", "V2",),
    "wf1": ("P", "G0", "V0",),
    "f1": ("O0", "V1",),
    "wf3": ("V3",),
    "f3": ("P", "G1", "V2",),
    "n3": ("V0", "V1",),
    "wst": ("O1", "P", "V3", "V2", "V0", "G0", "V1", "N", "V3", "V0", "V2", "V1", "V3",),
    "t": ("V2", "V0",),
    "x3": ("V1",),
    "end": ("V3", "V2", "V3", "V3", "V3",),
}


class Reduced:
    def __init__(self, buf, base, rows, inbox, inbase, levels, sems, first):
        self.buf, self.inbox, self.levels = buf, inbox, levels
        self.send, self.recv, self.free = sems
        self.first = first
        self.lo, self.size, self.stack, self.offset = base, rows, [], inbase
        self.copies = {}

    def copy(self, src, dst, slot, partner):
        return pltpu.make_async_remote_copy(
            src_ref=src,
            dst_ref=dst,
            send_sem=self.send.at[slot],
            recv_sem=self.recv.at[slot],
            device_id=partner,
            device_id_type=MESH,
        )

    def start(self, level):
        partner, bit = self.levels[level]
        halved = can_halve(self.size)
        part = self.size // 2 if halved else self.size
        theirs = self.lo + (1 - bit) * part if halved else self.lo
        mine = self.lo + bit * part if halved else self.lo
        copy = self.copy(
            self.buf.at[pl.ds(pl.multiple_of(theirs, 16), part), :],
            self.inbox.at[pl.ds(self.offset, part), :],
            self.first + level,
            partner,
        )
        copy.start()
        self.copies[level] = (copy, mine, part, self.offset, halved)
        self.offset += part

    def finish(self, level):
        copy, mine, part, offset, halved = self.copies[level]
        copy.wait()
        if halved:
            pl.semaphore_signal(
                self.free.at[self.first + level],
                inc=1,
                device_id=self.levels[level][0],
                device_id_type=MESH,
            )
        block = 64 if part % 64 == 0 else part

        def add(i):
            rows = pl.ds(pl.multiple_of(mine + i * block, 16), block)
            got = self.inbox[pl.ds(pl.multiple_of(offset + i * block, 16), block), :]
            self.buf[rows, :] = (self.buf[rows, :].astype(F32) + got.astype(F32)).astype(BF)

        loop(part // block, add)
        self.stack.append((self.lo, self.size, halved))
        self.lo, self.size = mine, part

    def spread_start(self, level):
        slot = self.first + len(self.levels) + level
        rows = pl.ds(pl.multiple_of(self.lo, 16), self.size)
        pl.semaphore_wait(self.free.at[self.first + level], 1)
        self.copies[level] = self.copy(self.buf.at[rows, :], self.buf.at[rows, :], slot, self.levels[level][0])
        self.copies[level].start()

    def halves(self):
        for level in range(len(self.levels)):
            self.start(level)
            yield
            self.finish(level)

    def spread(self):
        for level in range(len(self.levels) - 1, -1, -1):
            lo, size, halved = self.stack[level]
            if halved:
                self.spread_start(level)
                yield
                self.copies[level].wait()
            self.lo, self.size = lo, size

    def steps(self):
        yield from self.halves()
        yield from self.spread()


def kernel(dims, *refs):
    n, S, T, D, C, H, N, F = dims
    PW = C // H
    Sh = S // 2
    R = Sh * C // n
    q = n // Sh
    groups = max(1, R // PW)
    span = R // groups
    names = dims_names(dims)
    ref = dict(zip(names, refs))

    class A:
        pass

    a = A()
    a.__dict__.update(ref)
    me = lax.axis_index("seq")
    head = lax.axis_index("head")
    flip = lambda value, bit: value + bit - 2 * bit * lax.rem(value // bit, 2)
    core_peer = (me, flip(head, 1))
    x_peer = (me, flip(head, 2))
    diag = (me, flip(flip(head, 1), 2))
    barrier = pltpu.get_barrier_semaphore()
    for peer in (core_peer, x_peer, diag):
        pl.semaphore_signal(barrier, inc=1, device_id=peer, device_id_type=MESH)

    def greet(i):
        peer = (lax.rem(me + i + 1, n), head)
        pl.semaphore_signal(barrier, inc=1, device_id=peer, device_id_type=MESH)

    loop(n - 1, greet)

    lane = lax.broadcasted_iota(jnp.int32, (T, LANES), 1)
    first_half = lane < PW

    rows_i = lax.broadcasted_iota(jnp.int32, (T, T), 0)
    cols_i = lax.broadcasted_iota(jnp.int32, (T, T), 1)
    a.tri[...] = jnp.where(rows_i >= cols_i, 1.0, 0.0).astype(BF)
    a.triT[...] = jnp.where(rows_i <= cols_i, 1.0, 0.0).astype(BF)
    er = lax.broadcasted_iota(jnp.int32, (2 * LANES, C), 0)
    ec_ = lax.broadcasted_iota(jnp.int32, (2 * LANES, C), 1)
    a.E2[...] = jnp.where(lax.rem(er, LANES) == ec_ // PW, 1.0, 0.0).astype(BF)
    tr = lax.broadcasted_iota(jnp.int32, (C, LANES), 0)
    tc = lax.broadcasted_iota(jnp.int32, (C, LANES), 1)
    a.ET[...] = jnp.where(tr // PW == tc, 1.0, 0.0).astype(BF)
    a.stT[...] = jnp.zeros(a.stT.shape, BF)
    a.stT[0:H, :] = a.step_weight[...]
    a.small[...] = jnp.zeros(a.small.shape, F32)
    a.heads_sm[...] = jnp.zeros(a.heads_sm.shape, F32)
    a.shsm[...] = jnp.zeros(a.shsm.shape, F32)
    a.hrow[...] = jnp.zeros(a.hrow.shape, F32)
    a.hrow[0:1, 0:H] = a.step_bias[...]
    a.hrow[1:2, 0:H] = a.decay_rate[...]
    a.hrow[2:3, 0:H] = a.skip_weight[...]
    bias_row = a.hrow[0:1, :]
    rate_row = a.hrow[1:2, :]

    def expand(x):
        high, low = split(x)
        return mm(jnp.concatenate([high, low], axis=1), a.E2[...])

    a.skipE[...] = expand(jnp.broadcast_to(a.hrow[2:3, :], (8, LANES)))
    skip_row = a.skipE[0:1, :]
    gain = a.norm_gain[...]

    def norm_rows(x):
        scale = lax.rsqrt(jnp.mean(x * x, axis=-1, keepdims=True) + EPSILON)
        return (x * scale * gain).astype(BF), scale

    def norm_block(b):
        s, r = b // 4, pl.multiple_of(lax.rem(b, 4) * (T // 4), T // 4)
        rows = pl.ds(r, T // 4)
        x = a.tokens[s, rows, :].astype(F32)
        low, scale = norm_rows(x)
        a.normed[s, rows, :] = low
        a.raw[s, rows, :] = jnp.broadcast_to(scale, (T // 4, LANES))

    pl.semaphore_wait(barrier, n - 1 + 3)

    def halo_copy():
        return pltpu.make_async_remote_copy(
            src_ref=a.tokens.at[:, pl.ds(T - 16, 16), :],
            dst_ref=a.halo,
            send_sem=a.ssem.at[0],
            recv_sem=a.rsem.at[0],
            device_id=(lax.rem(me + 1, n), head),
            device_id_type=MESH,
        )

    @pl.when(me < n - 1)
    def _():
        halo_copy().start()

    def cot_copy(src, slot, sem, peer):
        return pltpu.make_async_remote_copy(
            src_ref=src,
            dst_ref=a.cotf.at[slot],
            send_sem=a.ssem.at[sem],
            recv_sem=a.rsem.at[sem],
            device_id=peer,
            device_id_type=MESH,
        )

    cot_x = cot_copy(a.cotangent, head, 1, x_peer)
    cot_x.start()
    cot_c = cot_copy(a.cotangent, head, 2, core_peer)
    cot_c.start()
    cot_own = pltpu.make_async_copy(a.cotangent, a.cotf.at[head], a.lsem.at[0])
    cot_own.start()

    def half(which, f):
        loop(Sh, lambda i: f(which * Sh + i))

    loop(4 * Sh, norm_block)

    def project_b(s):
        x = a.normed[s]
        a.vext[s, 8 : 8 + T, :] = mm(x, a.value_weight[...])
        a.sext[s, 8 : 8 + T, :] = mm(x, a.shared_weight[...])
        a.raw[s] = jnp.where(lane == H, a.raw[s], nt(x, a.stT[...]) + bias_row)

    half(0, project_b)

    @pl.when(me > 0)
    def _():
        halo_copy().wait_recv()

    @pl.when(me == 0)
    def _():
        a.halo[...] = jnp.zeros(a.halo.shape, BF)

    @pl.when(me < n - 1)
    def _():
        halo_copy().wait_send()

    hx = jnp.concatenate([a.halo[s] for s in range(S)], axis=0).astype(F32)
    hlow, _ = norm_rows(hx)
    vh = mm(hlow, a.value_weight[...])
    sh = mm(hlow, a.shared_weight[...])
    for s in range(S):
        a.vext[s, 0:8, :] = vh[s * 16 + 8 : s * 16 + 16, :]
        a.sext[s, 0:8, :] = sh[s * 16 + 8 : s * 16 + 16, :]

    def conv(ext, w, b, s, c):
        running = b[0:1, c : c + LANES] + jnp.zeros((T, LANES), F32)
        for k in range(4):
            running = running + w[k : k + 1, c : c + LANES] * ext[s, pl.ds(5 + k, T), c : c + LANES]
        sig = sigmoid(running)
        return running * sig, sig * (1.0 + running * (1.0 - sig))

    def states(tag, reverse):
        m1, o2 = a.__dict__["m1" + tag[1]], a.__dict__["o2" + tag[1]]
        i1, i2 = (a.__dict__[k + tag] for k in ("i1", "i2"))
        s1, r1, s2, r2 = (a.__dict__[k + tag] for k in ("s1", "r1", "s2", "r2"))

        def first(k):
            return pltpu.make_async_remote_copy(
                src_ref=m1.at[k],
                dst_ref=i1.at[me],
                send_sem=s1.at[k],
                recv_sem=r1.at[me],
                device_id=(k, head),
                device_id_type=MESH,
            )

        def first_wait(k):
            return pltpu.make_async_remote_copy(
                src_ref=m1.at[k],
                dst_ref=i1.at[k],
                send_sem=s1.at[k],
                recv_sem=r1.at[k],
                device_id=(k, head),
                device_id_type=MESH,
            )

        def second(k):
            return pltpu.make_async_remote_copy(
                src_ref=o2.at[k, pl.ds(0, back_rows)],
                dst_ref=i2.at[me, pl.ds(0, back_rows)],
                send_sem=s2.at[k],
                recv_sem=r2.at[me],
                device_id=(k, head),
                device_id_type=MESH,
            )

        def second_wait(k):
            return pltpu.make_async_remote_copy(
                src_ref=o2.at[k, pl.ds(0, back_rows)],
                dst_ref=i2.at[k, pl.ds(0, back_rows)],
                send_sem=s2.at[k],
                recv_sem=r2.at[k],
                device_id=(k, head),
                device_id_type=MESH,
            )

        none = n - 1 if reverse else 0
        back_rows = R if reverse else R + 16

        def pack(i, state, decay):
            high, low = split(decay)
            hf, lf = high.astype(F32), low.astype(F32)
            for j in range(q):
                h0 = j * R // PW
                k = i * q + j
                m1[k, 0:R, :] = state[j * R : (j + 1) * R, :].astype(BF)
                both = [hf[h0:], hf[:h0], lf[h0:], lf[:h0]] if h0 else [hf, lf]
                m1[k, R : R + 16, :] = jnp.concatenate(both, axis=0).astype(BF)

                @pl.when(k != me)
                def _():
                    first(k).start()

                @pl.when(k == me)
                def _():
                    i1[k] = m1[k]

        group_row = lax.broadcasted_iota(jnp.int32, (8, LANES), 0)
        group_lane = lax.broadcasted_iota(jnp.int32, (8, LANES), 1) // span

        def join():
            def wait(k):
                @pl.when(k != me)
                def _():
                    first_wait(k).wait()

            loop(n, wait)

            def one(step):
                j = n - 1 - step if reverse else step
                tail = i1[j, R : R + 16, :].astype(F32)
                decay = tail[0:8] + tail[8:16]
                now = a.joined[step % 2 if isinstance(step, int) else lax.rem(step, 2)]
                if reverse:
                    o2[j, 0:R, :] = now[0:R].astype(BF)
                else:
                    means = [jnp.mean(now[g * span : (g + 1) * span], axis=0, keepdims=True) for g in range(groups)]
                    means = jnp.concatenate(means + [jnp.zeros((8 - groups, LANES), F32)], axis=0)
                    size = jnp.sum(means * means, axis=1, keepdims=True) + 1e-30
                    along = nt(means.astype(BF), now.astype(BF)) / size
                    along = jnp.where(group_row == group_lane, along, 0.0)
                    ah, mh = along.astype(BF).astype(F32), means.astype(BF).astype(F32)
                    al, ml = (along - ah).astype(BF).astype(F32), (means - mh).astype(BF).astype(F32)
                    left, right = [], []
                    for g in range(groups):
                        row = slice(g, g + 1)
                        left += [ah[row], ah[row], al[row]]
                        right += [mh[row], ml[row], mh[row]]
                    rest = [jnp.zeros((8 - 3 * groups, LANES), F32)]
                    left, right = jnp.concatenate(left + rest, axis=0), jnp.concatenate(right + rest, axis=0)
                    o2[j, 0:R, :] = (now - tn(left, right))[0:R].astype(BF)
                    o2[j, R : R + 16, :] = jnp.concatenate([left, right], axis=0).astype(BF)
                after = [
                    decay[g : g + 1, :] * now[g * span : (g + 1) * span]
                    + i1[j, g * span : (g + 1) * span, :].astype(F32)
                    for g in range(groups)
                ]
                if R < LANES:
                    after.append(jnp.zeros((LANES - R, N), F32))
                a.joined[(step + 1) % 2 if isinstance(step, int) else lax.rem(step + 1, 2)] = jnp.concatenate(after, axis=0)

                @pl.when((j != me) & (j != none))
                def _():
                    second(j).start()

                @pl.when((j == me) & (j != none))
                def _():
                    i2[j, 0:back_rows, :] = o2[j, 0:back_rows, :]

            a.joined[0] = jnp.zeros((LANES, N), F32)
            if n <= 8 and not reverse:
                for step in range(n):
                    one(step)
            else:
                loop(n, one)

        def collect(out, base):
            def wait(k):
                @pl.when((k != me) & (me != none))
                def _():
                    second_wait(k).wait_recv()

                @pl.when((k != me) & (k != none))
                def _():
                    second_wait(k).wait_send()

            loop(n, wait)

            @pl.when(me != none)
            def _():
                def one(k):
                    got = i2[k, 0:R, :].astype(F32)
                    if not reverse:
                        tail = i2[k, R : R + 16, :].astype(F32)
                        got = got + tn(tail[0:8], tail[8:16])[0:R]
                    out[pl.ds(pl.multiple_of(base + k * R, 16), R), :] = got

                if n <= 8:
                    for k in range(n):
                        one(k)
                else:
                    loop(n, one)

            @pl.when(me == none)
            def _():
                out[base : base + Sh * C, :] = jnp.zeros((Sh * C, N), F32)

        return pack, join, collect

    forward = [states("f" + x, False) for x in "01"]
    backward = [states("b" + x, True) for x in "01"]

    def scan_inputs(s, i, pack):
        for c in range(0, C, LANES):
            v, d = conv(a.vext, a.conv_value, a.conv_value_bias, s, c)
            a.V[s, :, c : c + LANES] = v.astype(BF)
            a.dsv[s, :, c : c + LANES] = d.astype(BF)
        for c in range(0, 2 * N, LANES):
            v, d = conv(a.sext, a.conv_shared, a.conv_shared_bias, s, c)
            a.KR[s, :, c : c + LANES] = v.astype(BF)
            a.dss[s, :, c : c + LANES] = d.astype(BF)
        raw = a.raw[s]
        steps = softplus(raw)
        cum = mm_exact_left(a.tri[...], -steps * rate_row)
        a.cum[s] = cum
        cumT = cum.T[0:8]
        a.cumT[s] = cumT
        last = cum[T - 1 : T, :]
        tail = jnp.exp(last - cum)
        V = a.V[s].astype(F32)
        a.U[s] = (expand(steps) * V).astype(BF)
        tU = (expand(steps * tail) * V).astype(BF)
        a.tU[s] = tU
        state = tn(tU, a.KR[s, :, 0:N])
        a.sp[pl.ds(pl.multiple_of(s * C, C), C), :] = state
        decay = jnp.broadcast_to(jnp.exp(cumT[:, T - 1 : T]), (8, LANES))
        a.decay[s] = decay
        pack(i, state, decay)

    def scan_half(which):
        loop(Sh, lambda i: scan_inputs(which * Sh + i, i, forward[which][0]))

    scan_half(0)
    loop(4 * Sh, lambda b: norm_block(4 * Sh + b))
    half(1, project_b)
    scan_half(1)

    def project_gate(s):
        a.gate[s] = mm(a.normed[s], a.gate_weight[...])

    def intra_forward(s):
        K, Rm = a.KR[s, :, 0:N], a.KR[s, :, N : 2 * N]
        G = jnp.where(rows_i >= cols_i, nt(Rm, K), 0.0)
        for p in range(H // 2):
            pair = slice(p * LANES, (p + 1) * LANES)
            U2 = a.U[s, :, pair]
            z = []
            for h in (2 * p, 2 * p + 1):
                gap = a.cum[s, :, h : h + 1] - a.cumT[s, h : h + 1, :]
                M = (jnp.exp(jnp.minimum(gap, 0.0)) * G).astype(BF)
                z.append(mm(M, U2))
            a.Y[s, :, pair] = jnp.where(first_half, z[0], z[1])

    loop(S, project_gate)
    half(0, intra_forward)
    forward[0][1]()
    half(1, intra_forward)

    cot_x.wait()
    cot_f = cot_copy(a.cotf.at[flip(head, 2)], flip(head, 2), 3, core_peer)
    cot_f.start()
    cot_c.wait()
    cot_f.wait()
    cot_own.wait()

    def back_out(s):
        total = nt(a.cotf[0, s], a.output_weight[:, 0:F])
        for f in range(1, D // F):
            total = total + nt(a.cotf[f, s], a.output_weight[:, f * F : (f + 1) * F])
        a.dext[s, 0:T, :] = total

    loop(S, back_out)
    forward[1][1]()

    def transposed(s):
        rows = pl.ds(pl.multiple_of(s * T, T), T)
        for c in range(0, D, 256):
            a.normT[c : c + 256, rows] = a.normed[s, :, c : c + 256].T

    loop(S, transposed)

    def outputs(s, i, stat):
        rows = pl.ds(pl.multiple_of(s * C, C), C)
        high, low = split(a.Sin[rows, :])
        Rm = a.KR[s, :, N : 2 * N]
        reach = expand(jnp.exp(a.cum[s]))
        outer = reach * (nt(Rm, high) + nt(Rm, low))
        Y = a.Y[s] + outer + skip_row * a.V[s].astype(F32)
        a.Y[s] = Y
        g = a.gate[s]
        gated = Y * (g * sigmoid(g))
        dots = a.dext[s, 0:T, :] * a.out_gain[...] * gated
        ones = jnp.ones((8, C), BF)
        sq = nt(ones, (gated * gated).astype(BF))
        dt = nt(ones, dots.astype(BF))
        row8 = lax.broadcasted_iota(jnp.int32, (8, T), 0)
        part = jnp.where(row8 == 2 * i, sq, 0.0) + jnp.where(row8 == 2 * i + 1, dt, 0.0)
        stat[...] = part + jnp.where(row8 < 2 * i, stat[...], 0.0)

    def head_sums(stat, inbox, first):
        return [
            pltpu.make_async_remote_copy(
                src_ref=stat,
                dst_ref=inbox.at[i],
                send_sem=a.ssem.at[first + i],
                recv_sem=a.rsem.at[first + i],
                device_id=peer,
                device_id_type=MESH,
            )
            for i, peer in enumerate((x_peer, diag, core_peer))
        ]

    stats = [head_sums(a.stat.at[w], a.stin.at[w], 9 + 3 * w) for w in range(2)]
    inner = C * lax.axis_size("head")

    def output_half(w):
        a.stat[w] = jnp.zeros((8, T), F32)
        loop(Sh, lambda i: outputs(w * Sh + i, i, a.stat.at[w]))
        for copy in stats[w]:
            copy.start()

    def stat_half(w):
        for copy in stats[w]:
            copy.wait()
        total = a.stat[w] + (a.stin[w, 0] + a.stin[w, 1]) + a.stin[w, 2]
        columns = []
        for i in range(Sh):
            scale = lax.rsqrt(total[2 * i : 2 * i + 1] / inner + EPSILON)
            columns += [scale, total[2 * i + 1 : 2 * i + 2] * scale / inner]
        stacked = jnp.concatenate(columns + [jnp.zeros((LANES - 2 * Sh, T), F32)], axis=0).T
        for i in range(Sh):
            a.gscale[i] = jnp.broadcast_to(stacked[:, 2 * i : 2 * i + 1], (T, LANES))
            a.gmean[i] = jnp.broadcast_to(stacked[:, 2 * i + 1 : 2 * i + 2], (T, LANES))

    def gate_back(s, i, pack):
        reach = expand(jnp.exp(a.cum[s]))
        scale, mean = a.gscale[i], a.gmean[i]
        cols = pl.ds(pl.multiple_of(s * T, T), T)
        for c in range(0, C, LANES):
            ch = slice(c, c + LANES)
            g, Y = a.gate[s, :, ch], a.Y[s, :, ch]
            sig = sigmoid(g)
            act = g * sig
            gu = Y * act * scale
            og = a.out_gain[0:1, ch]
            ny = gu * og
            a.ny[s, :, ch] = ny.astype(BF)
            a.nyT[ch, cols] = ny.T.astype(BF)
            dn = a.dext[s, 0:T, ch]
            a.small[5:6, ch] += jnp.sum(dn * gu, axis=0, keepdims=True)
            dg = scale * (dn * og - gu * mean)
            dY = (dg * act).astype(BF)
            a.dY[s, :, ch] = dY
            a.ecdY[s, :, ch] = (reach[:, ch] * dY.astype(F32)).astype(BF)
            a.normed[s, :, ch] = (dg * Y * sig * (1.0 + g * (1.0 - sig))).astype(BF)
        state = tn(a.ecdY[s], a.KR[s, :, N : 2 * N])
        pack(i, state, a.decay[s])

    for w in range(2):
        forward[w][2](a.Sin, w * Sh * C)
        output_half(w)
    for w in range(2):
        stat_half(w)
        loop(Sh, lambda i: gate_back(w * Sh + i, i, backward[w][0]))

    levels = []
    bit = 1
    while bit < n:
        levels.append(((flip(me, bit), head), lax.rem(me // bit, 2)))
        bit *= 2
    L = len(levels)
    sems = (a.asend, a.arecv, a.afree)
    head_levels = [(core_peer, lax.rem(head, 2)), (x_peer, lax.rem(head // 2, 2))]
    later = levels[1:] + levels[:1]
    tasks = {}
    used = inbase = 0
    VR = D // 4
    SR = D // 4 // 2
    for name, buf, inbox, base, rows, order in (
        ("O0", a.gwo, a.gwo_in, 0, C, ORDERS["O0"]),
        ("O1", a.gwo, a.gwo_in, C, C, ORDERS["O1"]),
        ("G0", a.gwg, a.gwg_in, 0, D // 2, ORDERS["G0"]),
        ("G1", a.gwg, a.gwg_in, D // 2, D // 2, ORDERS["G1"]),
        ("V0", a.gwv, a.gwv_in, 0, VR, ORDERS["V0"]),
        ("V1", a.gwv, a.gwv_in, VR, VR, ORDERS["V1"]),
        ("V2", a.gwv, a.gwv_in, 2 * VR, VR, ORDERS["V2"]),
        ("W", a.gwv, a.gwv_in, 3 * VR, VR + SR, ORDERS["V3"]),
        ("H", a.gws, a.gws_in, 0, D, None),
    ):
        order = head_levels if order is None else (later if order else levels)
        inbase = 0 if name in ("O0", "G0", "V0", "H") else inbase
        tasks[name] = Reduced(buf, base, rows, inbox, inbase, order, sems, used)
        inbase += inbox_rows(rows, len(order))
        used += 2 * len(order)

    def last_chunk(over_heads, own):
        shared = over_heads.halves()
        yield from shared
        mine = pl.multiple_of(over_heads.lo, 16)
        for i in range(2):
            half = pl.ds(pl.multiple_of(mine + i * SR, 16), SR)
            a.gwv[D : D + SR, i * 2 * N : (i + 1) * 2 * N] = a.gws[half, :]
        yield from own.steps()
        for i in range(2):
            half = pl.ds(pl.multiple_of(mine + i * SR, 16), SR)
            a.gws[half, :] = a.gwv[D : D + SR, i * 2 * N : (i + 1) * 2 * N]
        yield from over_heads.spread()

    tasks["V3"] = last_chunk(tasks.pop("H"), tasks.pop("W"))
    for name in tasks:
        if name != "V3":
            tasks[name] = tasks[name].steps()

    def pump(*names):
        for name in names:
            next(tasks[name], None)

    def at(point):
        pump(*PLAN.get(point, ()))

    def feature_sum(tag, block):
        sb1, sb2 = a.sb1, a.sb2
        rb1, rb2 = (a.__dict__[k + tag] for k in ("rb1", "rb2"))
        sem = a.__dict__["fsem" + tag]

        def copy1(s):
            return pltpu.make_async_remote_copy(
                src_ref=sb1.at[s],
                dst_ref=rb1.at[s],
                send_sem=sem.at[0, s],
                recv_sem=sem.at[1, s],
                device_id=core_peer,
                device_id_type=MESH,
            )

        def copy2(s):
            return pltpu.make_async_remote_copy(
                src_ref=sb2.at[s],
                dst_ref=rb2.at[s],
                send_sem=sem.at[2, s],
                recv_sem=sem.at[3, s],
                device_id=x_peer,
                device_id_type=MESH,
            )

        def one(s):
            sb1[s, 0] = block(s, flip(head, 1)).astype(BF)
            sb1[s, 1] = block(s, flip(flip(head, 1), 2)).astype(BF)
            copy1(s).start()

        def two(s):
            far = block(s, flip(head, 2))
            copy1(s).wait()
            sb2[s] = (far + rb1[s, 1].astype(F32)).astype(BF)
            copy2(s).start()

        def three(s):
            near = block(s, head)
            copy2(s).wait()
            return near + rb1[s, 0].astype(F32) + rb2[s].astype(F32)

        return one, two, three

    def features(f):
        return pl.ds(pl.multiple_of(f * F, F), F)

    o_one, o_two, o_three = feature_sum("o", lambda s, f: mm(a.ny[s], a.output_weight[:, features(f)]))

    def grad_out_weight(half_index):
        for g in range(D // F // 2):
            f = half_index * (D // F // 2) + g
            x = mm(a.nyT[...], a.cotf[f].reshape(S * T, F))
            a.gwo[half_index * C : (half_index + 1) * C, g * F : (g + 1) * F] = x.astype(BF)

    def weight_grad(out, r, rows, columns):
        out[r : r + rows, :] = mm(a.normT[r : r + rows, :], columns()).astype(BF)

    def intra_backward(s):
        K, Rm = a.KR[s, :, 0:N], a.KR[s, :, N : 2 * N]
        GT = jnp.where(rows_i <= cols_i, nt(K, Rm), 0.0)
        dGT = jnp.zeros((T, T), F32)
        for p in range(H // 2):
            pair = slice(p * LANES, (p + 1) * LANES)
            dY2, U2 = a.dY[s, :, pair], a.U[s, :, pair]
            z = []
            for h in (2 * p, 2 * p + 1):
                gap = a.cumT[s, h : h + 1, :] - a.cum[s, :, h : h + 1]
                LT = jnp.exp(jnp.minimum(gap, 0.0))
                mine = first_half if h == 2 * p else jnp.logical_not(first_half)
                Um = jnp.where(mine, U2.astype(F32), 0.0).astype(BF)
                dGT = dGT + nt(Um, dY2) * LT
                z.append(mm((LT * GT).astype(BF), dY2))
            a.dext[s, 0:T, pair] = jnp.where(first_half, z[0], z[1])
        a.dGT[s] = jnp.where(rows_i <= cols_i, dGT, 0.0).astype(BF)

    def out_rows(s):
        total = o_three(s)
        own = a.tokens[s, :, features(head)].astype(F32)
        a.mixed[s] = (own + total).astype(BF)

    def state_back(s):
        rows = pl.ds(pl.multiple_of(s * C, C), C)
        K, Rm = a.KR[s, :, 0:N], a.KR[s, :, N : 2 * N]
        gout, Sin = a.gout[rows, :], a.Sin[rows, :]
        gob = gout.astype(BF)
        cum, steps = a.cum[s], softplus(a.raw[s])
        tail = expand(jnp.exp(cum[T - 1 : T, :] - cum))
        V = a.V[s].astype(F32)
        dY = a.dY[s].astype(F32)
        dU = a.dext[s, 0:T, :] + tail * nt(K, gob)
        skipV = skip_row * V
        dV = expand(steps) * dU + skip_row * dY
        a.small[6:7, :] += jnp.sum(dY * V, axis=0, keepdims=True)
        ph, plo = split(dU * V)
        dsd = mm(ph, a.ET[...]) + mm(plo, a.ET[...])
        ph, plo = split(dY * (a.Y[s] - skipV))
        row = mm(ph, a.ET[...]) + mm(plo, a.ET[...])
        dcv = dV * a.dsv[s].astype(F32)
        a.dext[s, 0:T, :] = dcv
        dGT = a.dGT[s]
        sh, sl = split(Sin)
        dK = mm(dGT, Rm) + mm(a.tU[s], gob)
        dR = tn(dGT, K) + (mm(a.ecdY[s], sh) + mm(a.ecdY[s], sl))
        a.dsext[s, 0:T, 0:N] = dK * a.dss[s, :, 0:N].astype(F32)
        a.dsext[s, 0:T, N : 2 * N] = dR * a.dss[s, :, N : 2 * N].astype(F32)
        decay = a.decay[s]
        sums = []
        for h in range(H):
            hs = slice(h * PW, (h + 1) * PW)
            sp = a.sp[pl.ds(pl.multiple_of(s * C + h * PW, PW), PW), :]
            sums.append(jnp.sum(gout[hs] * (decay[h : h + 1] * Sin[hs] + sp), axis=0, keepdims=True))
        sums = jnp.concatenate(sums + [jnp.zeros((LANES - H, LANES), F32)], axis=0)
        ones = jnp.ones((8, LANES), BF)
        lh, ll = split(sums)
        end = (nt(ones, lh) + nt(ones, ll))[0:1]
        dld = mm_exact_left(a.triT[...], row - steps * dsd) + end
        draw = (dsd - rate_row * dld) * sigmoid(a.raw[s])
        a.heads_sm[0:1, :] += jnp.sum(draw, axis=0, keepdims=True)
        a.heads_sm[1:2, :] -= jnp.sum(steps * dld, axis=0, keepdims=True)
        a.dst[s] = draw.astype(BF)
        a.dstT[:, pl.ds(pl.multiple_of(s * T, T), T)] = draw.T[0:16].astype(BF)

    def gate_grad(r):
        weight_grad(a.gwg, r * D // 2, D // 2, lambda: a.normed[:, :, 0:C].reshape(S * T, C))

    grad_out_weight(0)
    pump("O0")
    grad_out_weight(1)
    pump("O1")
    at("g")
    gate_grad(0)
    pump("G0")
    at("g0")
    half(0, intra_backward)
    at("i1")
    at("wa0")
    backward[0][1]()
    at("p1")
    gate_grad(1)
    pump("G1")
    at("g1")
    at("wa1")
    backward[1][1]()
    at("p4")
    half(1, intra_backward)
    at("i3")
    at("wb0")
    backward[0][2](a.gout, 0)
    half(0, state_back)
    at("s1")
    at("wb1")
    backward[1][2](a.gout, Sh * C)
    half(1, state_back)
    at("s3")
    a.stepsum[...] = nt(a.dstT[...], a.normT[...])[0:8]

    def edge_copy(src, dst, sem):
        return pltpu.make_async_remote_copy(
            src_ref=src.at[:, pl.ds(0, 8), :],
            dst_ref=dst,
            send_sem=a.ssem.at[sem],
            recv_sem=a.rsem.at[sem],
            device_id=(lax.rem(me + n - 1, n), head),
            device_id_type=MESH,
        )

    edges = [edge_copy(a.dext, a.ev, 7), edge_copy(a.dsext, a.es, 8)]

    @pl.when(me > 0)
    def _():
        for copy in edges:
            copy.start()


    def conv_grads(s):
        for ext, grad, out, base, width in (
            (a.vext, a.dext, a.small, 0, C),
            (a.sext, a.dsext, a.shsm, 0, 2 * N),
        ):
            for c in range(0, width, LANES):
                ch = slice(c, c + LANES)
                d = grad[s, 0:T, ch]
                for k in range(4):
                    x = ext[s, pl.ds(5 + k, T), ch]
                    out[base + k : base + k + 1, ch] += jnp.sum(d * x, axis=0, keepdims=True)
                out[base + 4 : base + 5, ch] += jnp.sum(d, axis=0, keepdims=True)

    half(0, conv_grads)
    at("c0")
    half(1, conv_grads)
    at("c1")
    a.pack[...] = jnp.zeros(a.pack.shape, F32)
    a.pack[0:7, 0:C] = a.small[0:7, :]
    a.pack[0:2, C : C + LANES] = a.heads_sm[0:2, :]
    a.pack[8:16, :] = a.stepsum[...]
    a.pack[16:21, 0 : 2 * N] = a.shsm[0:5, :]

    def whole_sum(buf, inbox, partners, first):
        for i, partner in enumerate(partners):
            copy = pltpu.make_async_remote_copy(
                src_ref=buf,
                dst_ref=inbox.at[i],
                send_sem=a.psend.at[first + i],
                recv_sem=a.precv.at[first + i],
                device_id=partner,
                device_id_type=MESH,
            )
            copy.start()
            yield
            copy.wait()
            buf[...] = buf[...] + inbox[i]

    def small_sums():
        partners = [partner for partner, _ in levels]
        yield from whole_sum(a.pack, a.packin, partners, 0)
        yield from whole_sum(a.pack.at[pl.ds(16, 8), :], a.shin, [x_peer, core_peer], L)

    tasks["P"] = small_sums()

    def gain_sum():
        def copy(j):
            return pltpu.make_async_remote_copy(
                src_ref=a.ngain,
                dst_ref=a.ngin.at[me],
                send_sem=a.nsend.at[j],
                recv_sem=a.nrecv.at[me],
                device_id=(j, head),
                device_id_type=MESH,
            )

        def arrival(j):
            return pltpu.make_async_remote_copy(
                src_ref=a.ngain,
                dst_ref=a.ngin.at[j],
                send_sem=a.nsend.at[j],
                recv_sem=a.nrecv.at[j],
                device_id=(j, head),
                device_id_type=MESH,
            )

        def start(j):
            @pl.when(j != me)
            def _():
                copy(j).start()

        def wait(j):
            @pl.when(j != me)
            def _():
                arrival(j).wait()

        loop(n, start)
        yield
        loop(n, wait)
        a.ngin[me] = a.ngain[...]
        a.ngain[...] = jnp.zeros(a.ngain.shape, F32)

        def add(j):
            a.ngain[...] += a.ngin[j]

        loop(n, add)

    tasks["N"] = gain_sum()

    pump("P")
    at("we")

    @pl.when(me < n - 1)
    def _():
        for copy in edges:
            copy.wait_recv()
        for s in range(S):
            a.dext[s, T : T + 8, :] = a.ev[s]
            a.dsext[s, T : T + 8, :] = a.es[s]

    @pl.when(me == n - 1)
    def _():
        for s in range(S):
            a.dext[s, T : T + 8, :] = jnp.zeros((8, C), F32)
            a.dsext[s, T : T + 8, :] = jnp.zeros((8, 2 * N), F32)

    @pl.when(me > 0)
    def _():
        for copy in edges:
            copy.wait_send()

    def conv_back(grad, w, out, shift, width):
        def one(s):
            for c in range(0, width, LANES):
                ch = slice(c, c + LANES)
                total = w[3:4, ch] * grad[s, 0:T, ch]
                for k in range(3):
                    total = total + w[k : k + 1, ch] * grad[s, pl.ds(3 - k, T), ch]
                out[s, :, shift + c : shift + c + LANES] = total.astype(BF)

        loop(S, one)

    conv_back(a.dsext, a.conv_shared, a.dsl, 0, 2 * N)
    weight_grad(a.gws, 0, D, lambda: a.dsl[...].reshape(S * T, 2 * N))
    pump("V3")
    at("v")
    conv_back(a.dext, a.conv_value, a.normed, C, C)
    at("vv")
    for c in range(4):
        weight_grad(a.gwv, c * D // 4, D // 4, lambda: a.normed[:, :, C : 2 * C].reshape(S * T, C))
        if c < 3:
            pump("V" + str(c))
        at("v" + str(c))

    def d_normed(s, f):
        rows = features(f)
        return (
            nt(a.normed[s, :, 0:C], a.gate_weight[rows, :])
            + nt(a.normed[s, :, C : 2 * C], a.value_weight[rows, :])
            + nt(a.dsl[s], a.shared_weight[rows, :])
            + mm(a.dst[s], a.stT[:, rows])
        )

    d_one, d_two, d_three = feature_sum("d", d_normed)
    half(0, d_one)
    at("d1")
    half(1, d_one)
    at("d3")
    half(0, d_two)
    at("e1")
    half(1, d_two)
    at("e3")
    loop(S, o_one)
    at("o3")

    own_gain = a.norm_gain[0:1, features(head)]

    def feature_rows(s):
        d = d_three(s)
        a.Y[s, :, 0:F] = d
        unit = a.tokens[s, :, features(head)].astype(F32) * a.raw[s, :, H : H + 1]
        a.ngain[0:1, :] += jnp.sum(d * unit, axis=0, keepdims=True)
        ones = jnp.ones((8, F), BF)
        dh, dl = split(d * own_gain * unit)
        dot = nt(ones, dh) + nt(ones, dl)
        row8 = lax.broadcasted_iota(jnp.int32, (8, T), 0)
        a.stat2[...] = jnp.where(row8 == s, dot, 0.0) + jnp.where(row8 < s, a.stat2[...], 0.0)

    a.ngain[...] = jnp.zeros(a.ngain.shape, F32)
    a.stat2[...] = jnp.zeros(a.stat2.shape, F32)
    at("wf1")
    half(0, feature_rows)
    at("f1")
    at("wf3")
    half(1, feature_rows)
    at("f3")
    pump("N")
    loop(S, o_two)
    at("n3")
    stats2 = head_sums(a.stat2, a.stin2, 15)
    for copy in stats2:
        copy.start()
    at("wst")
    for copy in stats2:
        copy.wait()
    total2 = a.stat2[...] + (a.stin2[0] + a.stin2[1]) + a.stin2[2]
    cols2 = jnp.concatenate([total2 / D, jnp.zeros((LANES - 8, T), F32)], axis=0).T
    for s in range(S):
        unit = a.tokens[s, :, features(head)].astype(F32) * a.raw[s, :, H : H + 1]
        inner_part = a.Y[s, :, 0:F] * own_gain - unit * cols2[:, s : s + 1]
        a.gtok[s] = a.cotangent[s].astype(F32) + a.raw[s, :, H : H + 1] * inner_part
    at("t")
    at("wx3")
    loop(S, out_rows)
    at("x3")
    at("end")
    for _ in range(2 * L + 8):
        pump(*tasks)
    done = [
        pltpu.make_async_copy(a.gwo, a.out_gwo, a.lsem.at[1]),
        pltpu.make_async_copy(a.gwg, a.out_gwg, a.lsem.at[2]),
        pltpu.make_async_copy(a.gwv.at[pl.ds(0, D), :], a.out_gwv, a.lsem.at[3]),
        pltpu.make_async_copy(a.gws, a.out_gws, a.lsem.at[4]),
    ]
    for copy in done:
        copy.start()
    a.o_small[...] = a.pack[...]
    a.o_ngain[...] = a.ngain[...]
    for copy in done:
        copy.wait()


INPUTS = [
    "tokens",
    "norm_gain",
    "gate_weight",
    "value_weight",
    "shared_weight",
    "step_weight",
    "conv_value",
    "conv_value_bias",
    "conv_shared",
    "conv_shared_bias",
    "step_bias",
    "decay_rate",
    "skip_weight",
    "out_gain",
    "output_weight",
    "cotangent",
]
OUTPUTS = ["mixed", "gtok", "out_gwg", "out_gwv", "out_gws", "out_gwo", "o_small", "o_ngain"]


def inbox_rows(size, count):
    total = 0
    for _ in range(count):
        size = size // 2 if can_halve(size) else size
        total += size
    return total


def scratch(dims):
    n, S, T, D, C, H, N, F = dims
    R = S // 2 * C // n
    L = n.bit_length() - 1
    vm = pltpu.VMEM
    dma = pltpu.SemaphoreType.DMA
    items = dict(
        tri=vm((T, T), BF),
        triT=vm((T, T), BF),
        E2=vm((2 * LANES, C), BF),
        ET=vm((C, LANES), BF),
        stT=vm((LANES, D), BF),
        skipE=vm((8, C), F32),
        hrow=vm((8, LANES), F32),
        small=vm((8, C), F32),
        heads_sm=vm((8, LANES), F32),
        shsm=vm((8, 2 * N), F32),
        normed=vm((S, T, D), BF),
        normT=vm((D, S * T), BF),
        halo=vm((S, 16, D), BF),
        cotf=vm((D // F, S, T, F), BF),
        vext=vm((S, T + 8, C), F32),
        sext=vm((S, T + 8, 2 * N), F32),
        raw=vm((S, T, LANES), F32),
        cum=vm((S, T, LANES), F32),
        cumT=vm((S, 8, T), F32),
        decay=vm((S, 8, LANES), F32),
        V=vm((S, T, C), BF),
        KR=vm((S, T, 2 * N), BF),
        dsv=vm((S, T, C), BF),
        dss=vm((S, T, 2 * N), BF),
        U=vm((S, T, C), BF),
        tU=vm((S, T, C), BF),
        sp=vm((S * C, N), F32),
        Sin=vm((S * C, N), F32),
        gout=vm((S * C, N), F32),
        joined=vm((2, LANES, N), F32),
        gate=vm((S, T, C), F32),
        Y=vm((S, T, C), F32),
        stat=vm((2, 8, T), F32),
        stin=vm((2, 3, 8, T), F32),
        stat2=vm((8, T), F32),
        stin2=vm((3, 8, T), F32),
        gscale=vm((S // 2, T, LANES), F32),
        gmean=vm((S // 2, T, LANES), F32),
        ny=vm((S, T, C), BF),
        nyT=vm((C, S * T), BF),
        dY=vm((S, T, C), BF),
        ecdY=vm((S, T, C), BF),
        dGT=vm((S, T, T), BF),
        dext=vm((S, T + 8, C), F32),
        dsext=vm((S, T + 8, 2 * N), F32),
        ev=vm((S, 8, C), F32),
        es=vm((S, 8, 2 * N), F32),
        dsl=vm((S, T, 2 * N), BF),
        dst=vm((S, T, LANES), BF),
        dstT=vm((16, S * T), BF),
        stepsum=vm((8, D), F32),
        gwo=vm((2 * C, D // 2), BF),
        gwo_in=vm((2 * inbox_rows(C, L), D // 2), BF),
        gwg=vm((D, C), BF),
        gwg_in=vm((2 * inbox_rows(D // 2, L), C), BF),
        gwv=vm((D + D // 8, C), BF),
        gwv_in=vm((3 * inbox_rows(D // 4, L) + inbox_rows(D // 4 + D // 8, L), C), BF),
        gws=vm((D, 2 * N), BF),
        gws_in=vm((inbox_rows(D, 2), 2 * N), BF),
        ngain=vm((8, F), F32),
        pack=vm((24, D), F32),
        packin=vm((L, 24, D), F32),
        shin=vm((2, 8, D), F32),
        ngin=vm((n, 8, F), F32),
        ssem=dma((18,)),
        rsem=dma((18,)),
        lsem=dma((5,)),
        asend=dma((16 * L + 4,)),
        arecv=dma((16 * L + 4,)),
        afree=pltpu.SemaphoreType.REGULAR((16 * L + 4,)),
        psend=dma((L + 2,)),
        precv=dma((L + 2,)),
        nsend=dma((n,)),
        nrecv=dma((n,)),
    )
    for key in ("m10", "m11", "o20", "o21"):
        items[key] = vm((n, R + 16, N), BF)
    items["sb1"] = vm((S, 2, T, F), BF)
    items["sb2"] = vm((S, T, F), BF)
    for tag in ("f0", "f1", "b0", "b1"):
        for key in ("i1", "i2"):
            items[key + tag] = vm((n, R + 16, N), BF)
        for key in ("s1", "r1", "s2", "r2"):
            items[key + tag] = dma((n,))
    for tag in "od":
        items["rb1" + tag] = vm((S, 2, T, F), BF)
        items["rb2" + tag] = vm((S, T, F), BF)
        items["fsem" + tag] = dma((4, S))
    return items


def dims_names(dims):
    return INPUTS + OUTPUTS + list(scratch(dims))


def finish(dims, mixed, gtok, gwg, gwv, gws, left, right, small, ngain, *outs):
    n, S, T, D, C, H, N, F = dims
    PW = C // H
    outs[0][...] = mixed[...]
    outs[1][...] = gtok[...]
    outs[3][...] = gwg[...].astype(F32)
    outs[4][...] = gwv[...].astype(F32)
    outs[5][...] = gws[...].astype(F32)
    outs[15][:, 0 : D // 2] = left[...].astype(F32)
    outs[15][:, D // 2 : D] = right[...].astype(F32)

    @pl.when(pl.program_id(0) == 0)
    def _():
        outs[2][...] = ngain[0:1, :]
        outs[6][...] = small[8 : 8 + H, :]
        outs[7][...] = small[0:4, 0:C]
        outs[8][...] = small[4:5, 0:C]
        outs[9][...] = small[16:20, 0 : 2 * N]
        outs[10][...] = small[20:21, 0 : 2 * N]
        outs[11][...] = small[0:1, C : C + H]
        outs[12][...] = small[1:2, C : C + H]
        sums = [jnp.sum(small[6:7, h * PW : (h + 1) * PW], axis=1, keepdims=True) for h in range(H)]
        outs[13][...] = jnp.concatenate(sums, axis=1)
        outs[14][...] = small[5:6, 0:C]


def shards(*args):
    tokens, gate_weight, step_weight, shared_weight = args[0], args[2], args[5], args[4]
    cotangent = args[15]
    S, T, D = tokens.shape
    C, H, N, F = gate_weight.shape[1], step_weight.shape[1], shared_weight.shape[1] // 2, cotangent.shape[2]
    n = lax.axis_size("seq")
    dims = (n, S, T, D, C, H, N, F)
    args = [x.reshape(1, -1) if x.ndim == 1 else x for x in args]
    args[5] = step_weight.T
    items = scratch(dims)
    whole = pl.BlockSpec(memory_space=pltpu.VMEM)
    hbm = pl.BlockSpec(memory_space=pl.ANY)
    struct = jax.ShapeDtypeStruct
    mixed, gtok, gwg, gwv, gws, gwo, small, ngain = pl.pallas_call(
        lambda *refs: kernel(dims, *refs),
        out_shape=(
            struct((S, T, F), BF),
            struct((S, T, F), F32),
            struct((D, C), BF),
            struct((D, C), BF),
            struct((D, 2 * N), BF),
            struct((2 * C, D // 2), BF),
            struct((24, D), F32),
            struct((8, F), F32),
        ),
        in_specs=[whole] * len(args),
        out_specs=(whole, whole, hbm, hbm, hbm, hbm, whole, whole),
        scratch_shapes=list(items.values()),
        compiler_params=pltpu.CompilerParams(
            collective_id=0, has_side_effects=True, vmem_limit_bytes=63 * 2**20
        ),
        name="block",
    )(*args)
    outs = pl.pallas_call(
        lambda *refs: finish(dims, *refs),
        grid=(S,),
        out_shape=(
            struct((S, T, F), BF),
            struct((S, T, F), F32),
            struct((1, F), F32),
            struct((D, C), F32),
            struct((D, C), F32),
            struct((D, 2 * N), F32),
            struct((H, D), F32),
            struct((4, C), F32),
            struct((1, C), F32),
            struct((4, 2 * N), F32),
            struct((1, 2 * N), F32),
            struct((1, H), F32),
            struct((1, H), F32),
            struct((1, H), F32),
            struct((1, C), F32),
            struct((C, D), F32),
        ),
        in_specs=[
            pl.BlockSpec((1, T, F), lambda i: (i, 0, 0)),
            pl.BlockSpec((1, T, F), lambda i: (i, 0, 0)),
            pl.BlockSpec((D // S, C), lambda i: (i, 0)),
            pl.BlockSpec((D // S, C), lambda i: (i, 0)),
            pl.BlockSpec((D // S, 2 * N), lambda i: (i, 0)),
            pl.BlockSpec((C // S, D // 2), lambda i: (i, 0)),
            pl.BlockSpec((C // S, D // 2), lambda i: (i + S, 0)),
            pl.BlockSpec((24, D), lambda i: (0, 0)),
            pl.BlockSpec((8, F), lambda i: (0, 0)),
        ],
        out_specs=(
            pl.BlockSpec((1, T, F), lambda i: (i, 0, 0)),
            pl.BlockSpec((1, T, F), lambda i: (i, 0, 0)),
            pl.BlockSpec((1, F), lambda i: (0, 0)),
            pl.BlockSpec((D // S, C), lambda i: (i, 0)),
            pl.BlockSpec((D // S, C), lambda i: (i, 0)),
            pl.BlockSpec((D // S, 2 * N), lambda i: (i, 0)),
            pl.BlockSpec((H, D), lambda i: (0, 0)),
            pl.BlockSpec((4, C), lambda i: (0, 0)),
            pl.BlockSpec((1, C), lambda i: (0, 0)),
            pl.BlockSpec((4, 2 * N), lambda i: (0, 0)),
            pl.BlockSpec((1, 2 * N), lambda i: (0, 0)),
            pl.BlockSpec((1, H), lambda i: (0, 0)),
            pl.BlockSpec((1, H), lambda i: (0, 0)),
            pl.BlockSpec((1, H), lambda i: (0, 0)),
            pl.BlockSpec((1, C), lambda i: (0, 0)),
            pl.BlockSpec((C // S, D), lambda i: (i, 0)),
        ),
        name="finish",
    )(mixed, gtok, gwg, gwv, gws, gwo, gwo, small, ngain)
    outs = list(outs)
    outs[6] = outs[6].T
    for i in (2, 8, 10, 11, 12, 13, 14):
        outs[i] = outs[i].reshape(-1)
    return tuple(outs)


def solution(mesh):
    head = P("head")
    return jax.shard_map(
        shards,
        mesh=mesh,
        in_specs=(
            P(None, "seq", None),
            P(),
            P(None, "head"),
            P(None, "head"),
            P(),
            P(None, "head"),
            P(None, "head"),
            head,
            P(),
            P(),
            head,
            head,
            head,
            head,
            P("head", None),
            P(None, "seq", "head"),
        ),
        out_specs=(
            P(None, "seq", "head"),
            P(None, "seq", "head"),
            head,
            P(None, "head"),
            P(None, "head"),
            P(),
            P(None, "head"),
            P(None, "head"),
            head,
            P(),
            P(),
            head,
            head,
            head,
            head,
            P("head", None),
        ),
        check_vma=False,
    )
```

```python
import jax
import jax.numpy as jnp
from jax import lax
from jax.experimental import pallas as pl
from jax.experimental.pallas import tpu as pltpu
from jax.sharding import PartitionSpec as P

EPSILON = 1e-05
F32 = jnp.float32
BF = jnp.bfloat16
MESH = pl.DeviceIdType.MESH
LANES = 128


def mm(a, b):
    return lax.dot_general(a, b, (((1,), (0,)), ((), ())), preferred_element_type=F32)


def nt(a, b):
    return lax.dot_general(a, b, (((1,), (1,)), ((), ())), preferred_element_type=F32)


def tn(a, b):
    return lax.dot_general(a, b, (((0,), (0,)), ((), ())), preferred_element_type=F32)


def split(x):
    high = x.astype(BF)
    return high, (x - high.astype(F32)).astype(BF)


def mm_exact_left(a, x):
    high, rest = x.astype(BF), x - x.astype(BF).astype(F32)
    mid, low = split(rest)
    return mm(a, high) + (mm(a, mid) + mm(a, low))


def sigmoid(x):
    return 0.5 * jnp.tanh(0.5 * x) + 0.5


def softplus(x):
    return jnp.maximum(x, 0.0) + jnp.log1p(jnp.exp(-jnp.abs(x)))


def loop(count, body):
    def step(i, carry):
        body(i)
        return carry

    lax.fori_loop(0, count, step, 0)


def can_halve(size):
    return size % 32 == 0


STEPS = 2
ORDERS = dict(O0=0, O1=0, G0=1, G1=0, V0=0, V1=0, V3=0)
PLAN = {
    "wa1": ("O0",),
    "i3": ("G0",),
    "wb0": ("O1",),
    "s1": ("O0",),
    "wb1": ("G1",),
    "s3": ("G0", "O1",),
    "c0": ("O0",),
    "we": ("G1", "G0",),
    "v": ("O1", "P",),
    "v3": ("O0", "G0",),
    "v1": ("G1", "V3",),
    "d1": ("P",),
    "d3": ("O1", "O0",),
    "e1": ("V0", "V3",),
    "e3": ("G0",),
    "wf1": ("V1", "G1", "O1", "P",),
    "f1": ("V0", "O0",),
    "wf3": ("V3", "G0",),
    "f3": ("P", "V1",),
    "wst": ("G1", "O1", "P", "V0", "V3", "V1", "N", "V0", "V3", "G1", "V1", "V0",),
    "t": ("V3",),
    "x3": ("V1",),
    "end": ("V0", "V3", "V1", "V3", "V3", "V3",),
}


class Reduced:
    def __init__(self, buf, base, rows, inbox, inbase, levels, sems, first):
        self.buf, self.inbox, self.levels = buf, inbox, levels
        self.send, self.recv, self.free = sems
        self.first = first
        self.lo, self.size, self.stack, self.offset = base, rows, [], inbase
        self.copies = {}

    def copy(self, src, dst, slot, partner):
        return pltpu.make_async_remote_copy(
            src_ref=src,
            dst_ref=dst,
            send_sem=self.send.at[slot],
            recv_sem=self.recv.at[slot],
            device_id=partner,
            device_id_type=MESH,
        )

    def start(self, level):
        partner, bit = self.levels[level]
        halved = can_halve(self.size)
        part = self.size // 2 if halved else self.size
        theirs = self.lo + (1 - bit) * part if halved else self.lo
        mine = self.lo + bit * part if halved else self.lo
        copy = self.copy(
            self.buf.at[pl.ds(pl.multiple_of(theirs, 16), part), :],
            self.inbox.at[pl.ds(self.offset, part), :],
            self.first + level,
            partner,
        )
        copy.start()
        self.copies[level] = (copy, mine, part, self.offset, halved)
        self.offset += part

    def finish(self, level):
        copy, mine, part, offset, halved = self.copies[level]
        copy.wait()
        if halved:
            pl.semaphore_signal(
                self.free.at[self.first + level],
                inc=1,
                device_id=self.levels[level][0],
                device_id_type=MESH,
            )
        block = 64 if part % 64 == 0 else part

        def add(i):
            rows = pl.ds(pl.multiple_of(mine + i * block, 16), block)
            got = self.inbox[pl.ds(pl.multiple_of(offset + i * block, 16), block), :]
            self.buf[rows, :] = (self.buf[rows, :].astype(F32) + got.astype(F32)).astype(BF)

        loop(part // block, add)
        self.stack.append((self.lo, self.size, halved))
        self.lo, self.size = mine, part

    def spread_start(self, level):
        slot = self.first + len(self.levels) + level
        rows = pl.ds(pl.multiple_of(self.lo, 16), self.size)
        pl.semaphore_wait(self.free.at[self.first + level], 1)
        self.copies[level] = self.copy(self.buf.at[rows, :], self.buf.at[rows, :], slot, self.levels[level][0])
        self.copies[level].start()

    def halves(self):
        for level in range(len(self.levels)):
            self.start(level)
            yield
            self.finish(level)

    def spread(self):
        for level in range(len(self.levels) - 1, -1, -1):
            lo, size, halved = self.stack[level]
            if halved:
                self.spread_start(level)
                yield
                self.copies[level].wait()
            self.lo, self.size = lo, size

    def steps(self):
        yield from self.halves()
        yield from self.spread()


def kernel(dims, *refs):
    n, S, T, D, C, H, N, F = dims
    PW = C // H
    Sh = S // 2
    R = Sh * C // n
    q = n // Sh
    groups = max(1, R // PW)
    span = R // groups
    names = dims_names(dims)
    ref = dict(zip(names, refs))

    class A:
        pass

    a = A()
    a.__dict__.update(ref)
    me = lax.axis_index("seq")
    head = lax.axis_index("head")
    flip = lambda value, bit: value + bit - 2 * bit * lax.rem(value // bit, 2)
    core_peer = (me, flip(head, 1))
    x_peer = (me, flip(head, 2))
    diag = (me, flip(flip(head, 1), 2))
    barrier = pltpu.get_barrier_semaphore()
    for peer in (core_peer, x_peer, diag):
        pl.semaphore_signal(barrier, inc=1, device_id=peer, device_id_type=MESH)

    def greet(i):
        peer = (lax.rem(me + i + 1, n), head)
        pl.semaphore_signal(barrier, inc=1, device_id=peer, device_id_type=MESH)

    loop(n - 1, greet)

    lane = lax.broadcasted_iota(jnp.int32, (T, LANES), 1)
    first_half = lane < PW

    rows_i = lax.broadcasted_iota(jnp.int32, (T, T), 0)
    cols_i = lax.broadcasted_iota(jnp.int32, (T, T), 1)
    a.tri[...] = jnp.where(rows_i >= cols_i, 1.0, 0.0).astype(BF)
    a.triT[...] = jnp.where(rows_i <= cols_i, 1.0, 0.0).astype(BF)
    er = lax.broadcasted_iota(jnp.int32, (2 * LANES, C), 0)
    ec_ = lax.broadcasted_iota(jnp.int32, (2 * LANES, C), 1)
    a.E2[...] = jnp.where(lax.rem(er, LANES) == ec_ // PW, 1.0, 0.0).astype(BF)
    tr = lax.broadcasted_iota(jnp.int32, (C, LANES), 0)
    tc = lax.broadcasted_iota(jnp.int32, (C, LANES), 1)
    a.ET[...] = jnp.where(tr // PW == tc, 1.0, 0.0).astype(BF)
    a.stT[...] = jnp.zeros(a.stT.shape, BF)
    a.stT[0:H, :] = a.step_weight[...]
    a.small[...] = jnp.zeros(a.small.shape, F32)
    a.heads_sm[...] = jnp.zeros(a.heads_sm.shape, F32)
    a.shsm[...] = jnp.zeros(a.shsm.shape, F32)
    a.hrow[...] = jnp.zeros(a.hrow.shape, F32)
    a.hrow[0:1, 0:H] = a.step_bias[...]
    a.hrow[1:2, 0:H] = a.decay_rate[...]
    a.hrow[2:3, 0:H] = a.skip_weight[...]
    bias_row = a.hrow[0:1, :]
    rate_row = a.hrow[1:2, :]

    def expand(x):
        high, low = split(x)
        return mm(jnp.concatenate([high, low], axis=1), a.E2[...])

    a.skipE[...] = expand(jnp.broadcast_to(a.hrow[2:3, :], (8, LANES)))
    skip_row = a.skipE[0:1, :]
    gain = a.norm_gain[...]

    def norm_rows(x):
        scale = lax.rsqrt(jnp.mean(x * x, axis=-1, keepdims=True) + EPSILON)
        return (x * scale * gain).astype(BF), scale

    def norm_block(b):
        s, r = b // 4, pl.multiple_of(lax.rem(b, 4) * (T // 4), T // 4)
        rows = pl.ds(r, T // 4)
        x = a.tokens[s, rows, :].astype(F32)
        low, scale = norm_rows(x)
        a.normed[s, rows, :] = low
        a.raw[s, rows, :] = jnp.broadcast_to(scale, (T // 4, LANES))

    def half(which, f):
        loop(Sh, lambda i: f(which * Sh + i))

    loop(4 * Sh, norm_block)
    pl.semaphore_wait(barrier, n - 1 + 3)

    def halo_copy():
        return pltpu.make_async_remote_copy(
            src_ref=a.tokens.at[:, pl.ds(T - 16, 16), :],
            dst_ref=a.halo,
            send_sem=a.ssem.at[0],
            recv_sem=a.rsem.at[0],
            device_id=(lax.rem(me + 1, n), head),
            device_id_type=MESH,
        )

    @pl.when(me < n - 1)
    def _():
        halo_copy().start()

    def cot_copy(src, slot, sem, peer):
        return pltpu.make_async_remote_copy(
            src_ref=src,
            dst_ref=a.cotf.at[slot],
            send_sem=a.ssem.at[sem],
            recv_sem=a.rsem.at[sem],
            device_id=peer,
            device_id_type=MESH,
        )

    cot_x = cot_copy(a.cotangent, head, 1, x_peer)
    cot_x.start()
    cot_c = cot_copy(a.cotangent, head, 2, core_peer)
    cot_c.start()
    cot_own = pltpu.make_async_copy(a.cotangent, a.cotf.at[head], a.lsem.at[0])
    cot_own.start()

    def project_b(s):
        x = a.normed[s]
        a.vext[s, 8 : 8 + T, :] = mm(x, a.value_weight[...])
        a.sext[s, 8 : 8 + T, :] = mm(x, a.shared_weight[...])
        a.raw[s] = jnp.where(lane == H, a.raw[s], nt(x, a.stT[...]) + bias_row)

    half(0, project_b)

    @pl.when(me > 0)
    def _():
        halo_copy().wait_recv()

    @pl.when(me == 0)
    def _():
        a.halo[...] = jnp.zeros(a.halo.shape, BF)

    @pl.when(me < n - 1)
    def _():
        halo_copy().wait_send()

    hx = jnp.concatenate([a.halo[s] for s in range(S)], axis=0).astype(F32)
    hlow, _ = norm_rows(hx)
    vh = mm(hlow, a.value_weight[...])
    sh = mm(hlow, a.shared_weight[...])
    for s in range(S):
        a.vext[s, 0:8, :] = vh[s * 16 + 8 : s * 16 + 16, :]
        a.sext[s, 0:8, :] = sh[s * 16 + 8 : s * 16 + 16, :]

    def conv(ext, w, b, s, c):
        running = b[0:1, c : c + LANES] + jnp.zeros((T, LANES), F32)
        for k in range(4):
            running = running + w[k : k + 1, c : c + LANES] * ext[s, pl.ds(5 + k, T), c : c + LANES]
        sig = sigmoid(running)
        return running * sig, sig * (1.0 + running * (1.0 - sig))

    def states(tag, reverse):
        m1, o2 = a.__dict__["m1" + tag[1]], a.__dict__["o2" + tag[1]]
        i1, i2 = (a.__dict__[k + tag] for k in ("i1", "i2"))
        s1, r1, s2, r2 = (a.__dict__[k + tag] for k in ("s1", "r1", "s2", "r2"))

        def first(k):
            return pltpu.make_async_remote_copy(
                src_ref=m1.at[k],
                dst_ref=i1.at[me],
                send_sem=s1.at[k],
                recv_sem=r1.at[me],
                device_id=(k, head),
                device_id_type=MESH,
            )

        def first_wait(k):
            return pltpu.make_async_remote_copy(
                src_ref=m1.at[k],
                dst_ref=i1.at[k],
                send_sem=s1.at[k],
                recv_sem=r1.at[k],
                device_id=(k, head),
                device_id_type=MESH,
            )

        def second(k):
            return pltpu.make_async_remote_copy(
                src_ref=o2.at[k, pl.ds(0, back_rows)],
                dst_ref=i2.at[me, pl.ds(0, back_rows)],
                send_sem=s2.at[k],
                recv_sem=r2.at[me],
                device_id=(k, head),
                device_id_type=MESH,
            )

        def second_wait(k):
            return pltpu.make_async_remote_copy(
                src_ref=o2.at[k, pl.ds(0, back_rows)],
                dst_ref=i2.at[k, pl.ds(0, back_rows)],
                send_sem=s2.at[k],
                recv_sem=r2.at[k],
                device_id=(k, head),
                device_id_type=MESH,
            )

        none = n - 1 if reverse else 0
        back_rows = R if reverse else R + 16

        def pack(i, state, decay):
            high, low = split(decay)
            hf, lf = high.astype(F32), low.astype(F32)
            for j in range(q):
                h0 = j * R // PW
                k = i * q + j
                m1[k, 0:R, :] = state[j * R : (j + 1) * R, :].astype(BF)
                both = [hf[h0:], hf[:h0], lf[h0:], lf[:h0]] if h0 else [hf, lf]
                m1[k, R : R + 16, :] = jnp.concatenate(both, axis=0).astype(BF)

                @pl.when(k != me)
                def _():
                    first(k).start()

                @pl.when(k == me)
                def _():
                    i1[k] = m1[k]

        group_row = lax.broadcasted_iota(jnp.int32, (8, LANES), 0)
        group_lane = lax.broadcasted_iota(jnp.int32, (8, LANES), 1) // span

        def join():
            def wait(k):
                @pl.when(k != me)
                def _():
                    first_wait(k).wait()

            loop(n, wait)

            def one(step):
                j = n - 1 - step if reverse else step
                tail = i1[j, R : R + 16, :].astype(F32)
                decay = tail[0:8] + tail[8:16]
                now = a.joined[step % 2 if isinstance(step, int) else lax.rem(step, 2)]
                if reverse:
                    o2[j, 0:R, :] = now[0:R].astype(BF)
                else:
                    means = [jnp.mean(now[g * span : (g + 1) * span], axis=0, keepdims=True) for g in range(groups)]
                    means = jnp.concatenate(means + [jnp.zeros((8 - groups, LANES), F32)], axis=0)
                    size = jnp.sum(means * means, axis=1, keepdims=True) + 1e-30
                    along = nt(means.astype(BF), now.astype(BF)) / size
                    along = jnp.where(group_row == group_lane, along, 0.0)
                    ah, mh = along.astype(BF).astype(F32), means.astype(BF).astype(F32)
                    al, ml = (along - ah).astype(BF).astype(F32), (means - mh).astype(BF).astype(F32)
                    left, right = [], []
                    for g in range(groups):
                        row = slice(g, g + 1)
                        left += [ah[row], ah[row], al[row]]
                        right += [mh[row], ml[row], mh[row]]
                    rest = [jnp.zeros((8 - 3 * groups, LANES), F32)]
                    left, right = jnp.concatenate(left + rest, axis=0), jnp.concatenate(right + rest, axis=0)
                    o2[j, 0:R, :] = (now - tn(left, right))[0:R].astype(BF)
                    o2[j, R : R + 16, :] = jnp.concatenate([left, right], axis=0).astype(BF)
                after = [
                    decay[g : g + 1, :] * now[g * span : (g + 1) * span]
                    + i1[j, g * span : (g + 1) * span, :].astype(F32)
                    for g in range(groups)
                ]
                if R < LANES:
                    after.append(jnp.zeros((LANES - R, N), F32))
                a.joined[(step + 1) % 2 if isinstance(step, int) else lax.rem(step + 1, 2)] = jnp.concatenate(after, axis=0)

                @pl.when((j != me) & (j != none))
                def _():
                    second(j).start()

                @pl.when((j == me) & (j != none))
                def _():
                    i2[j, 0:back_rows, :] = o2[j, 0:back_rows, :]

            a.joined[0] = jnp.zeros((LANES, N), F32)
            if n <= 8 and not reverse:
                for step in range(n):
                    one(step)
            else:
                loop(n, one)

        def collect(out, base):
            def wait(k):
                @pl.when((k != me) & (me != none))
                def _():
                    second_wait(k).wait_recv()

                @pl.when((k != me) & (k != none))
                def _():
                    second_wait(k).wait_send()

            loop(n, wait)

            @pl.when(me != none)
            def _():
                def one(k):
                    got = i2[k, 0:R, :].astype(F32)
                    if not reverse:
                        tail = i2[k, R : R + 16, :].astype(F32)
                        got = got + tn(tail[0:8], tail[8:16])[0:R]
                    out[pl.ds(pl.multiple_of(base + k * R, 16), R), :] = got

                if n <= 8:
                    for k in range(n):
                        one(k)
                else:
                    loop(n, one)

            @pl.when(me == none)
            def _():
                out[base : base + Sh * C, :] = jnp.zeros((Sh * C, N), F32)

        return pack, join, collect

    forward = [states("f" + x, False) for x in "01"]
    backward = [states("b" + x, True) for x in "01"]

    def scan_inputs(s, i, pack):
        for c in range(0, C, LANES):
            v, d = conv(a.vext, a.conv_value, a.conv_value_bias, s, c)
            a.V[s, :, c : c + LANES] = v.astype(BF)
            a.dsv[s, :, c : c + LANES] = d.astype(BF)
        for c in range(0, 2 * N, LANES):
            v, d = conv(a.sext, a.conv_shared, a.conv_shared_bias, s, c)
            a.KR[s, :, c : c + LANES] = v.astype(BF)
            a.dss[s, :, c : c + LANES] = d.astype(BF)
        raw = a.raw[s]
        steps = softplus(raw)
        cum = mm_exact_left(a.tri[...], -steps * rate_row)
        a.cum[s] = cum
        cumT = cum.T[0:8]
        a.cumT[s] = cumT
        last = cum[T - 1 : T, :]
        tail = jnp.exp(last - cum)
        V = a.V[s].astype(F32)
        a.U[s] = (expand(steps) * V).astype(BF)
        tU = (expand(steps * tail) * V).astype(BF)
        a.tU[s] = tU
        state = tn(tU, a.KR[s, :, 0:N])
        a.sp[pl.ds(pl.multiple_of(s * C, C), C), :] = state
        decay = jnp.broadcast_to(jnp.exp(cumT[:, T - 1 : T]), (8, LANES))
        a.decay[s] = decay
        pack(i, state, decay)

    def scan_half(which):
        loop(Sh, lambda i: scan_inputs(which * Sh + i, i, forward[which][0]))

    scan_half(0)
    loop(4 * Sh, lambda b: norm_block(4 * Sh + b))
    half(1, project_b)
    scan_half(1)

    def project_gate(s):
        a.gate[s] = mm(a.normed[s], a.gate_weight[...])

    def intra_forward(s):
        K, Rm = a.KR[s, :, 0:N], a.KR[s, :, N : 2 * N]
        G = jnp.where(rows_i >= cols_i, nt(Rm, K), 0.0)
        for p in range(H // 2):
            pair = slice(p * LANES, (p + 1) * LANES)
            U2 = a.U[s, :, pair]
            z = []
            for h in (2 * p, 2 * p + 1):
                gap = a.cum[s, :, h : h + 1] - a.cumT[s, h : h + 1, :]
                M = (jnp.exp(jnp.minimum(gap, 0.0)) * G).astype(BF)
                z.append(mm(M, U2))
            a.Y[s, :, pair] = jnp.where(first_half, z[0], z[1])

    loop(S, project_gate)
    half(0, intra_forward)
    forward[0][1]()
    half(1, intra_forward)

    cot_x.wait()
    cot_f = cot_copy(a.cotf.at[flip(head, 2)], flip(head, 2), 3, core_peer)
    cot_f.start()
    cot_c.wait()
    cot_f.wait()
    cot_own.wait()

    def back_out(s):
        total = nt(a.cotf[0, s], a.output_weight[:, 0:F])
        for f in range(1, D // F):
            total = total + nt(a.cotf[f, s], a.output_weight[:, f * F : (f + 1) * F])
        a.dext[s, 0:T, :] = total

    loop(S, back_out)
    forward[1][1]()

    def transposed(s):
        rows = pl.ds(pl.multiple_of(s * T, T), T)
        for c in range(0, D, 256):
            a.normT[c : c + 256, rows] = a.normed[s, :, c : c + 256].T

    loop(S, transposed)

    def outputs(s, i, stat):
        rows = pl.ds(pl.multiple_of(s * C, C), C)
        high, low = split(a.Sin[rows, :])
        Rm = a.KR[s, :, N : 2 * N]
        reach = expand(jnp.exp(a.cum[s]))
        outer = reach * (nt(Rm, high) + nt(Rm, low))
        Y = a.Y[s] + outer + skip_row * a.V[s].astype(F32)
        a.Y[s] = Y
        g = a.gate[s]
        gated = Y * (g * sigmoid(g))
        dots = a.dext[s, 0:T, :] * a.out_gain[...] * gated
        ones = jnp.ones((8, C), BF)
        sq = nt(ones, (gated * gated).astype(BF))
        dt = nt(ones, dots.astype(BF))
        row8 = lax.broadcasted_iota(jnp.int32, (8, T), 0)
        part = jnp.where(row8 == 2 * i, sq, 0.0) + jnp.where(row8 == 2 * i + 1, dt, 0.0)
        stat[...] = part + jnp.where(row8 < 2 * i, stat[...], 0.0)

    def head_sums(stat, inbox, first):
        return [
            pltpu.make_async_remote_copy(
                src_ref=stat,
                dst_ref=inbox.at[i],
                send_sem=a.ssem.at[first + i],
                recv_sem=a.rsem.at[first + i],
                device_id=peer,
                device_id_type=MESH,
            )
            for i, peer in enumerate((x_peer, diag, core_peer))
        ]

    stats = [head_sums(a.stat.at[w], a.stin.at[w], 9 + 3 * w) for w in range(2)]
    inner = C * lax.axis_size("head")

    def output_half(w):
        a.stat[w] = jnp.zeros((8, T), F32)
        loop(Sh, lambda i: outputs(w * Sh + i, i, a.stat.at[w]))
        for copy in stats[w]:
            copy.start()

    def stat_half(w):
        for copy in stats[w]:
            copy.wait()
        total = a.stat[w] + (a.stin[w, 0] + a.stin[w, 1]) + a.stin[w, 2]
        columns = []
        for i in range(Sh):
            scale = lax.rsqrt(total[2 * i : 2 * i + 1] / inner + EPSILON)
            columns += [scale, total[2 * i + 1 : 2 * i + 2] * scale / inner]
        stacked = jnp.concatenate(columns + [jnp.zeros((LANES - 2 * Sh, T), F32)], axis=0).T
        for i in range(Sh):
            a.gscale[i] = jnp.broadcast_to(stacked[:, 2 * i : 2 * i + 1], (T, LANES))
            a.gmean[i] = jnp.broadcast_to(stacked[:, 2 * i + 1 : 2 * i + 2], (T, LANES))

    def normed_output(s, i):
        scale = a.gscale[i]
        cols = pl.ds(pl.multiple_of(s * T, T), T)
        for c in range(0, C, LANES):
            ch = slice(c, c + LANES)
            g = a.gate[s, :, ch]
            ny = a.Y[s, :, ch] * (g * sigmoid(g)) * scale * a.out_gain[0:1, ch]
            a.ny[s, :, ch] = ny.astype(BF)
            a.nyT[ch, cols] = ny.T.astype(BF)

    def gate_back(s, i, pack):
        reach = expand(jnp.exp(a.cum[s]))
        scale, mean = a.gscale[i], a.gmean[i]
        cols = pl.ds(pl.multiple_of(s * T, T), T)
        for c in range(0, C, LANES):
            ch = slice(c, c + LANES)
            g, Y = a.gate[s, :, ch], a.Y[s, :, ch]
            sig = sigmoid(g)
            act = g * sig
            gu = Y * act * scale
            og = a.out_gain[0:1, ch]
            dn = a.dext[s, 0:T, ch]
            a.small[5:6, ch] += jnp.sum(dn * gu, axis=0, keepdims=True)
            dg = scale * (dn * og - gu * mean)
            dY = (dg * act).astype(BF)
            a.dY[s, :, ch] = dY
            a.ecdY[s, :, ch] = (reach[:, ch] * dY.astype(F32)).astype(BF)
            a.normed[s, :, ch] = (dg * Y * sig * (1.0 + g * (1.0 - sig))).astype(BF)
        state = tn(a.ecdY[s], a.KR[s, :, N : 2 * N])
        pack(i, state, a.decay[s])

    for w in range(2):
        forward[w][2](a.Sin, w * Sh * C)
        output_half(w)
    for w in range(2):
        stat_half(w)
        loop(Sh, lambda i: gate_back(w * Sh + i, i, backward[w][0]))
        loop(Sh, lambda i: normed_output(w * Sh + i, i))

    levels = []
    bit = 1
    while bit < n:
        levels.append(((flip(me, bit), head), lax.rem(me // bit, 2)))
        bit *= 2
    L = len(levels)
    sems = (a.asend, a.arecv, a.afree)
    head_levels = [(core_peer, lax.rem(head, 2)), (x_peer, lax.rem(head // 2, 2))]
    later = levels[1:] + levels[:1]
    tasks = {}
    used = inbase = 0
    SR = D // 8
    VR = (D + SR) // 3
    for name, buf, inbox, base, rows, order in (
        ("O0", a.gwo, a.gwo_in, 0, C, ORDERS["O0"]),
        ("O1", a.gwo, a.gwo_in, C, C, ORDERS["O1"]),
        ("G0", a.gwg, a.gwg_in, 0, D // 2, ORDERS["G0"]),
        ("G1", a.gwg, a.gwg_in, D // 2, D // 2, ORDERS["G1"]),
        ("V0", a.gwv, a.gwv_in, 0, VR, ORDERS["V0"]),
        ("V1", a.gwv, a.gwv_in, VR, VR, ORDERS["V1"]),
        ("W", a.gwv, a.gwv_in, 2 * VR, VR, ORDERS["V3"]),
        ("H", a.gws, a.gws_in, 0, D, None),
    ):
        order = head_levels if order is None else (later if order else levels)
        inbase = 0 if name in ("O0", "G0", "V0", "H") else inbase
        tasks[name] = Reduced(buf, base, rows, inbox, inbase, order, sems, used)
        inbase += inbox_rows(rows, len(order))
        used += 2 * len(order)

    def last_chunk(over_heads, own):
        shared = over_heads.halves()
        yield from shared
        mine = pl.multiple_of(over_heads.lo, 16)
        for i in range(2):
            half = pl.ds(pl.multiple_of(mine + i * SR, 16), SR)
            a.gwv[D : D + SR, i * 2 * N : (i + 1) * 2 * N] = a.gws[half, :]
        yield from own.steps()
        for i in range(2):
            half = pl.ds(pl.multiple_of(mine + i * SR, 16), SR)
            a.gws[half, :] = a.gwv[D : D + SR, i * 2 * N : (i + 1) * 2 * N]
        yield from over_heads.spread()

    tasks["V3"] = last_chunk(tasks.pop("H"), tasks.pop("W"))
    done = []

    def copied_out(steps, pieces):
        yield from steps
        for src, dst in pieces:
            copy = pltpu.make_async_copy(src, dst, a.lsem.at[1 + len(done)])
            copy.start()
            done.append(copy)

    out_of = {"O": (a.gwo, a.out_gwo), "G": (a.gwg, a.out_gwg), "V": (a.gwv, a.out_gwv)}
    for name, task in tasks.items():
        if name == "V3":
            rows = pl.ds(2 * VR, VR - SR)
            pieces = [(a.gwv.at[rows, :], a.out_gwv.at[rows, :]), (a.gws, a.out_gws)]
            tasks[name] = copied_out(task, pieces)
        else:
            src, dst = out_of[name[0]]
            rows = pl.ds(task.lo, task.size)
            tasks[name] = copied_out(task.steps(), [(src.at[rows, :], dst.at[rows, :])])

    def pump(*names):
        for name in names:
            next(tasks[name], None)

    def at(point):
        pump(*PLAN.get(point, ()))

    def feature_sum(tag, block):
        sb1, sb2 = a.sb1, a.sb2
        rb1, rb2 = (a.__dict__[k + tag] for k in ("rb1", "rb2"))
        sem = a.__dict__["fsem" + tag]

        def copy1(s):
            return pltpu.make_async_remote_copy(
                src_ref=sb1.at[s],
                dst_ref=rb1.at[s],
                send_sem=sem.at[0, s],
                recv_sem=sem.at[1, s],
                device_id=core_peer,
                device_id_type=MESH,
            )

        def copy2(s):
            return pltpu.make_async_remote_copy(
                src_ref=sb2.at[s],
                dst_ref=rb2.at[s],
                send_sem=sem.at[2, s],
                recv_sem=sem.at[3, s],
                device_id=x_peer,
                device_id_type=MESH,
            )

        def one(s):
            sb1[s, 0] = block(s, flip(head, 1)).astype(BF)
            sb1[s, 1] = block(s, flip(flip(head, 1), 2)).astype(BF)
            copy1(s).start()

        def two(s):
            far = block(s, flip(head, 2))
            copy1(s).wait()
            sb2[s] = (far + rb1[s, 1].astype(F32)).astype(BF)
            copy2(s).start()

        def three(s):
            near = block(s, head)
            copy2(s).wait()
            return near + rb1[s, 0].astype(F32) + rb2[s].astype(F32)

        return one, two, three

    def features(f):
        return pl.ds(pl.multiple_of(f * F, F), F)

    o_one, o_two, o_three = feature_sum("o", lambda s, f: mm(a.ny[s], a.output_weight[:, features(f)]))

    def grad_out_weight(half_index):
        for g in range(D // F // 2):
            f = half_index * (D // F // 2) + g
            x = mm(a.nyT[...], a.cotf[f].reshape(S * T, F))
            a.gwo[half_index * C : (half_index + 1) * C, g * F : (g + 1) * F] = x.astype(BF)

    def weight_grad(out, r, rows, columns):
        out[r : r + rows, :] = mm(a.normT[r : r + rows, :], columns()).astype(BF)

    def intra_backward(s):
        K, Rm = a.KR[s, :, 0:N], a.KR[s, :, N : 2 * N]
        GT = jnp.where(rows_i <= cols_i, nt(K, Rm), 0.0)
        dGT = jnp.zeros((T, T), F32)
        for p in range(H // 2):
            pair = slice(p * LANES, (p + 1) * LANES)
            dY2, U2 = a.dY[s, :, pair], a.U[s, :, pair]
            z = []
            for h in (2 * p, 2 * p + 1):
                gap = a.cumT[s, h : h + 1, :] - a.cum[s, :, h : h + 1]
                LT = jnp.exp(jnp.minimum(gap, 0.0))
                mine = first_half if h == 2 * p else jnp.logical_not(first_half)
                Um = jnp.where(mine, U2.astype(F32), 0.0).astype(BF)
                dGT = dGT + nt(Um, dY2) * LT
                z.append(mm((LT * GT).astype(BF), dY2))
            a.dext[s, 0:T, pair] = jnp.where(first_half, z[0], z[1])
        a.dGT[s] = jnp.where(rows_i <= cols_i, dGT, 0.0).astype(BF)

    def out_rows(s):
        total = o_three(s)
        own = a.tokens[s, :, features(head)].astype(F32)
        a.mixed[s] = (own + total).astype(BF)

    def state_back(s):
        rows = pl.ds(pl.multiple_of(s * C, C), C)
        K, Rm = a.KR[s, :, 0:N], a.KR[s, :, N : 2 * N]
        gout, Sin = a.gout[rows, :], a.Sin[rows, :]
        gob = gout.astype(BF)
        cum, steps = a.cum[s], softplus(a.raw[s])
        tail = expand(jnp.exp(cum[T - 1 : T, :] - cum))
        V = a.V[s].astype(F32)
        dY = a.dY[s].astype(F32)
        dU = a.dext[s, 0:T, :] + tail * nt(K, gob)
        skipV = skip_row * V
        dV = expand(steps) * dU + skip_row * dY
        a.small[6:7, :] += jnp.sum(dY * V, axis=0, keepdims=True)
        ph, plo = split(dU * V)
        dsd = mm(ph, a.ET[...]) + mm(plo, a.ET[...])
        ph, plo = split(dY * (a.Y[s] - skipV))
        row = mm(ph, a.ET[...]) + mm(plo, a.ET[...])
        dcv = dV * a.dsv[s].astype(F32)
        a.dext[s, 0:T, :] = dcv
        dGT = a.dGT[s]
        sh, sl = split(Sin)
        dK = mm(dGT, Rm) + mm(a.tU[s], gob)
        dR = tn(dGT, K) + (mm(a.ecdY[s], sh) + mm(a.ecdY[s], sl))
        a.dsext[s, 0:T, 0:N] = dK * a.dss[s, :, 0:N].astype(F32)
        a.dsext[s, 0:T, N : 2 * N] = dR * a.dss[s, :, N : 2 * N].astype(F32)
        decay = a.decay[s]
        sums = []
        for h in range(H):
            hs = slice(h * PW, (h + 1) * PW)
            sp = a.sp[pl.ds(pl.multiple_of(s * C + h * PW, PW), PW), :]
            sums.append(jnp.sum(gout[hs] * (decay[h : h + 1] * Sin[hs] + sp), axis=0, keepdims=True))
        sums = jnp.concatenate(sums + [jnp.zeros((LANES - H, LANES), F32)], axis=0)
        ones = jnp.ones((8, LANES), BF)
        lh, ll = split(sums)
        end = (nt(ones, lh) + nt(ones, ll))[0:1]
        dld = mm_exact_left(a.triT[...], row - steps * dsd) + end
        draw = (dsd - rate_row * dld) * sigmoid(a.raw[s])
        a.heads_sm[0:1, :] += jnp.sum(draw, axis=0, keepdims=True)
        a.heads_sm[1:2, :] -= jnp.sum(steps * dld, axis=0, keepdims=True)
        a.dst[s] = draw.astype(BF)
        a.dstT[:, pl.ds(pl.multiple_of(s * T, T), T)] = draw.T[0:16].astype(BF)

    def gate_grad(r):
        weight_grad(a.gwg, r * D // 2, D // 2, lambda: a.normed[:, :, 0:C].reshape(S * T, C))

    grad_out_weight(0)
    pump("O0")
    grad_out_weight(1)
    pump("O1")
    at("g")
    gate_grad(0)
    pump("G0")
    at("g0")
    half(0, intra_backward)
    at("i1")
    at("wa0")
    backward[0][1]()
    at("p1")
    gate_grad(1)
    pump("G1")
    at("g1")
    at("wa1")
    backward[1][1]()
    at("p4")
    half(1, intra_backward)
    at("i3")
    at("wb0")
    backward[0][2](a.gout, 0)
    half(0, state_back)
    at("s1")
    at("wb1")
    backward[1][2](a.gout, Sh * C)
    half(1, state_back)
    at("s3")
    a.stepsum[...] = nt(a.dstT[...], a.normT[...])[0:8]

    def edge_copy(src, dst, sem):
        return pltpu.make_async_remote_copy(
            src_ref=src.at[:, pl.ds(0, 8), :],
            dst_ref=dst,
            send_sem=a.ssem.at[sem],
            recv_sem=a.rsem.at[sem],
            device_id=(lax.rem(me + n - 1, n), head),
            device_id_type=MESH,
        )

    edges = [edge_copy(a.dext, a.ev, 7), edge_copy(a.dsext, a.es, 8)]

    @pl.when(me > 0)
    def _():
        for copy in edges:
            copy.start()


    def conv_grads(s):
        for ext, grad, out, base, width in (
            (a.vext, a.dext, a.small, 0, C),
            (a.sext, a.dsext, a.shsm, 0, 2 * N),
        ):
            for c in range(0, width, LANES):
                ch = slice(c, c + LANES)
                d = grad[s, 0:T, ch]
                for k in range(4):
                    x = ext[s, pl.ds(5 + k, T), ch]
                    out[base + k : base + k + 1, ch] += jnp.sum(d * x, axis=0, keepdims=True)
                out[base + 4 : base + 5, ch] += jnp.sum(d, axis=0, keepdims=True)

    half(0, conv_grads)
    at("c0")
    half(1, conv_grads)
    at("c1")
    a.pack[...] = jnp.zeros(a.pack.shape, F32)
    a.pack[0:7, 0:C] = a.small[0:7, :]
    a.pack[0:2, C : C + LANES] = a.heads_sm[0:2, :]
    a.pack[8:16, :] = a.stepsum[...]
    a.pack[16:21, 0 : 2 * N] = a.shsm[0:5, :]

    def whole_sum(buf, inbox, partners, first):
        for i, partner in enumerate(partners):
            copy = pltpu.make_async_remote_copy(
                src_ref=buf,
                dst_ref=inbox.at[i],
                send_sem=a.psend.at[first + i],
                recv_sem=a.precv.at[first + i],
                device_id=partner,
                device_id_type=MESH,
            )
            copy.start()
            yield
            copy.wait()
            buf[...] = buf[...] + inbox[i]

    def small_sums():
        partners = [partner for partner, _ in levels]
        yield from whole_sum(a.pack, a.packin, partners, 0)
        yield from whole_sum(a.pack.at[pl.ds(16, 8), :], a.shin, [x_peer, core_peer], L)

    tasks["P"] = small_sums()

    def gain_sum():
        def copy(j):
            return pltpu.make_async_remote_copy(
                src_ref=a.ngain,
                dst_ref=a.ngin.at[me],
                send_sem=a.nsend.at[j],
                recv_sem=a.nrecv.at[me],
                device_id=(j, head),
                device_id_type=MESH,
            )

        def arrival(j):
            return pltpu.make_async_remote_copy(
                src_ref=a.ngain,
                dst_ref=a.ngin.at[j],
                send_sem=a.nsend.at[j],
                recv_sem=a.nrecv.at[j],
                device_id=(j, head),
                device_id_type=MESH,
            )

        def start(j):
            @pl.when(j != me)
            def _():
                copy(j).start()

        def wait(j):
            @pl.when(j != me)
            def _():
                arrival(j).wait()

        loop(n, start)
        yield
        loop(n, wait)
        a.ngin[me] = a.ngain[...]
        a.ngain[...] = jnp.zeros(a.ngain.shape, F32)

        def add(j):
            a.ngain[...] += a.ngin[j]

        loop(n, add)

    tasks["N"] = gain_sum()

    pump("P")
    at("we")

    @pl.when(me < n - 1)
    def _():
        for copy in edges:
            copy.wait_recv()
        for s in range(S):
            a.dext[s, T : T + 8, :] = a.ev[s]
            a.dsext[s, T : T + 8, :] = a.es[s]

    @pl.when(me == n - 1)
    def _():
        for s in range(S):
            a.dext[s, T : T + 8, :] = jnp.zeros((8, C), F32)
            a.dsext[s, T : T + 8, :] = jnp.zeros((8, 2 * N), F32)

    @pl.when(me > 0)
    def _():
        for copy in edges:
            copy.wait_send()

    def conv_back(grad, w, out, shift, width):
        def one(s):
            for c in range(0, width, LANES):
                ch = slice(c, c + LANES)
                total = w[3:4, ch] * grad[s, 0:T, ch]
                for k in range(3):
                    total = total + w[k : k + 1, ch] * grad[s, pl.ds(3 - k, T), ch]
                out[s, :, shift + c : shift + c + LANES] = total.astype(BF)

        loop(S, one)

    conv_back(a.dsext, a.conv_shared, a.dsl, 0, 2 * N)
    weight_grad(a.gws, 0, D, lambda: a.dsl[...].reshape(S * T, 2 * N))
    pump("V3")
    at("v")
    conv_back(a.dext, a.conv_value, a.normed, C, C)
    at("vv")
    def value_grad(r, rows):
        weight_grad(a.gwv, r, rows, lambda: a.normed[:, :, C : 2 * C].reshape(S * T, C))

    value_grad(2 * VR, VR - SR)
    at("v3")
    value_grad(0, VR)
    pump("V0")
    at("v0")
    value_grad(VR, VR)
    pump("V1")
    at("v1")

    def d_normed(s, f):
        rows = features(f)
        return (
            nt(a.normed[s, :, 0:C], a.gate_weight[rows, :])
            + nt(a.normed[s, :, C : 2 * C], a.value_weight[rows, :])
            + nt(a.dsl[s], a.shared_weight[rows, :])
            + mm(a.dst[s], a.stT[:, rows])
        )

    d_one, d_two, d_three = feature_sum("d", d_normed)
    half(0, d_one)
    at("d1")
    half(1, d_one)
    at("d3")
    half(0, d_two)
    at("e1")
    half(1, d_two)
    at("e3")
    loop(S, o_one)
    at("o3")

    own_gain = a.norm_gain[0:1, features(head)]

    def feature_rows(s):
        d = d_three(s)
        a.Y[s, :, 0:F] = d
        unit = a.tokens[s, :, features(head)].astype(F32) * a.raw[s, :, H : H + 1]
        a.ngain[0:1, :] += jnp.sum(d * unit, axis=0, keepdims=True)
        ones = jnp.ones((8, F), BF)
        dh, dl = split(d * own_gain * unit)
        dot = nt(ones, dh) + nt(ones, dl)
        row8 = lax.broadcasted_iota(jnp.int32, (8, T), 0)
        a.stat2[...] = jnp.where(row8 == s, dot, 0.0) + jnp.where(row8 < s, a.stat2[...], 0.0)

    a.ngain[...] = jnp.zeros(a.ngain.shape, F32)
    a.stat2[...] = jnp.zeros(a.stat2.shape, F32)
    at("wf1")
    half(0, feature_rows)
    at("f1")
    at("wf3")
    half(1, feature_rows)
    at("f3")
    pump("N")
    loop(S, o_two)
    at("n3")
    stats2 = head_sums(a.stat2, a.stin2, 15)
    for copy in stats2:
        copy.start()
    at("wst")
    for copy in stats2:
        copy.wait()
    total2 = a.stat2[...] + (a.stin2[0] + a.stin2[1]) + a.stin2[2]
    cols2 = jnp.concatenate([total2 / D, jnp.zeros((LANES - 8, T), F32)], axis=0).T
    for s in range(S):
        unit = a.tokens[s, :, features(head)].astype(F32) * a.raw[s, :, H : H + 1]
        inner_part = a.Y[s, :, 0:F] * own_gain - unit * cols2[:, s : s + 1]
        a.gtok[s] = a.cotangent[s].astype(F32) + a.raw[s, :, H : H + 1] * inner_part
    at("t")
    at("wx3")
    loop(S, out_rows)
    at("x3")
    at("end")
    for _ in range(2 * L + 8):
        pump(*tasks)
    a.o_small[...] = a.pack[...]
    a.o_ngain[...] = a.ngain[...]
    for copy in done:
        copy.wait()


INPUTS = [
    "tokens",
    "norm_gain",
    "gate_weight",
    "value_weight",
    "shared_weight",
    "step_weight",
    "conv_value",
    "conv_value_bias",
    "conv_shared",
    "conv_shared_bias",
    "step_bias",
    "decay_rate",
    "skip_weight",
    "out_gain",
    "output_weight",
    "cotangent",
]
OUTPUTS = ["mixed", "gtok", "out_gwg", "out_gwv", "out_gws", "out_gwo", "o_small", "o_ngain"]


def inbox_rows(size, count):
    total = 0
    for _ in range(count):
        size = size // 2 if can_halve(size) else size
        total += size
    return total


def scratch(dims):
    n, S, T, D, C, H, N, F = dims
    R = S // 2 * C // n
    L = n.bit_length() - 1
    vm = pltpu.VMEM
    dma = pltpu.SemaphoreType.DMA
    items = dict(
        tri=vm((T, T), BF),
        triT=vm((T, T), BF),
        E2=vm((2 * LANES, C), BF),
        ET=vm((C, LANES), BF),
        stT=vm((LANES, D), BF),
        skipE=vm((8, C), F32),
        hrow=vm((8, LANES), F32),
        small=vm((8, C), F32),
        heads_sm=vm((8, LANES), F32),
        shsm=vm((8, 2 * N), F32),
        normed=vm((S, T, D), BF),
        normT=vm((D, S * T), BF),
        halo=vm((S, 16, D), BF),
        cotf=vm((D // F, S, T, F), BF),
        vext=vm((S, T + 8, C), F32),
        sext=vm((S, T + 8, 2 * N), F32),
        raw=vm((S, T, LANES), F32),
        cum=vm((S, T, LANES), F32),
        cumT=vm((S, 8, T), F32),
        decay=vm((S, 8, LANES), F32),
        V=vm((S, T, C), BF),
        KR=vm((S, T, 2 * N), BF),
        dsv=vm((S, T, C), BF),
        dss=vm((S, T, 2 * N), BF),
        U=vm((S, T, C), BF),
        tU=vm((S, T, C), BF),
        sp=vm((S * C, N), F32),
        Sin=vm((S * C, N), F32),
        gout=vm((S * C, N), F32),
        joined=vm((2, LANES, N), F32),
        gate=vm((S, T, C), F32),
        Y=vm((S, T, C), F32),
        stat=vm((2, 8, T), F32),
        stin=vm((2, 3, 8, T), F32),
        stat2=vm((8, T), F32),
        stin2=vm((3, 8, T), F32),
        gscale=vm((S // 2, T, LANES), F32),
        gmean=vm((S // 2, T, LANES), F32),
        ny=vm((S, T, C), BF),
        nyT=vm((C, S * T), BF),
        dY=vm((S, T, C), BF),
        ecdY=vm((S, T, C), BF),
        dGT=vm((S, T, T), BF),
        dext=vm((S, T + 8, C), F32),
        dsext=vm((S, T + 8, 2 * N), F32),
        ev=vm((S, 8, C), F32),
        es=vm((S, 8, 2 * N), F32),
        dsl=vm((S, T, 2 * N), BF),
        dst=vm((S, T, LANES), BF),
        dstT=vm((16, S * T), BF),
        stepsum=vm((8, D), F32),
        gwo=vm((2 * C, D // 2), BF),
        gwo_in=vm((2 * inbox_rows(C, L), D // 2), BF),
        gwg=vm((D, C), BF),
        gwg_in=vm((2 * inbox_rows(D // 2, L), C), BF),
        gwv=vm((D + D // 8, C), BF),
        gwv_in=vm((3 * inbox_rows((D + D // 8) // 3, L), C), BF),
        gws=vm((D, 2 * N), BF),
        gws_in=vm((inbox_rows(D, 2), 2 * N), BF),
        ngain=vm((8, F), F32),
        pack=vm((24, D), F32),
        packin=vm((L, 24, D), F32),
        shin=vm((2, 8, D), F32),
        ngin=vm((n, 8, F), F32),
        ssem=dma((18,)),
        rsem=dma((18,)),
        lsem=dma((9,)),
        asend=dma((16 * L + 4,)),
        arecv=dma((16 * L + 4,)),
        afree=pltpu.SemaphoreType.REGULAR((16 * L + 4,)),
        psend=dma((L + 2,)),
        precv=dma((L + 2,)),
        nsend=dma((n,)),
        nrecv=dma((n,)),
    )
    for key in ("m10", "m11", "o20", "o21"):
        items[key] = vm((n, R + 16, N), BF)
    items["sb1"] = vm((S, 2, T, F), BF)
    items["sb2"] = vm((S, T, F), BF)
    for tag in ("f0", "f1", "b0", "b1"):
        for key in ("i1", "i2"):
            items[key + tag] = vm((n, R + 16, N), BF)
        for key in ("s1", "r1", "s2", "r2"):
            items[key + tag] = dma((n,))
    for tag in "od":
        items["rb1" + tag] = vm((S, 2, T, F), BF)
        items["rb2" + tag] = vm((S, T, F), BF)
        items["fsem" + tag] = dma((4, S))
    return items


def dims_names(dims):
    return INPUTS + OUTPUTS + list(scratch(dims))


def finish(dims, mixed, gtok, gwg, gwv, gws, left, right, small, ngain, *outs):
    n, S, T, D, C, H, N, F = dims
    PW = C // H
    outs[0][...] = mixed[...]
    outs[1][...] = gtok[...]
    outs[3][...] = gwg[...].astype(F32)
    outs[4][...] = gwv[...].astype(F32)
    outs[5][...] = gws[...].astype(F32)
    outs[15][:, 0 : D // 2] = left[...].astype(F32)
    outs[15][:, D // 2 : D] = right[...].astype(F32)

    @pl.when(pl.program_id(0) == 0)
    def _():
        outs[2][...] = ngain[0:1, :]
        outs[6][...] = small[8 : 8 + H, :]
        outs[7][...] = small[0:4, 0:C]
        outs[8][...] = small[4:5, 0:C]
        outs[9][...] = small[16:20, 0 : 2 * N]
        outs[10][...] = small[20:21, 0 : 2 * N]
        outs[11][...] = small[0:1, C : C + H]
        outs[12][...] = small[1:2, C : C + H]
        sums = [jnp.sum(small[6:7, h * PW : (h + 1) * PW], axis=1, keepdims=True) for h in range(H)]
        outs[13][...] = jnp.concatenate(sums, axis=1)
        outs[14][...] = small[5:6, 0:C]


def shards(*args):
    tokens, gate_weight, step_weight, shared_weight = args[0], args[2], args[5], args[4]
    cotangent = args[15]
    S, T, D = tokens.shape
    C, H, N, F = gate_weight.shape[1], step_weight.shape[1], shared_weight.shape[1] // 2, cotangent.shape[2]
    n = lax.axis_size("seq")
    dims = (n, S, T, D, C, H, N, F)
    args = [x.reshape(1, -1) if x.ndim == 1 else x for x in args]
    args[5] = step_weight.T
    items = scratch(dims)
    whole = pl.BlockSpec(memory_space=pltpu.VMEM)
    hbm = pl.BlockSpec(memory_space=pl.ANY)
    struct = jax.ShapeDtypeStruct
    mixed, gtok, gwg, gwv, gws, gwo, small, ngain = pl.pallas_call(
        lambda *refs: kernel(dims, *refs),
        out_shape=(
            struct((S, T, F), BF),
            struct((S, T, F), F32),
            struct((D, C), BF),
            struct((D, C), BF),
            struct((D, 2 * N), BF),
            struct((2 * C, D // 2), BF),
            struct((24, D), F32),
            struct((8, F), F32),
        ),
        in_specs=[whole] * len(args),
        out_specs=(whole, whole, hbm, hbm, hbm, hbm, whole, whole),
        scratch_shapes=list(items.values()),
        compiler_params=pltpu.CompilerParams(
            collective_id=0, has_side_effects=True, vmem_limit_bytes=63 * 2**20
        ),
        name="block",
    )(*args)
    G = STEPS
    outs = pl.pallas_call(
        lambda *refs: finish(dims, *refs),
        grid=(G,),
        out_shape=(
            struct((S * T, F), BF),
            struct((S * T, F), F32),
            struct((1, F), F32),
            struct((D, C), F32),
            struct((D, C), F32),
            struct((D, 2 * N), F32),
            struct((H, D), F32),
            struct((4, C), F32),
            struct((1, C), F32),
            struct((4, 2 * N), F32),
            struct((1, 2 * N), F32),
            struct((1, H), F32),
            struct((1, H), F32),
            struct((1, H), F32),
            struct((1, C), F32),
            struct((C, D), F32),
        ),
        in_specs=[
            pl.BlockSpec((S * T // G, F), lambda i: (i, 0)),
            pl.BlockSpec((S * T // G, F), lambda i: (i, 0)),
            pl.BlockSpec((D // G, C), lambda i: (i, 0)),
            pl.BlockSpec((D // G, C), lambda i: (i, 0)),
            pl.BlockSpec((D // G, 2 * N), lambda i: (i, 0)),
            pl.BlockSpec((C // G, D // 2), lambda i: (i, 0)),
            pl.BlockSpec((C // G, D // 2), lambda i: (i + G, 0)),
            pl.BlockSpec((24, D), lambda i: (0, 0)),
            pl.BlockSpec((8, F), lambda i: (0, 0)),
        ],
        out_specs=(
            pl.BlockSpec((S * T // G, F), lambda i: (i, 0)),
            pl.BlockSpec((S * T // G, F), lambda i: (i, 0)),
            pl.BlockSpec((1, F), lambda i: (0, 0)),
            pl.BlockSpec((D // G, C), lambda i: (i, 0)),
            pl.BlockSpec((D // G, C), lambda i: (i, 0)),
            pl.BlockSpec((D // G, 2 * N), lambda i: (i, 0)),
            pl.BlockSpec((H, D), lambda i: (0, 0)),
            pl.BlockSpec((4, C), lambda i: (0, 0)),
            pl.BlockSpec((1, C), lambda i: (0, 0)),
            pl.BlockSpec((4, 2 * N), lambda i: (0, 0)),
            pl.BlockSpec((1, 2 * N), lambda i: (0, 0)),
            pl.BlockSpec((1, H), lambda i: (0, 0)),
            pl.BlockSpec((1, H), lambda i: (0, 0)),
            pl.BlockSpec((1, H), lambda i: (0, 0)),
            pl.BlockSpec((1, C), lambda i: (0, 0)),
            pl.BlockSpec((C // G, D), lambda i: (i, 0)),
        ),
        name="finish",
    )(mixed.reshape(S * T, F), gtok.reshape(S * T, F), gwg, gwv, gws, gwo, gwo, small, ngain)
    outs = list(outs)
    outs[0], outs[1] = outs[0].reshape(S, T, F), outs[1].reshape(S, T, F)
    outs[6] = outs[6].T
    for i in (2, 8, 10, 11, 12, 13, 14):
        outs[i] = outs[i].reshape(-1)
    return tuple(outs)


def solution(mesh):
    head = P("head")
    return jax.shard_map(
        shards,
        mesh=mesh,
        in_specs=(
            P(None, "seq", None),
            P(),
            P(None, "head"),
            P(None, "head"),
            P(),
            P(None, "head"),
            P(None, "head"),
            head,
            P(),
            P(),
            head,
            head,
            head,
            head,
            P("head", None),
            P(None, "seq", "head"),
        ),
        out_specs=(
            P(None, "seq", "head"),
            P(None, "seq", "head"),
            head,
            P(None, "head"),
            P(None, "head"),
            P(),
            P(None, "head"),
            P(None, "head"),
            head,
            P(),
            P(),
            head,
            head,
            head,
            head,
            P("head", None),
        ),
        check_vma=False,
    )
```
